256 devices in a mesh: gx: 8 (over z), gy: 32 (over y, x, core).
Axes of the slice: x: 4, y: 4, z: 8, core: 2. Of those that a mesh axis runs over, the one named last changes fastest.
Arguments:
- design_fraction: float32 [512, 256, 256], P('gx', 'gy'), may hold values from 0.05 to 1
- voltage_field: float32 [512, 256, 256], P('gx', 'gy'), may hold values from -6 to 6
- warmth_field: float32 [512, 256, 256], P('gx', 'gy'), may hold values from 0.5 to 2
- dual_state: float32 [512, 256, 256], P('gx', 'gy'), may hold values from -6 to 6
- injected_charge: float32 [512, 256, 256], P('gx', 'gy'), may hold values from -6 to 6
- objective_weighting: float32 [512, 256, 256], P('gx', 'gy'), may hold values from 0.1 to 1
- empty_flag: int32 [512, 256, 256], P('gx', 'gy'), may hold values 0 or 1
- solid_flag: int32 [512, 256, 256], P('gx', 'gy'), may hold values 0 or 1
- grounded_voltage_flag: int32 [512, 256, 256], P('gx', 'gy'), may hold values 0 or 1
- clamped_warmth_flag: int32 [512, 256, 256], P('gx', 'gy'), may hold values 0 or 1
Outputs:
- voltage_field_next: float32 [512, 256, 256], P('gx', 'gy')
- warmth_field_next: float32 [512, 256, 256], P('gx', 'gy')
- dual_state_next: float32 [512, 256, 256], P('gx', 'gy')
- scaled_derivative: float32 [512, 256, 256], P('gx', 'gy')
- occupied_fraction: float32 [], replicated
- mean_warmth: float32 [], replicated
The draws below stay inside these ranges and needn't reach their ends.
All inputs are finite; a program needn't handle non-finite values. No bound on the sum of `empty_flag` or of `solid_flag` or of `grounded_voltage_flag` or of `clamped_warmth_flag` on one device may be relied on, other than what follows from the above.
Results may differ from the reference program's by a relative error of at most 0.00002.
Values sent between devices are 32-bit elements; how exact they have to be, the bound alone decides.
A program may use at most 64 MiB of HBM per device.

```python
import math
import jax
import jax.numpy as jnp
from jax import lax

BRICKS_HEIGHT = 256
BRICKS_WIDTH = 512
BRICKS_DEPTH = 256


def set_ends(array, rng, smallest, high):
    dims = array.shape
    spot = [jax.random.randint(jax.random.fold_in(rng, axis), (), 0, dims[axis]) for axis in range(len(dims))]
    array = array.at[tuple(spot)].set(smallest)
    longest = dims.index(max(dims))
    spot[longest] = (spot[longest] + 1) % dims[longest]
    return array.at[tuple(spot)].set(high)


def shard_levels(stream_key, dims, split, least, high):
    loudness = 1.0
    for dim, blocks in split:
        steps = jax.random.uniform(jax.random.fold_in(jax.random.fold_in(stream_key, 6), dim), (blocks,), jnp.float32, least / len(split), high / len(split))
        loudness = loudness * jnp.repeat(jnp.exp(steps), dims[dim] // blocks).reshape((-1,) + (1,) * (len(dims) - 1 - dim))
    return loudness


def noise(key, shape, spread, bound, pieces=(), kind=jnp.bfloat16):
    level = shard_levels(key, shape, pieces, -0.22, 0.18) if pieces else 1.0
    values = jax.random.normal(key, shape, jnp.float32) * spread * level
    return jnp.minimum(jnp.maximum(values, -bound), bound).astype(kind)


def setup_inputs(seed: int = 0) -> dict:
    streams_of = jax.random.split(jax.random.key(seed), 11)
    design_fraction = jnp.clip(0.05 + 0.95 * jax.random.uniform(streams_of[0], (BRICKS_WIDTH, BRICKS_DEPTH, BRICKS_HEIGHT), jnp.float32) ** shard_levels(streams_of[0], (BRICKS_WIDTH, BRICKS_DEPTH, BRICKS_HEIGHT), ((0, 8), (1, 32)), -0.2, 0.2), 0.05, 1.0)
    voltage_field = noise(streams_of[1], (BRICKS_WIDTH, BRICKS_DEPTH, BRICKS_HEIGHT), 1.0, 6.0, ((0, 8), (1, 32)), jnp.float32)
    warmth_field = jnp.clip(0.5 + 1.5 * jax.random.uniform(streams_of[2], (BRICKS_WIDTH, BRICKS_DEPTH, BRICKS_HEIGHT), jnp.float32) ** shard_levels(streams_of[2], (BRICKS_WIDTH, BRICKS_DEPTH, BRICKS_HEIGHT), ((0, 8), (1, 32)), -0.2, 0.2), 0.5, 2.0)
    dual_state = noise(streams_of[3], (BRICKS_WIDTH, BRICKS_DEPTH, BRICKS_HEIGHT), 1.0, 6.0, ((0, 8), (1, 32)), jnp.float32)
    injected_charge = noise(streams_of[4], (BRICKS_WIDTH, BRICKS_DEPTH, BRICKS_HEIGHT), 1.0, 6.0, ((0, 8), (1, 32)), jnp.float32)
    objective_weighting = jnp.clip(jnp.exp(math.log(1.0) - 2.3025851 * jax.random.uniform(streams_of[5], (BRICKS_WIDTH, BRICKS_DEPTH, BRICKS_HEIGHT), jnp.float32) ** shard_levels(streams_of[5], (BRICKS_WIDTH, BRICKS_DEPTH, BRICKS_HEIGHT), ((0, 8), (1, 32)), -0.2, 0.2)), 0.1, 1.0)
    empty_flag = set_ends((jax.random.randint(streams_of[6], (BRICKS_WIDTH, BRICKS_DEPTH, BRICKS_HEIGHT), 0, 16) < 1).astype(jnp.int32), jax.random.fold_in(streams_of[6], 1), 0, 1)
    solid_flag = set_ends((jax.random.randint(streams_of[7], (BRICKS_WIDTH, BRICKS_DEPTH, BRICKS_HEIGHT), 0, 16) < 1).astype(jnp.int32), jax.random.fold_in(streams_of[7], 1), 0, 1)
    grounded_voltage_flag = set_ends((jax.random.randint(streams_of[8], (BRICKS_WIDTH, BRICKS_DEPTH, BRICKS_HEIGHT), 0, 32) < 1).astype(jnp.int32), jax.random.fold_in(streams_of[8], 1), 0, 1)
    clamped_warmth_flag = set_ends((jax.random.randint(streams_of[9], (BRICKS_WIDTH, BRICKS_DEPTH, BRICKS_HEIGHT), 0, 32) < 1).astype(jnp.int32), jax.random.fold_in(streams_of[9], 1), 0, 1)
    return {"design_fraction": design_fraction, "voltage_field": voltage_field, "warmth_field": warmth_field, "dual_state": dual_state, "injected_charge": injected_charge, "objective_weighting": objective_weighting, "empty_flag": empty_flag, "solid_flag": solid_flag, "grounded_voltage_flag": grounded_voltage_flag, "clamped_warmth_flag": clamped_warmth_flag}


RADIUS = 3
WEIGHTS = (1.0, 2.0, 3.0, 4.0, 3.0, 2.0, 1.0)
CONDUCT_FLOOR = 0.001
CONDUCT_LOWEST = 0.05
DAMPING_FACTOR = 0.6
CORNERS = tuple(((a, b, c) for a in (0, 1) for b in (0, 1) for c in (0, 1)))

def tent_along(padded, direction, length):
    summed = WEIGHTS[0] * lax.slice_in_dim(padded, 0, length, axis=direction)
    for offset in range(1, 2 * RADIUS + 1):
        summed = summed + WEIGHTS[offset] * lax.slice_in_dim(padded, offset, offset + length, axis=direction)
    return summed

def tent_filter(field):
    result = field
    for direction in range(3):
        length = result.shape[direction]
        widths = [(0, 0), (0, 0), (0, 0)]
        widths[direction] = (RADIUS, RADIUS)
        result = tent_along(jnp.pad(result, widths), direction, length)
    return result

def window_sum(length):
    positions = jnp.arange(length, dtype=jnp.int32)
    summed = jnp.zeros((length,), jnp.float32)
    for offset in range(2 * RADIUS + 1):
        inside = (positions + offset - RADIUS >= 0) & (positions + offset - RADIUS < length)
        summed = summed + WEIGHTS[offset] * inside.astype(jnp.float32)
    return summed

def vertex_pieces(extended, entry_dimensions):
    return [extended[a:a + entry_dimensions[0], b:b + entry_dimensions[1], c:c + entry_dimensions[2]] for a, b, c in CORNERS]

def element_apply(views, weight_field):
    overall = views[0]
    for corner in range(1, 8):
        overall = overall + views[corner]
    result = []
    for corner in range(8):
        nearby = views[corner ^ 4] + views[corner ^ 2] + views[corner ^ 1]
        result.append(weight_field * (5.0 / 12.0 * views[corner] + nearby / 12.0 - overall / 12.0))
    return result

def stored_work(left_views, right_views):
    images = element_apply(right_views, 1.0)
    summed = left_views[0] * images[0]
    for corner in range(1, 8):
        summed = summed + left_views[corner] * images[corner]
    return summed

def scatter_local(parts, entry_dimensions):
    extended = jnp.zeros((entry_dimensions[0] + 1, entry_dimensions[1] + 1, entry_dimensions[2] + 1), jnp.float32)
    for corner, (a, b, c) in enumerate(CORNERS):
        extended = extended + jnp.pad(parts[corner], ((a, 1 - a), (b, 1 - b), (c, 1 - c)))
    return extended

def grow_higher(field):
    return jnp.pad(field, ((0, 1), (0, 1), (0, 1)))

def assemble(parts):
    entry_dimensions = parts[0].shape
    return scatter_local(parts, entry_dimensions)[:entry_dimensions[0], :entry_dimensions[1], :entry_dimensions[2]]

def reference(design_fraction, voltage_field, warmth_field, dual_state, injected_charge, objective_weighting, empty_flag, solid_flag, grounded_voltage_flag, clamped_warmth_flag):
    entry_dimensions = design_fraction.shape
    element_number_sum = entry_dimensions[0] * entry_dimensions[1] * entry_dimensions[2]
    window = window_sum(entry_dimensions[0])[:, None, None] * window_sum(entry_dimensions[1])[None, :, None] * window_sum(entry_dimensions[2])[None, None, :]
    solid = tent_filter(design_fraction) / window
    physical = jnp.where(empty_flag == 1, 0.0, jnp.where(solid_flag == 1, 1.0, solid)).astype(jnp.float32)
    occupied_fraction = jnp.sum(physical) / element_number_sum
    cubed = physical * physical * physical
    elec_weight = CONDUCT_FLOOR + (1.0 - CONDUCT_FLOOR) * cubed
    conduction_factor = CONDUCT_LOWEST + (1.0 - CONDUCT_LOWEST) * cubed
    electric_unfixed = 1.0 - grounded_voltage_flag.astype(jnp.float32)
    loose_warmth_flag = 1.0 - clamped_warmth_flag.astype(jnp.float32)
    diag_e = electric_unfixed * assemble([elec_weight / 3.0] * 8) + (1.0 - electric_unfixed)
    conduction_pivot = loose_warmth_flag * assemble([conduction_factor / 3.0] * 8) + (1.0 - loose_warmth_flag)

    def stiffness_product(field, weight_field, free_mask):
        views = vertex_pieces(grow_higher(free_mask * field), entry_dimensions)
        return free_mask * assemble(element_apply(views, weight_field)) + (1.0 - free_mask) * field
    voltage_field_next = voltage_field + DAMPING_FACTOR * (electric_unfixed * injected_charge - stiffness_product(voltage_field, elec_weight, electric_unfixed)) / diag_e
    power_views = vertex_pieces(grow_higher(voltage_field_next), entry_dimensions)
    resistive_power = stored_work(power_views, power_views)
    warmth_injection = loose_warmth_flag * assemble([elec_weight * resistive_power / 8.0] * 8)
    warmth_field_next = warmth_field + DAMPING_FACTOR * (warmth_injection - stiffness_product(warmth_field, conduction_factor, loose_warmth_flag)) / conduction_pivot
    dual_state_next = dual_state + DAMPING_FACTOR * (loose_warmth_flag * objective_weighting - stiffness_product(dual_state, conduction_factor, loose_warmth_flag)) / conduction_pivot
    mean_warmth = jnp.sum(objective_weighting * warmth_field_next) / element_number_sum
    warmth_pieces = vertex_pieces(grow_higher(warmth_field_next), entry_dimensions)
    dual_windows = vertex_pieces(grow_higher(dual_state_next), entry_dimensions)
    dual_average = dual_windows[0]
    for corner in range(1, 8):
        dual_average = dual_average + dual_windows[corner]
    dual_average = dual_average / 8.0
    derivative_part = 3.0 * physical * physical
    raw_derivative = derivative_part * ((1.0 - CONDUCT_FLOOR) * resistive_power * dual_average - (1.0 - CONDUCT_LOWEST) * stored_work(warmth_pieces, dual_windows))
    design = (1.0 - empty_flag.astype(jnp.float32)) * (1.0 - solid_flag.astype(jnp.float32))
    filtered = tent_filter(raw_derivative * design / window)
    scale_norm = jnp.sqrt(jnp.sum(filtered * filtered) / element_number_sum + 1e-06)
    scaled_derivative = filtered / scale_norm
    return (voltage_field_next, warmth_field_next, dual_state_next, scaled_derivative, occupied_fraction, mean_warmth)
```

```python
import functools

import jax
import jax.numpy as jnp
from jax import lax
from jax.experimental import pallas as pl
from jax.experimental.pallas import tpu as pltpu
from jax.sharding import PartitionSpec as P

MESH = pl.DeviceIdType.MESH
F32 = jnp.float32
BF16 = jnp.bfloat16
PAD = 8
OFFSETS = ((0, 1), (0, -1), (1, 1), (-1, 1), (1, -1), (-1, -1), (1, 0), (-1, 0))


def lanes(shape):
    return lax.broadcasted_iota(jnp.int32, shape, len(shape) - 1)


def z_next(p):
    r = pltpu.roll(p, 127, axis=p.ndim - 1)
    lane = lanes(p.shape[1:])
    low = jnp.where(lane < 127, r[0], r[1])
    high = jnp.where(lane < 127, r[1], 0.0)
    return jnp.stack([low, high])


def z_prev(p):
    r = pltpu.roll(p, 1, axis=p.ndim - 1)
    lane = lanes(p.shape[1:])
    low = jnp.where(lane > 0, r[0], 0.0)
    high = jnp.where(lane > 0, r[1], r[0])
    return jnp.stack([low, high])


def rows_of(shape):
    return lax.broadcasted_iota(jnp.int32, shape, len(shape) - 2)


def y_next(p, row):
    r = pltpu.roll(p, 7, axis=1)
    return jnp.where(rows_of(p.shape) < 7, r, jnp.broadcast_to(row, p.shape))


def y_prev(p):
    r = pltpu.roll(p, 1, axis=1)
    return jnp.where(rows_of(p.shape) > 0, r, 0.0)


def yz_forward(p, row):
    q = y_next(p, row)
    s, d = p + q, q - p
    sz, dz = z_next(s), z_next(d)
    return s + sz, sz - s, d + dz, dz - d


def z_forward_rows(s, d):
    sz, dz = z_next(s), z_next(d)
    return s + sz, sz - s, d + dz, dz - d


def x_forward(a, b):
    return [a[i] + b[i] for i in range(1, 4)], [b[i] - a[i] for i in range(4)]


def weigh(sums, diffs, w):
    w1, w2, w3 = w * (1.0 / 48.0), w * (1.0 / 24.0), w * (1.0 / 16.0)
    return (
        [w3 * sums[0], w3 * sums[1], w2 * sums[2]],
        [w3 * diffs[0], w2 * diffs[1], w2 * diffs[2], w1 * diffs[3]],
    )


def x_backward(sums, diffs):
    front = [-diffs[0]] + [sums[i] - diffs[i + 1] for i in range(3)]
    behind = [diffs[0]] + [sums[i] + diffs[i + 1] for i in range(3)]
    return front, behind


def yz_backward(n):
    ns = (n[0] - n[2]) + y_prev(n[0] + n[2])
    nd = (n[1] - n[3]) + y_prev(n[1] + n[3])
    return (ns - nd) + z_prev(ns + nd)


def energy(sa, da, sb, db):
    three = da[0] * db[0] + sa[0] * sb[0] + sa[1] * sb[1]
    two = da[1] * db[1] + da[2] * db[2] + sa[2] * sb[2]
    return (1.0 / 16.0) * three + (1.0 / 24.0) * two + (1.0 / 48.0) * (da[3] * db[3])


def spread(p):
    t = p + y_prev(p)
    return t + z_prev(t)


def row_pack(ref, h, first, planes, row):
    every = ref.shape[1]
    flat = ref.reshape(2 * every * 8, 128)
    return flat[pl.ds((h * every + first) * 8 + row, planes, stride=8), :]


def row_add(ref, h, first, planes, row, value):
    every = ref.shape[1]
    flat = ref.reshape(2 * every * 8, 128)
    where = pl.ds((h * every + first) * 8 + row, planes, stride=8)
    flat[where, :] = flat[where, :] + value


def edge_column(edge, h, p):
    every = edge.shape[2]
    flat = edge.reshape(8 * 2 * every, 128)
    return flat[pl.ds(h * every + p, 8, stride=2 * every), :]


def kernel(
    nx, ny, n,
    des_in, v_in, t_in, d_in, q_in, o_in, e_in, s_in, g_in, c_in,
    v_out, t_out, d_out, f_out, occ_out, mean_out,
    des, raw, flg, fld, flx,
    cc, cup, cdn, flo, fhi, fup, fdn,
    wz, yf, ph, cub, cube, cubs, ca,
    kap, v1, v1lo, v1hi, v1up, v1dn,
    d1, d1hi, d1dn, t0, tr, t1, t1hi, t1dn, joule,
    sen, scc, sup, sdn, fil, slots1, slots2,
    in_sem, out_sem, send_sem, recv_sem, r1_send, r1_recv, r2_send, r2_recv,
):
    gx, gy = lax.axis_index("gx"), lax.axis_index("gy")
    group = min(16, ny)
    blocks = ny // group
    total = float(nx * n * ny * 8 * 256)
    end = PAD + n
    first_x, last_x = gx == 0, gx == nx - 1
    first_y, last_y = gy == 0, gy == ny - 1

    loads = []
    plan = [
        (des_in, lambda h: des.at[h, PAD:end]),
        (v_in, lambda h: raw.at[0, h]),
        (g_in, lambda h: flg.at[2, h]),
        (t_in, lambda h: raw.at[1, h]),
        (d_in, lambda h: raw.at[2, h]),
        (c_in, lambda h: flg.at[3, h]),
        (e_in, lambda h: flg.at[0, h]),
        (s_in, lambda h: flg.at[1, h]),
        (q_in, lambda h: raw.at[3, h]),
        (o_in, lambda h: raw.at[4, h]),
    ]
    for i, (src, dst) in enumerate(plan):
        pair = []
        for h in range(2):
            c = pltpu.make_async_copy(
                src.at[:, :, pl.ds(128 * h, 128)], dst(h), in_sem.at[2 * i + h]
            )
            c.start()
            pair.append(c)
        loads.append(pair)

    def loaded(*which):
        for i in which:
            for c in loads[i]:
                c.wait()

    barrier = pltpu.get_barrier_semaphore()

    def device(dx, dy):
        return (lax.rem(gx + (nx + dx), nx), lax.rem(gy + (ny + dy), ny))

    me1, block = lax.rem(gy, group), lax.div(gy, group)
    me2 = gx * blocks + block

    def peer1(k):
        return (gx, block * group + lax.rem(me1 + k, group))

    def peer2(k):
        other = lax.rem(me2 + k, nx * blocks)
        return (lax.div(other, blocks), lax.rem(other, blocks) * group + me1)

    for dx, dy in OFFSETS:
        pl.semaphore_signal(barrier, inc=1, device_id=device(dx, dy), device_id_type=MESH)
    for k in range(1, group):
        pl.semaphore_signal(barrier, inc=1, device_id=peer1(k), device_id_type=MESH)
    for k in range(1, nx * blocks):
        pl.semaphore_signal(barrier, inc=1, device_id=peer2(k), device_id_type=MESH)

    count = [0]

    def send(src, dst, dx, dy):
        k = count[0]
        count[0] += 1
        c = pltpu.make_async_remote_copy(
            src_ref=src, dst_ref=dst, send_sem=send_sem.at[k], recv_sem=recv_sem.at[k],
            device_id=device(dx, dy), device_id_type=MESH,
        )
        c.start()
        return c

    def send_up(src, dst):
        return [
            send(src, dst.at[:, :, PAD:end], 0, 1),
            send(src.at[:, :, n - PAD : n], dst.at[:, :, 0:PAD], 1, 1),
            send(src.at[:, :, 0:PAD], dst.at[:, :, end : end + PAD], -1, 1),
        ]

    def send_down(src, dst, both=True):
        some = [
            send(src, dst.at[:, :, PAD:end], 0, -1),
            send(src.at[:, :, 0:PAD], dst.at[:, :, end : end + PAD], -1, -1),
        ]
        if both:
            some.append(send(src.at[:, :, n - PAD : n], dst.at[:, :, 0:PAD], 1, -1))
        return some

    pending = []

    def arrived(copies):
        for c in copies:
            c.wait_recv()
        pending.extend(copies)

    def tails(ref, up, down):
        for h in range(2):
            r = [row_pack(ref, h, PAD, n, j) for j in (0, 1, 2, 5, 6, 7)]
            up[0, h] = r[3] + 2.0 * r[4] + 3.0 * r[5]
            up[1, h] = r[4] + 2.0 * r[5]
            up[2, h] = r[5]
            down[0, h] = r[0]
            down[1, h] = 2.0 * r[0] + r[1]
            down[2, h] = 3.0 * r[0] + 2.0 * r[1] + r[2]

    zero_rows = jnp.zeros((2, 2, end + PAD, 128), F32)
    cc[3:5] = zero_rows
    scc[3:5] = zero_rows
    wi = lax.broadcasted_iota(jnp.int32, (256, 256), 0)
    wj = lax.broadcasted_iota(jnp.int32, (256, 256), 1)
    wz[...] = jnp.maximum(4 - jnp.abs(wi - wj), 0).astype(F32).astype(BF16)

    loaded(0)
    tails(des, cup, cdn)
    pl.semaphore_wait(barrier, len(OFFSETS) + group - 1 + nx * blocks - 1)
    moving = send_up(cup, cc.at[0:3]) + send_down(cdn, cc.at[5:8])
    moving += [
        send(des.at[:, end - 4 : end], des.at[:, PAD - 4 : PAD], 1, 0),
        send(des.at[:, PAD : PAD + 3], des.at[:, end : end + 3], -1, 0),
    ]
    loaded(1, 2, 3, 4, 5, 6, 7)
    moving.append(send(flg.at[0:2, :, n - 1], flx, 1, 0))

    def mask_body(i, carry):
        x = i * 4
        free_e = flg[2, :, pl.ds(x, 4)] == 0
        free_t = flg[3, :, pl.ds(x, 4)] == 0
        fld[0, :, pl.ds(PAD + x, 4)] = jnp.where(free_e, raw[0, :, pl.ds(x, 4)], 0.0)
        fld[1, :, pl.ds(PAD + x, 4)] = jnp.where(free_t, raw[1, :, pl.ds(x, 4)], 0.0)
        fld[2, :, pl.ds(PAD + x, 4)] = jnp.where(free_t, raw[2, :, pl.ds(x, 4)], 0.0)
        return carry

    lax.fori_loop(0, n // 4, mask_body, 0)
    for f in range(3):
        for h in range(2):
            fup[f, h] = row_pack(fld.at[f], h, PAD, n, 7)
            fdn[f, h] = row_pack(fld.at[f], h, PAD, n, 0)
    fields_moving = send_up(fup, flo) + send_down(fdn, fhi)
    fields_moving += [
        send(fld.at[:, :, end - 1 : end], fld.at[:, :, PAD - 1 : PAD], 1, 0),
        send(fld.at[:, :, PAD : PAD + 1], fld.at[:, :, end : end + 1], -1, 0),
    ]

    row = lax.broadcasted_iota(jnp.int32, (8, 128), 0)

    def filter_y(ref, edge, p):
        for h in range(2):
            a = ref[h, p]
            out = 4.0 * a + edge_column(edge, h, p)
            for k in (1, 2, 3):
                out += jnp.where(row < 8 - k, float(4 - k), 0.0) * pltpu.roll(a, 8 - k, axis=0)
                out += jnp.where(row >= k, float(4 - k), 0.0) * pltpu.roll(a, k, axis=0)
            yf[h, p] = out

    def filter_y_all(ref, edge, low):
        def body(i, carry):
            for u in range(4):
                filter_y(ref, edge, PAD + 4 * i + u)
            return carry

        lax.fori_loop(0, n // 4, body, 0)
        for p in list(range(PAD - low, PAD)) + list(range(end, end + 3)):
            filter_y(ref, edge, p)

    def filter_xz(p, planes):
        halves = []
        for h in range(2):
            a = yf[h, pl.ds(p - 3, planes + 6)]
            a = a[:-1] + a[1:]
            a = a[:-2] + a[2:]
            a = a[:-1] + a[1:]
            a = a[:-2] + a[2:]
            halves.append(a.reshape(planes * 8, 128))
        a = jnp.concatenate(halves, axis=1)
        high = a.astype(BF16)
        rest = a - high.astype(F32)
        mid = rest.astype(BF16)
        low = (rest - mid.astype(F32)).astype(BF16)
        w = wz[...]
        out = (
            jnp.dot(low, w, preferred_element_type=F32)
            + jnp.dot(mid, w, preferred_element_type=F32)
            + jnp.dot(high, w, preferred_element_type=F32)
        )
        return jnp.stack(
            [out[:, :128].reshape(planes, 8, 128), out[:, 128:].reshape(planes, 8, 128)]
        )

    def inverse_window(i, full):
        w = jnp.where(i == 0, 10, jnp.where(i == 1, 13, jnp.where(i == 2, 15, 16)))
        k = full - 1 - i
        return jnp.where(k == 0, w - 6, jnp.where(k == 1, w - 3, jnp.where(k == 2, w - 1, w)))

    shape = (2, 8, 128)
    yy = gy * 8 + lax.broadcasted_iota(jnp.int32, shape, 1)
    zz = lax.broadcasted_iota(jnp.int32, shape, 0) * 128 + lax.broadcasted_iota(jnp.int32, shape, 2)
    inv_yz = 1.0 / (inverse_window(yy, ny * 8) * inverse_window(zz, 256)).astype(F32)
    touch_yz = (jnp.where(yy == 0, 1, 2) * jnp.where(zz == 0, 1, 2)).astype(F32)

    def inv_x(p):
        i = gx * n + (p - PAD)
        full = nx * n
        r = jnp.where(i == 0, 1 / 10.0, jnp.where(i == 1, 1 / 13.0, jnp.where(i == 2, 1 / 15.0, 1 / 16.0)))
        k = full - 1 - i
        return jnp.where(
            k == 0, 1 / 10.0, jnp.where(k == 1, 1 / 13.0, jnp.where(k == 2, 1 / 15.0, r))
        ).astype(F32)

    arrived(moving)

    def clear(edge, field, low, high):
        @pl.when(first_x)
        def _():
            if low:
                field[:, PAD - low : PAD] = jnp.zeros((2, low, 8, 128), F32)
            edge[:, :, 0:PAD] = jnp.zeros((8, 2, PAD, 128), F32)

        @pl.when(last_x)
        def _():
            field[:, end : end + high] = jnp.zeros((2, high, 8, 128), F32)
            edge[:, :, end : end + PAD] = jnp.zeros((8, 2, PAD, 128), F32)

        @pl.when(first_y)
        def _():
            edge[0:3] = jnp.zeros((3, 2, end + PAD, 128), F32)

        @pl.when(last_y)
        def _():
            edge[5:8] = jnp.zeros((3, 2, end + PAD, 128), F32)

    clear(cc, des, 4, 3)
    filter_y_all(des, cc, 4)
    there_x = jnp.where(first_x, 0.0, 1.0).astype(F32)
    there_y = jnp.where(first_y, 0.0, 1.0).astype(F32)

    def density(smoothed, p, e, s):
        solid = smoothed * inv_yz * inv_x(p)
        return jnp.where(e == 1, 0.0, jnp.where(s == 1, 1.0, solid))

    before = density(filter_xz(PAD - 2, 2)[:, 1], PAD - 1, flx[0], flx[1])
    cub[:, PAD - 1] = there_x * (before * before * before)

    def density_body(i, acc):
        p = PAD + 8 * i
        smoothed = filter_xz(p, 8)
        for u in range(8):
            x = 8 * i + u
            rho = density(smoothed[:, u], p + u, flg[0, :, x], flg[1, :, x])
            ph[:, x] = rho
            cub[:, p + u] = rho * rho * rho
            acc = acc + rho
        return acc

    occupied = lax.fori_loop(0, n // 8, density_body, jnp.zeros(shape, F32))

    for h in range(2):
        cubs[0, h] = row_pack(cub, h, 0, end, 7)
    cube_moving = [send(cubs, cube, 0, 1)]

    def gather_body(i, last):
        for u in range(4):
            now = spread(cub[:, PAD + 4 * i + u])
            ca[:, 4 * i + u] = now + last
            last = now
        return last

    lax.fori_loop(0, n // 4, gather_body, spread(cub[:, PAD - 1]))

    arrived(fields_moving)

    @pl.when(last_x)
    def _():
        fld[:, :, end] = jnp.zeros((3, 2, 8, 128), F32)
        flo[:, :, end : end + PAD] = jnp.zeros((3, 2, PAD, 128), F32)
        fhi[:, :, end : end + PAD] = jnp.zeros((3, 2, PAD, 128), F32)

    @pl.when(last_y)
    def _():
        fhi[...] = jnp.zeros((3, 2, end + PAD, 128), F32)

    weights = ((0.001, 0.999), (0.05, 0.95), (0.05, 0.95))

    def apply_main(f):
        base, slope = weights[f]

        def forward(p):
            return yz_forward(fld[f, :, p], fhi[f, :, pl.ds(p, 1)])

        def element(a, b, w):
            return x_backward(*weigh(*x_forward(a, b), w))

        a = forward(PAD - 1)
        b = forward(PAD)
        _, behind = element(a, b, there_x * base + slope * cub[:, PAD - 1])

        def body(i, carry):
            a, behind = carry
            for u in range(2):
                x = 2 * i + u
                b = forward(PAD + x + 1)
                front, new = element(a, b, base + slope * cub[:, PAD + x])
                kap[f, :, x] = yz_backward([front[c] + behind[c] for c in range(4)])
                a, behind = b, new
            return tuple(a), tuple(new)

        lax.fori_loop(0, n // 2, body, (tuple(b), tuple(behind)))

    def edge_weight(base, slope):
        where = lax.broadcasted_iota(jnp.int32, (2, end, 128), 1)
        real = jnp.where(where == PAD - 1, there_x, 1.0) * there_y
        return base * real + (slope * there_y) * cube[0]

    def apply_edge(f):
        low, own = flo[f, :, 0:end], fdn[f]
        mine = jnp.concatenate([fld_first(f, PAD - 8, 8), own], axis=1)
        s, d = mine + low, mine - low
        a = z_forward_rows(s, d)
        last_own = fld_first(f, end, 1)
        last_low = flo[f, :, end : end + 1]
        b_end = z_forward_rows(last_own + last_low, last_own - last_low)
        where = lax.broadcasted_iota(jnp.int32, (2, end, 128), 1)
        b = [
            jnp.where(where == end - 1, jnp.broadcast_to(b_end[c], a[c].shape), pltpu.roll(a[c], end - 1, axis=1))
            for c in range(4)
        ]
        front, behind = x_backward(*weigh(*x_forward(a, b), edge_weight(*weights[f])))
        m = [front[c] + pltpu.roll(behind[c], 1, axis=1) for c in range(4)]
        ns, nd = m[0] + m[2], m[1] + m[3]
        out = (ns - nd) + z_prev(ns + nd)
        for h in range(2):
            row_add(kap.at[f], h, 0, n, 0, out[h, PAD:end])

    def fld_first(f, p, planes):
        return jnp.stack([row_pack(fld.at[f], h, p, planes, 0) for h in range(2)])

    apply_main(0)

    arrived(cube_moving)
    apply_edge(0)
    edge_cube = cube[0] * there_y
    edge_cube = edge_cube + pltpu.roll(edge_cube, 1, axis=1)
    edge_cube = edge_cube + z_prev(edge_cube)
    for h in range(2):
        row_add(ca, h, 0, n, 0, edge_cube[h, PAD:end])

    def pivot(x, base, slope):
        cx = jnp.where(gx * n + x == 0, 1.0, 2.0).astype(F32)
        return base * (cx * touch_yz) + slope * ca[:, x]

    loaded(8, 9)

    def volt_body(i, carry):
        for u in range(4):
            x = 4 * i + u
            v = raw[0, :, x]
            moved = 1.8 * (raw[3, :, x] - kap[0, :, x]) / pivot(x, 0.001, 0.999)
            v1[:, PAD + x] = v + jnp.where(flg[2, :, x] == 0, moved, -0.6 * v)
        return carry

    lax.fori_loop(0, n // 4, volt_body, 0)
    for h in range(2):
        v1up[0, h] = row_pack(v1, h, PAD, n, 7)
        v1dn[0, h] = row_pack(v1, h, PAD, n, 0)
    volt_moving = send_up(v1up, v1lo) + send_down(v1dn, v1hi)
    volt_moving += [
        send(v1.at[:, end - 1 : end], v1.at[:, PAD - 1 : PAD], 1, 0),
        send(v1.at[:, PAD : PAD + 1], v1.at[:, end : end + 1], -1, 0),
    ]
    stores = []

    def store(src, dst):
        for h in range(2):
            c = pltpu.make_async_copy(
                src(h), dst.at[:, :, pl.ds(128 * h, 128)], out_sem.at[len(stores)]
            )
            c.start()
            stores.append(c)

    store(lambda h: v1.at[h, PAD:end], v_out)

    apply_main(2)
    apply_edge(2)
    apply_main(1)
    apply_edge(1)

    def heat_body(i, carry):
        for u in range(2):
            x = 2 * i + u
            free = flg[3, :, x] == 0
            step = 1.8 / pivot(x, 0.05, 0.95)
            d = raw[2, :, x]
            d1[:, PAD + x] = d + jnp.where(free, step * (raw[4, :, x] - kap[2, :, x]), -0.6 * d)
            t = raw[1, :, x]
            t0[:, x] = t - jnp.where(free, step * kap[1, :, x], 0.6 * t)
            tr[:, x] = jnp.where(free, step, 0.0)
        return carry

    lax.fori_loop(0, n // 2, heat_body, 0)
    for h in range(2):
        d1dn[0, h] = row_pack(d1, h, PAD, n, 0)
    dual_moving = send_down(d1dn, d1hi, both=False)
    dual_moving.append(send(d1.at[:, PAD : PAD + 1], d1.at[:, end : end + 1], -1, 0))
    store(lambda h: d1.at[h, PAD:end], d_out)

    arrived(volt_moving)

    def clear_high(field, *edges):
        @pl.when(last_x)
        def _():
            field[:, end] = jnp.zeros((2, 8, 128), F32)
            for edge in edges:
                edge[0, :, end : end + PAD] = jnp.zeros((2, PAD, 128), F32)

        @pl.when(last_y)
        def _():
            edges[0][0] = jnp.zeros((2, end + PAD, 128), F32)

    clear_high(v1, v1hi, v1lo)

    def volt_forward(p):
        return yz_forward(v1[:, p], v1hi[0, :, pl.ds(p, 1)])

    a = volt_forward(PAD - 1)
    b = volt_forward(PAD)
    s, d = x_forward(a, b)
    lead = energy(s, d, s, d) * ((there_x * 0.001 + 0.999 * cub[:, PAD - 1]) / 8.0)

    def joule_body(i, carry):
        a, last, acc = carry
        for u in range(2):
            x = 2 * i + u
            b = volt_forward(PAD + x + 1)
            s, d = x_forward(a, b)
            e = energy(s, d, s, d)
            joule[:, x] = e
            now = spread(e * (0.001 / 8.0 + (0.999 / 8.0) * cub[:, PAD + x]))
            t = t0[:, x] + tr[:, x] * (now + last)
            t1[:, PAD + x] = t
            acc = acc + raw[4, :, x] * t
            a, last = b, now
        return tuple(a), last, acc

    _, _, warm = lax.fori_loop(
        0, n // 2, joule_body, (tuple(b), spread(lead), jnp.zeros(shape, F32))
    )

    def edge_heat():
        low = v1lo[0, :, 0:end]
        own = jnp.stack([row_pack(v1, h, 0, end, 0) for h in range(2)])
        a = z_forward_rows(own + low, own - low)
        last_own = jnp.stack([row_pack(v1, h, end, 1, 0) for h in range(2)])
        last_low = v1lo[0, :, end : end + 1]
        b_end = z_forward_rows(last_own + last_low, last_own - last_low)
        where = lax.broadcasted_iota(jnp.int32, (2, end, 128), 1)
        b = [
            jnp.where(where == end - 1, jnp.broadcast_to(b_end[c], a[c].shape), pltpu.roll(a[c], end - 1, axis=1))
            for c in range(4)
        ]
        s, d = x_forward(a, b)
        e = energy(s, d, s, d) * (edge_weight(0.001, 0.999) * 0.125)
        e = e + pltpu.roll(e, 1, axis=1)
        return (e + z_prev(e))[:, PAD:end]

    extra = edge_heat()
    warm_rows = jnp.zeros((8, 128), F32)
    for h in range(2):
        more = extra[h] * row_pack(tr, h, 0, n, 0)
        row_add(t1, h, PAD, n, 0, more)
        warm_rows = warm_rows + jnp.sum(
            (more * row_pack(raw.at[4], h, 0, n, 0)).reshape(n // 8, 8, 128), axis=0
        )
        t1dn[0, h] = row_pack(t1, h, PAD, n, 0)
    temp_moving = send_down(t1dn, t1hi, both=False)
    temp_moving.append(send(t1.at[:, PAD : PAD + 1], t1.at[:, end : end + 1], -1, 0))
    store(lambda h: t1.at[h, PAD:end], t_out)

    arrived(dual_moving)
    arrived(temp_moving)
    clear_high(d1, d1hi)
    clear_high(t1, t1hi)

    def pair_forward(p):
        return (
            tuple(yz_forward(t1[:, p], t1hi[0, :, pl.ds(p, 1)])),
            tuple(yz_forward(d1[:, p], d1hi[0, :, pl.ds(p, 1)])),
        )

    def sens_body(i, carry):
        ta, da = carry
        for u in range(2):
            x = 2 * i + u
            tb, db = pair_forward(PAD + x + 1)
            ts, td = x_forward(ta, tb)
            ds, dd = x_forward(da, db)
            mean = (0.999 / 8.0) * (da[0] + db[0])
            rho = ph[:, x]
            raw_value = joule[:, x] * mean - 0.95 * energy(ts, td, ds, dd)
            value = (3.0 * rho * rho) * raw_value * inv_yz * inv_x(PAD + x)
            held = (flg[0, :, x] + flg[1, :, x]) == 0
            sen[:, PAD + x] = jnp.where(held, value, 0.0)
            ta, da = tb, db
        return ta, da

    lax.fori_loop(0, n // 2, sens_body, pair_forward(PAD))
    tails(sen, sup, sdn)
    sens_moving = send_up(sup, scc.at[0:3]) + send_down(sdn, scc.at[5:8])
    sens_moving += [
        send(sen.at[:, end - 3 : end], sen.at[:, PAD - 3 : PAD], 1, 0),
        send(sen.at[:, PAD : PAD + 3], sen.at[:, end : end + 3], -1, 0),
    ]
    arrived(sens_moving)
    clear(scc, sen, 3, 3)
    filter_y_all(sen, scc, 3)

    def last_body(i, acc):
        out = filter_xz(PAD + 8 * i, 8)
        fil[:, pl.ds(8 * i, 8)] = out
        return acc + jnp.sum(out * out, axis=1)

    square = lax.fori_loop(0, n // 8, last_body, jnp.zeros(shape, F32))

    def fold(a):
        return jnp.sum(a, axis=0, keepdims=True)

    message = jnp.concatenate(
        [
            fold(square[0] + square[1]),
            fold(occupied[0] + occupied[1]),
            fold(warm[0] + warm[1] + warm_rows),
            jnp.zeros((5, 128), F32),
        ],
        axis=0,
    )

    def exchange(value, slots, me, size, peer, sends, recvs):
        slots[me] = value
        out = []
        for k in range(1, size):
            c = pltpu.make_async_remote_copy(
                src_ref=slots.at[me], dst_ref=slots.at[me], send_sem=sends.at[k],
                recv_sem=recvs.at[me], device_id=peer(k), device_id_type=MESH,
            )
            c.start()
            out.append(c)
        for k in range(1, size):
            source = lax.rem(me + k, size)
            pltpu.make_async_remote_copy(
                src_ref=slots.at[source], dst_ref=slots.at[source], send_sem=sends.at[k],
                recv_sem=recvs.at[source], device_id=peer(k), device_id_type=MESH,
            ).wait_recv()
        for c in out:
            c.wait_send()
        result = slots[0]
        for k in range(1, size):
            result = result + slots[k]
        return result

    message = exchange(message, slots1, me1, group, peer1, r1_send, r1_recv)
    message = exchange(message, slots2, me2, nx * blocks, peer2, r2_send, r2_recv)
    sums = jnp.sum(message, axis=1, keepdims=True)
    scale = 1.0 / jnp.sqrt(sums[0:1] * (1.0 / total) + 1e-6)
    scale = jnp.broadcast_to(scale, (8, 128))

    def scale_body(i, carry):
        fil[:, pl.ds(8 * i, 8)] = fil[:, pl.ds(8 * i, 8)] * scale
        return carry

    lax.fori_loop(0, n // 8, scale_body, 0)
    store(lambda h: fil.at[h], f_out)
    occ_out[...] = jnp.broadcast_to(sums[1:2] * (1.0 / total), (8, 128))
    mean_out[...] = jnp.broadcast_to(sums[2:3] * (1.0 / total), (8, 128))
    for c in pending:
        c.wait_send()
    for c in stores:
        c.wait()


def per_device(nx, ny, *args):
    n = args[0].shape[0]
    assert args[0].shape[1:] == (8, 256) and n % 8 == 0
    field = jax.ShapeDtypeStruct(args[0].shape, F32)
    tile = jax.ShapeDtypeStruct((8, 128), F32)
    wide = n + 2 * PAD

    def vm(*shape, dtype=F32):
        return pltpu.VMEM(shape, dtype)

    planes = vm(2, wide, 8, 128)
    own = vm(2, n, 8, 128)
    edge = vm(1, 2, wide, 128)
    edge_out = vm(1, 2, n, 128)
    group = min(16, ny)
    second = nx * (ny // group)
    scratch = [
        planes, vm(5, 2, n, 8, 128), vm(4, 2, n, 8, 128, dtype=jnp.int32),
        vm(3, 2, wide, 8, 128), vm(2, 2, 8, 128, dtype=jnp.int32),
        vm(8, 2, wide, 128), vm(3, 2, n, 128), vm(3, 2, n, 128),
        vm(3, 2, wide, 128), vm(3, 2, wide, 128), vm(3, 2, n, 128), vm(3, 2, n, 128),
        vm(256, 256, dtype=BF16), planes, own, planes,
        vm(1, 2, PAD + n, 128), vm(1, 2, PAD + n, 128), own,
        vm(3, 2, n, 8, 128), planes, edge, edge, edge_out, edge_out,
        planes, edge, edge_out, own, own, planes, edge, edge_out, own,
        planes, vm(8, 2, wide, 128), vm(3, 2, n, 128), vm(3, 2, n, 128), own,
        vm(group, 8, 128), vm(second, 8, 128),
        pltpu.SemaphoreType.DMA((20,)), pltpu.SemaphoreType.DMA((8,)),
        pltpu.SemaphoreType.DMA((48,)), pltpu.SemaphoreType.DMA((48,)),
        pltpu.SemaphoreType.DMA((group,)), pltpu.SemaphoreType.DMA((group,)),
        pltpu.SemaphoreType.DMA((second,)), pltpu.SemaphoreType.DMA((second,)),
    ]
    anywhere = pl.BlockSpec(memory_space=pl.ANY)
    vmem = pl.BlockSpec(memory_space=pltpu.VMEM)
    out = pl.pallas_call(
        functools.partial(kernel, nx, ny, n),
        out_shape=(field, field, field, field, tile, tile),
        in_specs=[anywhere] * 10,
        out_specs=(anywhere,) * 4 + (vmem, vmem),
        scratch_shapes=scratch,
        compiler_params=pltpu.CompilerParams(
            collective_id=0, has_side_effects=True, vmem_limit_bytes=56 * 1024 * 1024
        ),
    )(*args)
    return out[:4] + (out[4][0, 0], out[5][0, 0])


def solution(mesh):
    spec = P("gx", "gy", None)
    return jax.shard_map(
        functools.partial(per_device, mesh.shape["gx"], mesh.shape["gy"]),
        mesh=mesh,
        in_specs=(spec,) * 10,
        out_specs=(spec,) * 4 + (P(), P()),
        check_vma=False,
    )
```

```python
import functools

import jax
import jax.numpy as jnp
from jax import lax
from jax.experimental import pallas as pl
from jax.experimental.pallas import tpu as pltpu
from jax.sharding import PartitionSpec as P

MESH = pl.DeviceIdType.MESH
F32 = jnp.float32
BF16 = jnp.bfloat16
PAD = 8
OFFSETS = ((0, 1), (0, -1), (1, 1), (-1, 1), (1, -1), (-1, -1), (1, 0), (-1, 0))


def lanes(shape):
    return lax.broadcasted_iota(jnp.int32, shape, len(shape) - 1)


def z_next(p):
    r = pltpu.roll(p, 127, axis=p.ndim - 1)
    lane = lanes(p.shape[1:])
    low = jnp.where(lane < 127, r[0], r[1])
    high = jnp.where(lane < 127, r[1], 0.0)
    return jnp.stack([low, high])


def z_prev(p):
    r = pltpu.roll(p, 1, axis=p.ndim - 1)
    lane = lanes(p.shape[1:])
    low = jnp.where(lane > 0, r[0], 0.0)
    high = jnp.where(lane > 0, r[1], r[0])
    return jnp.stack([low, high])


def rows_of(shape):
    return lax.broadcasted_iota(jnp.int32, shape, len(shape) - 2)


def y_next(p, row):
    r = pltpu.roll(p, 7, axis=1)
    return jnp.where(rows_of(p.shape) < 7, r, jnp.broadcast_to(row, p.shape))


def y_prev(p):
    r = pltpu.roll(p, 1, axis=1)
    return jnp.where(rows_of(p.shape) > 0, r, 0.0)


def z_forward(p):
    q = z_next(p)
    return p + q, q - p


def yz_forward(p, row_s, row_d):
    s, d = z_forward(p)
    sy, dy = y_next(s, row_s), y_next(d, row_d)
    return s + sy, d + dy, sy - s, dy - d


def rows_forward(near, far):
    (s, d), (sy, dy) = z_forward(near), z_forward(far)
    return s + sy, d + dy, sy - s, dy - d


def planes_after(p):
    return pltpu.roll(p, p.shape[1] - 1, axis=1)


def planes_before(p):
    return pltpu.roll(p, 1, axis=1)


def x_forward(a, b):
    return [a[i] + b[i] for i in range(1, 4)], [b[i] - a[i] for i in range(4)]


def weigh(sums, diffs, w):
    w1, w2, w3 = w * (1.0 / 48.0), w * (1.0 / 24.0), w * (1.0 / 16.0)
    return (
        [w3 * sums[0], w3 * sums[1], w2 * sums[2]],
        [w3 * diffs[0], w2 * diffs[1], w2 * diffs[2], w1 * diffs[3]],
    )


def x_backward(sums, diffs):
    front = [-diffs[0]] + [sums[i] - diffs[i + 1] for i in range(3)]
    behind = [diffs[0]] + [sums[i] + diffs[i + 1] for i in range(3)]
    return front, behind


def yz_backward(n):
    ns = (n[0] - n[2]) + y_prev(n[0] + n[2])
    nd = (n[1] - n[3]) + y_prev(n[1] + n[3])
    return (ns - nd) + z_prev(ns + nd)


def energy(sa, da, sb, db):
    three = da[0] * db[0] + sa[0] * sb[0] + sa[1] * sb[1]
    two = da[1] * db[1] + da[2] * db[2] + sa[2] * sb[2]
    return (1.0 / 16.0) * three + (1.0 / 24.0) * two + (1.0 / 48.0) * (da[3] * db[3])


def spread(p):
    t = p + y_prev(p)
    return t + z_prev(t)


def row_pack(ref, h, first, planes, row):
    every = ref.shape[1]
    flat = ref.reshape(2 * every * 8, 128)
    return flat[pl.ds((h * every + first) * 8 + row, planes, stride=8), :]


def row_add(ref, h, first, planes, row, value):
    every = ref.shape[1]
    flat = ref.reshape(2 * every * 8, 128)
    where = pl.ds((h * every + first) * 8 + row, planes, stride=8)
    flat[where, :] = flat[where, :] + value


def edge_column(edge, h, p):
    every = edge.shape[2]
    flat = edge.reshape(8 * 2 * every, 128)
    return flat[pl.ds(h * every + p, 8, stride=2 * every), :]


def kernel(
    nx, ny, n,
    des_in, v_in, t_in, d_in, q_in, o_in, e_in, s_in, g_in, c_in,
    v_out, t_out, d_out, f_out, sums_out,
    des, raw, flg, fld, flx, zrow, coef,
    cc, cup, cdn, flo, fhi, fup, fdn,
    wz, yf, cub, cube, cubs, ca,
    kap, v1, v1lo, v1hi, v1up, v1dn,
    d1, d1hi, d1dn, t0, tr, t1, t1hi, t1dn, joule,
    sen, scc, sup, sdn, fil, slots1, slots2,
    in_sem, out_sem, send_sem, recv_sem, r1_send, r1_recv, r2_send, r2_recv,
):
    gx, gy = lax.axis_index("gx"), lax.axis_index("gy")
    group = min(16, ny)
    blocks = ny // group
    total = float(nx * n * ny * 8 * 256)
    end = PAD + n
    first_x, last_x = gx == 0, gx == nx - 1
    first_y, last_y = gy == 0, gy == ny - 1

    barrier = pltpu.get_barrier_semaphore()

    def device(dx, dy):
        return (lax.rem(gx + (nx + dx), nx), lax.rem(gy + (ny + dy), ny))

    me1, block = lax.rem(gy, group), lax.div(gy, group)
    me2 = gx * blocks + block

    def peer1(k):
        return (gx, block * group + lax.rem(me1 + k, group))

    def peer2(k):
        other = lax.rem(me2 + k, nx * blocks)
        return (lax.div(other, blocks), lax.rem(other, blocks) * group + me1)

    for dx, dy in OFFSETS:
        pl.semaphore_signal(barrier, inc=1, device_id=device(dx, dy), device_id_type=MESH)
    loads = []
    plan = [
        (des_in, lambda h: des.at[h, PAD:end]),
        (v_in, lambda h: raw.at[0, h]),
        (g_in, lambda h: flg.at[2, h]),
        (t_in, lambda h: raw.at[1, h]),
        (d_in, lambda h: raw.at[2, h]),
        (c_in, lambda h: flg.at[3, h]),
        (e_in, lambda h: flg.at[0, h]),
        (s_in, lambda h: flg.at[1, h]),
        (q_in, lambda h: raw.at[3, h]),
        (o_in, lambda h: raw.at[4, h]),
    ]
    for i, (src, dst) in enumerate(plan):
        pair = []
        for h in range(2):
            c = pltpu.make_async_copy(
                src.at[:, :, pl.ds(128 * h, 128)], dst(h), in_sem.at[2 * i + h]
            )
            c.start()
            pair.append(c)
        loads.append(pair)

    def loaded(*which):
        for i in which:
            for c in loads[i]:
                c.wait()

    for k in range(1, group):
        pl.semaphore_signal(barrier, inc=1, device_id=peer1(k), device_id_type=MESH)
    for k in range(1, nx * blocks):
        pl.semaphore_signal(barrier, inc=1, device_id=peer2(k), device_id_type=MESH)

    count = [0]

    def send(src, dst, dx, dy):
        k = count[0]
        count[0] += 1
        c = pltpu.make_async_remote_copy(
            src_ref=src, dst_ref=dst, send_sem=send_sem.at[k], recv_sem=recv_sem.at[k],
            device_id=device(dx, dy), device_id_type=MESH,
        )
        c.start()
        return c

    def send_up(src, dst):
        return [
            send(src, dst.at[:, :, PAD:end], 0, 1),
            send(src.at[:, :, n - PAD : n], dst.at[:, :, 0:PAD], 1, 1),
            send(src.at[:, :, 0:PAD], dst.at[:, :, end : end + PAD], -1, 1),
        ]

    def send_down(src, dst, both=True):
        some = [
            send(src, dst.at[:, :, PAD:end], 0, -1),
            send(src.at[:, :, 0:PAD], dst.at[:, :, end : end + PAD], -1, -1),
        ]
        if both:
            some.append(send(src.at[:, :, n - PAD : n], dst.at[:, :, 0:PAD], 1, -1))
        return some

    pending = []

    def arrived(copies):
        for c in copies:
            c.wait_recv()
        pending.extend(copies)

    def tails(ref, up, down):
        for h in range(2):
            r = [row_pack(ref, h, PAD, n, j) for j in (0, 1, 2, 5, 6, 7)]
            up[0, h] = r[3] + 2.0 * r[4] + 3.0 * r[5]
            up[1, h] = r[4] + 2.0 * r[5]
            up[2, h] = r[5]
            down[0, h] = r[0]
            down[1, h] = 2.0 * r[0] + r[1]
            down[2, h] = 3.0 * r[0] + 2.0 * r[1] + r[2]

    zero_rows = jnp.zeros((2, 2, end + PAD, 128), F32)
    cc[3:5] = zero_rows
    scc[3:5] = zero_rows
    wi = lax.broadcasted_iota(jnp.int32, (256, 256), 0)
    wj = lax.broadcasted_iota(jnp.int32, (256, 256), 1)
    wz[...] = jnp.maximum(4 - jnp.abs(wi - wj), 0).astype(F32).astype(BF16)

    loaded(0)
    tails(des, cup, cdn)
    loaded(1, 2, 3, 4, 5)

    def mask_body(i, carry):
        x = i * 8
        free_e = flg[2, :, pl.ds(x, 8)] == 0
        free_t = flg[3, :, pl.ds(x, 8)] == 0
        fld[0, :, pl.ds(PAD + x, 8)] = jnp.where(free_e, raw[0, :, pl.ds(x, 8)], 0.0)
        fld[1, :, pl.ds(PAD + x, 8)] = jnp.where(free_t, raw[1, :, pl.ds(x, 8)], 0.0)
        fld[2, :, pl.ds(PAD + x, 8)] = jnp.where(free_t, raw[2, :, pl.ds(x, 8)], 0.0)
        return carry

    lax.fori_loop(0, n // 8, mask_body, 0)
    for f in range(3):
        for h in range(2):
            fup[f, h] = row_pack(fld.at[f], h, PAD, n, 7)
            fdn[f, h] = row_pack(fld.at[f], h, PAD, n, 0)
    loaded(6, 7)
    pl.semaphore_wait(barrier, len(OFFSETS) + group - 1 + nx * blocks - 1)
    moving = send_up(cup, cc.at[0:3]) + send_down(cdn, cc.at[5:8])
    moving += [
        send(des.at[:, end - 4 : end], des.at[:, PAD - 4 : PAD], 1, 0),
        send(des.at[:, PAD : PAD + 3], des.at[:, end : end + 3], -1, 0),
        send(flg.at[0:2, :, n - 1], flx, 1, 0),
    ]
    fields_moving = send_up(fup, flo) + send_down(fdn, fhi)
    fields_moving += [
        send(fld.at[:, :, end - 1 : end], fld.at[:, :, PAD - 1 : PAD], 1, 0),
        send(fld.at[:, :, PAD : PAD + 1], fld.at[:, :, end : end + 1], -1, 0),
    ]

    row = lax.broadcasted_iota(jnp.int32, (8, 128), 0)

    def filter_y(ref, p):
        for h in range(2):
            a = ref[h, p]
            out = 4.0 * a
            for k in (1, 2, 3):
                out += jnp.where(row < 8 - k, float(4 - k), 0.0) * pltpu.roll(a, 8 - k, axis=0)
                out += jnp.where(row >= k, float(4 - k), 0.0) * pltpu.roll(a, k, axis=0)
            yf[h, p] = out

    def filter_y_own(ref):
        def body(i, carry):
            for u in range(8):
                filter_y(ref, PAD + 8 * i + u)
            return carry

        lax.fori_loop(0, n // 8, body, 0)

    def filter_y_rest(ref, edge, low):
        outer = list(range(PAD - low, PAD)) + list(range(end, end + 3))
        for p in outer:
            filter_y(ref, p)

        def add(p):
            for h in range(2):
                yf[h, p] += edge_column(edge, h, p)

        def body(i, carry):
            for u in range(8):
                add(PAD + 8 * i + u)
            return carry

        lax.fori_loop(0, n // 8, body, 0)
        for p in outer:
            add(p)

    def filter_xz(p, planes):
        halves = []
        for h in range(2):
            a = yf[h, pl.ds(p - 3, planes + 6)]
            a = a[:-1] + a[1:]
            a = a[:-2] + a[2:]
            a = a[:-1] + a[1:]
            a = a[:-2] + a[2:]
            halves.append(a.reshape(planes * 8, 128))
        a = jnp.concatenate(halves, axis=1)
        high = a.astype(BF16)
        rest = a - high.astype(F32)
        mid = rest.astype(BF16)
        low = (rest - mid.astype(F32)).astype(BF16)
        w = wz[...]
        out = (
            jnp.dot(low, w, preferred_element_type=F32)
            + jnp.dot(mid, w, preferred_element_type=F32)
            + jnp.dot(high, w, preferred_element_type=F32)
        )
        return jnp.stack(
            [out[:, :128].reshape(planes, 8, 128), out[:, 128:].reshape(planes, 8, 128)]
        )

    def inverse_window(i, full):
        w = jnp.where(i == 0, 10, jnp.where(i == 1, 13, jnp.where(i == 2, 15, 16)))
        k = full - 1 - i
        return jnp.where(k == 0, w - 6, jnp.where(k == 1, w - 3, jnp.where(k == 2, w - 1, w)))

    shape = (2, 8, 128)
    yy = gy * 8 + lax.broadcasted_iota(jnp.int32, shape, 1)
    zz = lax.broadcasted_iota(jnp.int32, shape, 0) * 128 + lax.broadcasted_iota(jnp.int32, shape, 2)
    inv_yz = 1.0 / (inverse_window(yy, ny * 8) * inverse_window(zz, 256)).astype(F32)
    touch_yz = (jnp.where(yy == 0, 1, 2) * jnp.where(zz == 0, 1, 2)).astype(F32)

    def inv_x(p):
        i = gx * n + (p - PAD)
        full = nx * n
        r = jnp.where(i == 0, 1 / 10.0, jnp.where(i == 1, 1 / 13.0, jnp.where(i == 2, 1 / 15.0, 1 / 16.0)))
        k = full - 1 - i
        return jnp.where(
            k == 0, 1 / 10.0, jnp.where(k == 1, 1 / 13.0, jnp.where(k == 2, 1 / 15.0, r))
        ).astype(F32)

    filter_y_own(des)
    arrived(moving)

    def clear(edge, field, low, high):
        @pl.when(first_x)
        def _():
            if low:
                field[:, PAD - low : PAD] = jnp.zeros((2, low, 8, 128), F32)
            edge[:, :, 0:PAD] = jnp.zeros((8, 2, PAD, 128), F32)

        @pl.when(last_x)
        def _():
            field[:, end : end + high] = jnp.zeros((2, high, 8, 128), F32)
            edge[:, :, end : end + PAD] = jnp.zeros((8, 2, PAD, 128), F32)

        @pl.when(first_y)
        def _():
            edge[0:3] = jnp.zeros((3, 2, end + PAD, 128), F32)

        @pl.when(last_y)
        def _():
            edge[5:8] = jnp.zeros((3, 2, end + PAD, 128), F32)

    clear(cc, des, 4, 3)
    filter_y_rest(des, cc, 4)
    there_x = jnp.where(first_x, 0.0, 1.0).astype(F32)
    there_y = jnp.where(first_y, 0.0, 1.0).astype(F32)

    def density(smoothed, p, e, s):
        solid = smoothed * inv_yz * inv_x(p)
        return jnp.where(e == 1, 0.0, jnp.where(s == 1, 1.0, solid))

    before = density(filter_xz(PAD - 2, 2)[:, 1], PAD - 1, flx[0], flx[1])
    cub[:, PAD - 1] = there_x * (before * before * before)

    def density_body(i, acc):
        p = PAD + 8 * i
        smoothed = filter_xz(p, 8)
        for u in range(8):
            x = 8 * i + u
            rho = density(smoothed[:, u], p + u, flg[0, :, x], flg[1, :, x])
            squared = rho * rho
            held = (flg[0, :, x] + flg[1, :, x]) == 0
            coef[:, x] = jnp.where(held, (3.0 * squared) * inv_yz * inv_x(p + u), 0.0)
            cub[:, p + u] = squared * rho
            acc = acc + rho
        return acc

    occupied = lax.fori_loop(0, n // 8, density_body, jnp.zeros(shape, F32))

    for h in range(2):
        cubs[0, h] = row_pack(cub, h, 0, end, 7)
    cube_moving = [send(cubs, cube.at[:, :, 0:end], 0, 1)]

    def gather_body(i, last):
        for u in range(8):
            now = spread(cub[:, PAD + 8 * i + u])
            ca[:, 8 * i + u] = now + last
            last = now
        return last

    lax.fori_loop(0, n // 8, gather_body, spread(cub[:, PAD - 1]))

    arrived(fields_moving)

    @pl.when(last_x)
    def _():
        fld[:, :, end] = jnp.zeros((3, 2, 8, 128), F32)
        flo[:, :, end : end + PAD] = jnp.zeros((3, 2, PAD, 128), F32)
        fhi[:, :, end : end + PAD] = jnp.zeros((3, 2, PAD, 128), F32)

    @pl.when(last_y)
    def _():
        fhi[...] = jnp.zeros((3, 2, end + PAD, 128), F32)

    def far_rows(k, edge):
        s, d = z_forward(edge)
        zrow[k, 0] = s
        zrow[k, 1] = d

    def forward_of(field, k):
        def forward(p):
            return yz_forward(
                field[:, p], zrow[k, 0, :, pl.ds(p, 1)], zrow[k, 1, :, pl.ds(p, 1)]
            )

        return forward

    for f in range(3):
        far_rows(f, fhi[f])
    weights = ((0.001, 0.999), (0.05, 0.95), (0.05, 0.95))

    def apply_main(f):
        base, slope = weights[f]

        forward = forward_of(fld.at[f], f)

        def element(a, b, w):
            return x_backward(*weigh(*x_forward(a, b), w))

        a = forward(PAD - 1)
        b = forward(PAD)
        _, behind = element(a, b, there_x * base + slope * cub[:, PAD - 1])

        def body(i, carry):
            a, behind = carry
            for u in range(8):
                x = 8 * i + u
                b = forward(PAD + x + 1)
                front, new = element(a, b, base + slope * cub[:, PAD + x])
                kap[f, :, x] = yz_backward([front[c] + behind[c] for c in range(4)])
                a, behind = b, new
            return tuple(a), tuple(new)

        lax.fori_loop(0, n // 8, body, (tuple(b), tuple(behind)))

    def edge_weight(base, slope):
        where = lax.broadcasted_iota(jnp.int32, (2, end + PAD, 128), 1)
        real = jnp.where(where == PAD - 1, there_x, 1.0) * there_y
        return base * real + (slope * there_y) * cube[0]

    def whole_row(ref, j):
        return jnp.stack([row_pack(ref, h, 0, end + PAD, j) for h in range(2)])

    def rows_x_forward(a):
        return x_forward(a, [planes_after(c) for c in a])

    def apply_edge(f):
        a = rows_forward(flo[f], whole_row(fld.at[f], 0))
        front, behind = x_backward(*weigh(*rows_x_forward(a), edge_weight(*weights[f])))
        m = [front[c] + planes_before(behind[c]) for c in range(4)]
        ns, nd = m[0] + m[2], m[1] + m[3]
        out = (ns - nd) + z_prev(ns + nd)
        for h in range(2):
            row_add(kap.at[f], h, 0, n, 0, out[h, PAD:end])

    apply_main(0)

    arrived(cube_moving)
    apply_edge(0)
    edge_cube = cube[0] * there_y
    edge_cube = edge_cube + planes_before(edge_cube)
    edge_cube = edge_cube + z_prev(edge_cube)
    for h in range(2):
        row_add(ca, h, 0, n, 0, edge_cube[h, PAD:end])

    def pivot(x, base, slope):
        cx = jnp.where(gx * n + x == 0, 1.0, 2.0).astype(F32)
        return base * (cx * touch_yz) + slope * ca[:, x]

    loaded(8, 9)

    def volt_body(i, carry):
        for u in range(8):
            x = 8 * i + u
            v = raw[0, :, x]
            moved = 1.8 * (raw[3, :, x] - kap[0, :, x]) / pivot(x, 0.001, 0.999)
            v1[:, PAD + x] = v + jnp.where(flg[2, :, x] == 0, moved, -0.6 * v)
        return carry

    lax.fori_loop(0, n // 8, volt_body, 0)
    for h in range(2):
        v1up[0, h] = row_pack(v1, h, PAD, n, 7)
        v1dn[0, h] = row_pack(v1, h, PAD, n, 0)
    volt_moving = send_up(v1up, v1lo) + send_down(v1dn, v1hi)
    volt_moving += [
        send(v1.at[:, end - 1 : end], v1.at[:, PAD - 1 : PAD], 1, 0),
        send(v1.at[:, PAD : PAD + 1], v1.at[:, end : end + 1], -1, 0),
    ]
    stores = []

    def store(src, dst):
        for h in range(2):
            c = pltpu.make_async_copy(
                src(h), dst.at[:, :, pl.ds(128 * h, 128)], out_sem.at[len(stores)]
            )
            c.start()
            stores.append(c)

    store(lambda h: v1.at[h, PAD:end], v_out)

    apply_main(2)
    apply_edge(2)
    apply_main(1)
    apply_edge(1)

    def heat_body(i, carry):
        for u in range(8):
            x = 8 * i + u
            free = flg[3, :, x] == 0
            step = 1.8 / pivot(x, 0.05, 0.95)
            d = raw[2, :, x]
            d1[:, PAD + x] = d + jnp.where(free, step * (raw[4, :, x] - kap[2, :, x]), -0.6 * d)
            t = raw[1, :, x]
            t0[:, x] = t - jnp.where(free, step * kap[1, :, x], 0.6 * t)
            tr[:, x] = jnp.where(free, step, 0.0)
        return carry

    lax.fori_loop(0, n // 8, heat_body, 0)
    for h in range(2):
        d1dn[0, h] = row_pack(d1, h, PAD, n, 0)
    dual_moving = send_down(d1dn, d1hi, both=False)
    dual_moving.append(send(d1.at[:, PAD : PAD + 1], d1.at[:, end : end + 1], -1, 0))
    store(lambda h: d1.at[h, PAD:end], d_out)

    arrived(volt_moving)

    def clear_high(field, *edges):
        @pl.when(last_x)
        def _():
            field[:, end] = jnp.zeros((2, 8, 128), F32)
            for edge in edges:
                edge[0, :, end : end + PAD] = jnp.zeros((2, PAD, 128), F32)

        @pl.when(last_y)
        def _():
            edges[0][0] = jnp.zeros((2, end + PAD, 128), F32)

    clear_high(v1, v1hi, v1lo)

    far_rows(3, v1hi[0])
    volt_forward = forward_of(v1, 3)
    a = volt_forward(PAD - 1)
    b = volt_forward(PAD)
    s, d = x_forward(a, b)
    lead = energy(s, d, s, d) * ((there_x * 0.001 + 0.999 * cub[:, PAD - 1]) / 8.0)

    def joule_body(i, carry):
        a, last, acc = carry
        for u in range(8):
            x = 8 * i + u
            b = volt_forward(PAD + x + 1)
            s, d = x_forward(a, b)
            e = energy(s, d, s, d)
            joule[:, x] = e
            now = spread(e * (0.001 / 8.0 + (0.999 / 8.0) * cub[:, PAD + x]))
            t = t0[:, x] + tr[:, x] * (now + last)
            t1[:, PAD + x] = t
            acc = acc + raw[4, :, x] * t
            a, last = b, now
        return tuple(a), last, acc

    _, _, warm = lax.fori_loop(
        0, n // 8, joule_body, (tuple(b), spread(lead), jnp.zeros(shape, F32))
    )

    def edge_heat():
        s, d = rows_x_forward(rows_forward(v1lo[0], whole_row(v1, 0)))
        e = energy(s, d, s, d) * (edge_weight(0.001, 0.999) * 0.125)
        e = e + planes_before(e)
        return (e + z_prev(e))[:, PAD:end]

    extra = edge_heat()
    warm_rows = jnp.zeros((8, 128), F32)
    for h in range(2):
        more = extra[h] * row_pack(tr, h, 0, n, 0)
        row_add(t1, h, PAD, n, 0, more)
        warm_rows = warm_rows + jnp.sum(
            (more * row_pack(raw.at[4], h, 0, n, 0)).reshape(n // 8, 8, 128), axis=0
        )
        t1dn[0, h] = row_pack(t1, h, PAD, n, 0)
    temp_moving = send_down(t1dn, t1hi, both=False)
    temp_moving.append(send(t1.at[:, PAD : PAD + 1], t1.at[:, end : end + 1], -1, 0))
    store(lambda h: t1.at[h, PAD:end], t_out)

    arrived(dual_moving)
    clear_high(d1, d1hi)
    far_rows(4, d1hi[0])
    dual_forward = forward_of(d1, 4)
    none = jnp.zeros((2, 1, 128), F32)

    def pair_forward(p):
        return tuple(yz_forward(t1[:, p], none, none)), tuple(dual_forward(p))

    def sens_body(i, carry):
        ta, da = carry
        for u in range(8):
            x = 8 * i + u
            tb, db = pair_forward(PAD + x + 1)
            ts, td = x_forward(ta, tb)
            ds, dd = x_forward(da, db)
            mean = (0.999 / 8.0) * (da[0] + db[0])
            value = joule[:, x] * mean - 0.95 * energy(ts, td, ds, dd)
            sen[:, PAD + x] = coef[:, x] * value
            ta, da = tb, db
        return ta, da

    carry = lax.fori_loop(0, n // 8 - 1, sens_body, pair_forward(PAD))
    dual_s, dual_d = rows_x_forward(rows_forward(whole_row(d1, 7), d1hi[0]))
    arrived(temp_moving)
    clear_high(t1, t1hi)
    sens_body(n // 8 - 1, carry)
    behind_s, behind_d = z_forward(t1hi[0])
    temp_s, temp_d = rows_x_forward((behind_s, behind_d, behind_s, behind_d))
    work = 0.95 * energy(temp_s, temp_d, dual_s, dual_d)
    for h in range(2):
        row_add(sen, h, PAD, n, 7, -work[h, PAD:end] * row_pack(coef, h, 0, n, 7))
    tails(sen, sup, sdn)
    sens_moving = send_up(sup, scc.at[0:3]) + send_down(sdn, scc.at[5:8])
    sens_moving += [
        send(sen.at[:, end - 3 : end], sen.at[:, PAD - 3 : PAD], 1, 0),
        send(sen.at[:, PAD : PAD + 3], sen.at[:, end : end + 3], -1, 0),
    ]
    filter_y_own(sen)

    def whole(a):
        return jnp.sum(jnp.sum(a, axis=0, keepdims=True), axis=1, keepdims=True)

    occupied_sum = whole(occupied[0] + occupied[1])
    warm_sum = whole(warm[0] + warm[1] + warm_rows)
    arrived(sens_moving)
    clear(scc, sen, 3, 3)
    filter_y_rest(sen, scc, 3)

    def last_body(i, acc):
        out = filter_xz(PAD + 8 * i, 8)
        fil[:, pl.ds(8 * i, 8)] = out
        return acc + jnp.sum(out * out, axis=1)

    square = lax.fori_loop(0, n // 8, last_body, jnp.zeros(shape, F32))
    store(lambda h: fil.at[h], f_out)

    lane = lax.broadcasted_iota(jnp.int32, (1, 128), 1)
    message = jnp.where(
        lane == 0,
        whole(square[0] + square[1]),
        jnp.where(lane == 1, occupied_sum, warm_sum),
    )

    def exchange(value, slots, me, size, peer, sends, recvs):
        slots[me, 0:1] = value
        for k in range(1, size):
            pltpu.make_async_remote_copy(
                src_ref=slots.at[me, pl.ds(0, 1)], dst_ref=slots.at[me, pl.ds(0, 1)],
                send_sem=sends.at[0], recv_sem=recvs.at[0],
                device_id=peer(k), device_id_type=MESH,
            ).start()
        others = slots.at[pl.ds(0, size - 1), pl.ds(0, 1)]
        every = pltpu.make_async_remote_copy(
            src_ref=others, dst_ref=others, send_sem=sends.at[0], recv_sem=recvs.at[0],
            device_id=peer(1), device_id_type=MESH,
        )
        every.wait_recv()
        pending.append(every)
        parts = [slots[k, 0:1] for k in range(size)]
        while len(parts) > 1:
            parts = [a + b for a, b in zip(parts[::2], parts[1::2])]
        return parts[0]

    message = exchange(message, slots1, me1, group, peer1, r1_send, r1_recv)
    message = exchange(message, slots2, me2, nx * blocks, peer2, r2_send, r2_recv)
    sums_out[...] = jnp.broadcast_to(message, (8, 128))
    for c in pending:
        c.wait_send()
    for c in stores:
        c.wait()


def finish(
    total, v, t, d, f, sums_ref, v_out, t_out, d_out, f_out, occ_out, mean_out, buf, sem
):
    copies = [
        pltpu.make_async_copy(src, dst, sem.at[i])
        for i, (src, dst) in enumerate(((f, buf), (v, v_out), (t, t_out), (d, d_out)))
    ]
    for c in copies:
        c.start()
    sums = sums_ref[0:1] * (1.0 / total)
    scale = jnp.broadcast_to(1.0 / jnp.sqrt(sums[:, 0:1] + 1e-6), (8, 256))
    occ_out[0] = sums[0, 1]
    mean_out[0] = sums[0, 2]
    copies[0].wait()
    parts = 4
    step = buf.shape[0] // parts
    for i in range(parts):
        part = pl.ds(step * i, step)
        buf[part] = buf[part] * scale
        c = pltpu.make_async_copy(buf.at[part], f_out.at[part], sem.at[4 + i])
        c.start()
        copies.append(c)
    for c in copies[1:]:
        c.wait()


def per_device(nx, ny, *args):
    n = args[0].shape[0]
    assert args[0].shape[1:] == (8, 256) and n % 8 == 0
    field = jax.ShapeDtypeStruct(args[0].shape, F32)
    tile = jax.ShapeDtypeStruct((8, 128), F32)
    wide = n + 2 * PAD

    def vm(*shape, dtype=F32):
        return pltpu.VMEM(shape, dtype)

    planes = vm(2, wide, 8, 128)
    own = vm(2, n, 8, 128)
    edge = vm(1, 2, wide, 128)
    edge_out = vm(1, 2, n, 128)
    group = min(16, ny)
    second = nx * (ny // group)
    scratch = [
        planes, vm(5, 2, n, 8, 128), vm(4, 2, n, 8, 128, dtype=jnp.int32),
        vm(3, 2, wide, 8, 128), vm(2, 2, 8, 128, dtype=jnp.int32),
        vm(5, 2, 2, wide, 128), own,
        vm(8, 2, wide, 128), vm(3, 2, n, 128), vm(3, 2, n, 128),
        vm(3, 2, wide, 128), vm(3, 2, wide, 128), vm(3, 2, n, 128), vm(3, 2, n, 128),
        vm(256, 256, dtype=BF16), planes, planes,
        edge, vm(1, 2, PAD + n, 128), own,
        vm(3, 2, n, 8, 128), planes, edge, edge, edge_out, edge_out,
        planes, edge, edge_out, own, own, planes, edge, edge_out, own,
        planes, vm(8, 2, wide, 128), vm(3, 2, n, 128), vm(3, 2, n, 128), own,
        vm(group, 8, 128), vm(second, 8, 128),
        pltpu.SemaphoreType.DMA((20,)), pltpu.SemaphoreType.DMA((8,)),
        pltpu.SemaphoreType.DMA((48,)), pltpu.SemaphoreType.DMA((48,)),
        pltpu.SemaphoreType.DMA((1,)), pltpu.SemaphoreType.DMA((1,)),
        pltpu.SemaphoreType.DMA((1,)), pltpu.SemaphoreType.DMA((1,)),
    ]
    anywhere = pl.BlockSpec(memory_space=pl.ANY)
    hbm = pl.BlockSpec(memory_space=pltpu.HBM)
    vmem = pl.BlockSpec(memory_space=pltpu.VMEM)
    smem = pl.BlockSpec(memory_space=pltpu.SMEM)
    *fields, sums = pl.pallas_call(
        functools.partial(kernel, nx, ny, n),
        out_shape=(field, field, field, field, tile),
        in_specs=[hbm] * 10,
        out_specs=(anywhere,) * 4 + (vmem,),
        scratch_shapes=scratch,
        compiler_params=pltpu.CompilerParams(
            collective_id=0, has_side_effects=True, vmem_limit_bytes=103 * 512 * 1024
        ),
    )(*args)
    one = jax.ShapeDtypeStruct((1,), F32)
    *outs, occupied, mean = pl.pallas_call(
        functools.partial(finish, float(nx * ny * n * 8 * 256)),
        out_shape=(field, field, field, field, one, one),
        in_specs=[anywhere] * 4 + [vmem],
        out_specs=(hbm,) * 4 + (smem, smem),
        scratch_shapes=[vm(n, 8, 256), pltpu.SemaphoreType.DMA((8,))],
        compiler_params=pltpu.CompilerParams(vmem_limit_bytes=8 * 1024 * 1024),
    )(*fields, sums)
    return (*outs, occupied.reshape(()), mean.reshape(()))


def solution(mesh):
    spec = P("gx", "gy", None)
    return jax.shard_map(
        functools.partial(per_device, mesh.shape["gx"], mesh.shape["gy"]),
        mesh=mesh,
        in_specs=(spec,) * 10,
        out_specs=(spec,) * 4 + (P(), P()),
        check_vma=False,
    )
```

```python
import functools

import jax
import jax.numpy as jnp
from jax import lax
from jax.experimental import pallas as pl
from jax.experimental.pallas import tpu as pltpu
from jax.sharding import PartitionSpec as P

MESH = pl.DeviceIdType.MESH
F32 = jnp.float32
BF16 = jnp.bfloat16
PAD = 8
OFFSETS = ((0, 1), (0, -1), (1, 1), (-1, 1), (1, -1), (-1, -1), (1, 0), (-1, 0))


def lanes(shape):
    return lax.broadcasted_iota(jnp.int32, shape, len(shape) - 1)


def z_next(p):
    r = pltpu.roll(p, 127, axis=p.ndim - 1)
    lane = lanes(p.shape[1:])
    low = jnp.where(lane < 127, r[0], r[1])
    high = jnp.where(lane < 127, r[1], 0.0)
    return jnp.stack([low, high])


def z_prev(p):
    r = pltpu.roll(p, 1, axis=p.ndim - 1)
    lane = lanes(p.shape[1:])
    low = jnp.where(lane > 0, r[0], 0.0)
    high = jnp.where(lane > 0, r[1], r[0])
    return jnp.stack([low, high])


def rows_of(shape):
    return lax.broadcasted_iota(jnp.int32, shape, len(shape) - 2)


def y_next(p, row):
    r = pltpu.roll(p, 7, axis=1)
    return jnp.where(rows_of(p.shape) < 7, r, jnp.broadcast_to(row, p.shape))


def y_prev(p):
    r = pltpu.roll(p, 1, axis=1)
    return jnp.where(rows_of(p.shape) > 0, r, 0.0)


def z_forward(p):
    q = z_next(p)
    return p + q, q - p


def yz_forward(p, row_s, row_d):
    s, d = z_forward(p)
    sy, dy = y_next(s, row_s), y_next(d, row_d)
    return s + sy, d + dy, sy - s, dy - d


def rows_forward(near, far):
    (s, d), (sy, dy) = z_forward(near), z_forward(far)
    return s + sy, d + dy, sy - s, dy - d


def planes_after(p):
    return pltpu.roll(p, p.shape[1] - 1, axis=1)


def planes_before(p):
    return pltpu.roll(p, 1, axis=1)


def x_forward(a, b):
    return [a[i] + b[i] for i in range(1, 4)], [b[i] - a[i] for i in range(4)]


def weigh(sums, diffs, w):
    w1, w2, w3 = w * (1.0 / 48.0), w * (1.0 / 24.0), w * (1.0 / 16.0)
    return (
        [w3 * sums[0], w3 * sums[1], w2 * sums[2]],
        [w3 * diffs[0], w2 * diffs[1], w2 * diffs[2], w1 * diffs[3]],
    )


def x_backward(sums, diffs):
    front = [-diffs[0]] + [sums[i] - diffs[i + 1] for i in range(3)]
    behind = [diffs[0]] + [sums[i] + diffs[i + 1] for i in range(3)]
    return front, behind


def yz_backward(n):
    ns = (n[0] - n[2]) + y_prev(n[0] + n[2])
    nd = (n[1] - n[3]) + y_prev(n[1] + n[3])
    return (ns - nd) + z_prev(ns + nd)


def energy(sa, da, sb, db):
    three = da[0] * db[0] + sa[0] * sb[0] + sa[1] * sb[1]
    two = da[1] * db[1] + da[2] * db[2] + sa[2] * sb[2]
    return (1.0 / 16.0) * three + (1.0 / 24.0) * two + (1.0 / 48.0) * (da[3] * db[3])


def spread(p):
    t = p + y_prev(p)
    return t + z_prev(t)


def row_pack(ref, h, first, planes, row):
    every = ref.shape[1]
    flat = ref.reshape(2 * every * 8, 128)
    return flat[pl.ds((h * every + first) * 8 + row, planes, stride=8), :]


def row_add(ref, h, first, planes, row, value):
    every = ref.shape[1]
    flat = ref.reshape(2 * every * 8, 128)
    where = pl.ds((h * every + first) * 8 + row, planes, stride=8)
    flat[where, :] = flat[where, :] + value


def edge_column(edge, h, p):
    every = edge.shape[2]
    flat = edge.reshape(8 * 2 * every, 128)
    return flat[pl.ds(h * every + p, 8, stride=2 * every), :]


def kernel(
    nx, ny, n,
    des_in, v_in, t_in, d_in, q_in, o_in, e_in, s_in, g_in, c_in,
    v_out, t_out, d_out, f_out, sums_out,
    des, raw, flg, fld, flx, zrow, coef,
    cc, cup, cdn, flo, fhi, fup, fdn,
    wz, yf, cub, cube, cubs, ca,
    kap, v1, v1lo, v1hi, v1up, v1dn,
    d1, d1hi, d1dn, t0, tr, t1, t1hi, t1dn, joule,
    sen, scc, sup, sdn, fil, slots1, slots2,
    in_sem, out_sem, send_sem, recv_sem, r1_send, r1_recv, r2_send, r2_recv,
):
    gx, gy = lax.axis_index("gx"), lax.axis_index("gy")
    total = float(nx * n * ny * 8 * 256)
    end = PAD + n
    first_x, last_x = gx == 0, gx == nx - 1
    first_y, last_y = gy == 0, gy == ny - 1

    barrier = pltpu.get_barrier_semaphore()

    def device(dx, dy):
        return (lax.rem(gx + (nx + dx), nx), lax.rem(gy + (ny + dy), ny))

    chip, core = lax.div(gy, 2), lax.rem(gy, 2)
    size1, size2 = nx * 2, ny // 2
    me1, me2 = gx * 2 + core, chip

    def peer1(k):
        other = lax.rem(me1 + k, size1)
        return (lax.div(other, 2), chip * 2 + lax.rem(other, 2))

    def peer2(k):
        return (gx, lax.rem(me2 + k, size2) * 2 + core)

    def farthest_first(size):
        return sorted(range(1, size), key=lambda k: abs(2 * k - size))

    for dx, dy in OFFSETS:
        pl.semaphore_signal(barrier, inc=1, device_id=device(dx, dy), device_id_type=MESH)
    loads = []
    plan = [
        (des_in, lambda h: des.at[h, PAD:end]),
        (v_in, lambda h: raw.at[0, h]),
        (g_in, lambda h: flg.at[2, h]),
        (t_in, lambda h: raw.at[1, h]),
        (d_in, lambda h: raw.at[2, h]),
        (c_in, lambda h: flg.at[3, h]),
        (e_in, lambda h: flg.at[0, h]),
        (s_in, lambda h: flg.at[1, h]),
        (q_in, lambda h: raw.at[3, h]),
        (o_in, lambda h: raw.at[4, h]),
    ]
    for i, (src, dst) in enumerate(plan):
        pair = []
        for h in range(2):
            c = pltpu.make_async_copy(
                src.at[:, :, pl.ds(128 * h, 128)], dst(h), in_sem.at[2 * i + h]
            )
            c.start()
            pair.append(c)
        loads.append(pair)

    def loaded(*which):
        for i in which:
            for c in loads[i]:
                c.wait()

    for k in farthest_first(size1):
        pl.semaphore_signal(barrier, inc=1, device_id=peer1(k), device_id_type=MESH)
    for k in farthest_first(size2):
        pl.semaphore_signal(barrier, inc=1, device_id=peer2(k), device_id_type=MESH)

    count = [0]

    def exists(dx, dy):
        x, y = gx + dx, gy + dy
        return (x >= 0) & (x < nx) & (y >= 0) & (y < ny)

    def send(src, dst, dx, dy):
        k = count[0]
        count[0] += 1
        c = pltpu.make_async_remote_copy(
            src_ref=src, dst_ref=dst, send_sem=send_sem.at[k], recv_sem=recv_sem.at[k],
            device_id=device(dx, dy), device_id_type=MESH,
        )

        @pl.when(exists(dx, dy))
        def _():
            c.start()

        return c, dx, dy

    def send_up(src, dst):
        return [
            send(src, dst.at[:, :, PAD:end], 0, 1),
            send(src.at[:, :, n - PAD : n], dst.at[:, :, 0:PAD], 1, 1),
            send(src.at[:, :, 0:PAD], dst.at[:, :, end : end + PAD], -1, 1),
        ]

    def send_down(src, dst, both=True):
        some = [
            send(src, dst.at[:, :, PAD:end], 0, -1),
            send(src.at[:, :, 0:PAD], dst.at[:, :, end : end + PAD], -1, -1),
        ]
        if both:
            some.append(send(src.at[:, :, n - PAD : n], dst.at[:, :, 0:PAD], 1, -1))
        return some

    pending = []

    def arrived(copies):
        for c, dx, dy in copies:

            @pl.when(exists(-dx, -dy))
            def _(c=c):
                c.wait_recv()

        pending.extend(copies)

    def tails(ref, up, down):
        for h in range(2):
            r = [row_pack(ref, h, PAD, n, j) for j in (0, 1, 2, 5, 6, 7)]
            up[0, h] = r[3] + 2.0 * r[4] + 3.0 * r[5]
            up[1, h] = r[4] + 2.0 * r[5]
            up[2, h] = r[5]
            down[0, h] = r[0]
            down[1, h] = 2.0 * r[0] + r[1]
            down[2, h] = 3.0 * r[0] + 2.0 * r[1] + r[2]

    zero_rows = jnp.zeros((2, 2, end + PAD, 128), F32)
    cc[3:5] = zero_rows
    scc[3:5] = zero_rows
    wi = lax.broadcasted_iota(jnp.int32, (256, 256), 0)
    wj = lax.broadcasted_iota(jnp.int32, (256, 256), 1)
    wz[...] = jnp.maximum(4 - jnp.abs(wi - wj), 0).astype(F32).astype(BF16)

    loaded(0)
    tails(des, cup, cdn)
    loaded(1, 2, 3, 4, 5)

    def mask_body(i, carry):
        x = i * 8
        free_e = flg[2, :, pl.ds(x, 8)] == 0
        free_t = flg[3, :, pl.ds(x, 8)] == 0
        fld[0, :, pl.ds(PAD + x, 8)] = jnp.where(free_e, raw[0, :, pl.ds(x, 8)], 0.0)
        fld[1, :, pl.ds(PAD + x, 8)] = jnp.where(free_t, raw[1, :, pl.ds(x, 8)], 0.0)
        fld[2, :, pl.ds(PAD + x, 8)] = jnp.where(free_t, raw[2, :, pl.ds(x, 8)], 0.0)
        return carry

    lax.fori_loop(0, n // 8, mask_body, 0)
    for f in range(3):
        for h in range(2):
            fup[f, h] = row_pack(fld.at[f], h, PAD, n, 7)
            fdn[f, h] = row_pack(fld.at[f], h, PAD, n, 0)
    loaded(6, 7)
    pl.semaphore_wait(barrier, len(OFFSETS) + size1 - 1 + size2 - 1)
    moving = send_up(cup, cc.at[0:3]) + send_down(cdn, cc.at[5:8])
    moving += [
        send(des.at[:, end - 4 : end], des.at[:, PAD - 4 : PAD], 1, 0),
        send(des.at[:, PAD : PAD + 3], des.at[:, end : end + 3], -1, 0),
        send(flg.at[0:2, :, n - 1], flx, 1, 0),
    ]

    def send_fields(a, b):
        return (
            send_up(fup.at[a:b], flo.at[a:b])
            + send_down(fdn.at[a:b], fhi.at[a:b])
            + [
                send(fld.at[a:b, :, end - 1 : end], fld.at[a:b, :, PAD - 1 : PAD], 1, 0),
                send(fld.at[a:b, :, PAD : PAD + 1], fld.at[a:b, :, end : end + 1], -1, 0),
            ]
        )

    volt_field_moving = send_fields(0, 1)

    row = lax.broadcasted_iota(jnp.int32, (8, 128), 0)

    def filter_y(ref, p):
        for h in range(2):
            a = ref[h, p]
            out = 4.0 * a
            for k in (1, 2, 3):
                out += jnp.where(row < 8 - k, float(4 - k), 0.0) * pltpu.roll(a, 8 - k, axis=0)
                out += jnp.where(row >= k, float(4 - k), 0.0) * pltpu.roll(a, k, axis=0)
            yf[h, p] = out

    def filter_y_own(ref):
        def body(i, carry):
            for u in range(8):
                filter_y(ref, PAD + 8 * i + u)
            return carry

        lax.fori_loop(0, n // 8, body, 0)

    def filter_y_rest(ref, edge, low):
        outer = list(range(PAD - low, PAD)) + list(range(end, end + 3))
        for p in outer:
            filter_y(ref, p)

        def add(p):
            for h in range(2):
                yf[h, p] += edge_column(edge, h, p)

        def body(i, carry):
            for u in range(8):
                add(PAD + 8 * i + u)
            return carry

        lax.fori_loop(0, n // 8, body, 0)
        for p in outer:
            add(p)

    def filter_xz(p, planes):
        halves = []
        for h in range(2):
            a = yf[h, pl.ds(p - 3, planes + 6)]
            a = a[:-1] + a[1:]
            a = a[:-2] + a[2:]
            a = a[:-1] + a[1:]
            a = a[:-2] + a[2:]
            halves.append(a.reshape(planes * 8, 128))
        a = jnp.concatenate(halves, axis=1)
        high = a.astype(BF16)
        rest = a - high.astype(F32)
        mid = rest.astype(BF16)
        low = (rest - mid.astype(F32)).astype(BF16)
        w = wz[...]
        out = (
            jnp.dot(low, w, preferred_element_type=F32)
            + jnp.dot(mid, w, preferred_element_type=F32)
            + jnp.dot(high, w, preferred_element_type=F32)
        )
        return jnp.stack(
            [out[:, :128].reshape(planes, 8, 128), out[:, 128:].reshape(planes, 8, 128)]
        )

    def inverse_window(i, full):
        w = jnp.where(i == 0, 10, jnp.where(i == 1, 13, jnp.where(i == 2, 15, 16)))
        k = full - 1 - i
        return jnp.where(k == 0, w - 6, jnp.where(k == 1, w - 3, jnp.where(k == 2, w - 1, w)))

    shape = (2, 8, 128)
    yy = gy * 8 + lax.broadcasted_iota(jnp.int32, shape, 1)
    zz = lax.broadcasted_iota(jnp.int32, shape, 0) * 128 + lax.broadcasted_iota(jnp.int32, shape, 2)
    inv_yz = 1.0 / (inverse_window(yy, ny * 8) * inverse_window(zz, 256)).astype(F32)
    touch_yz = (jnp.where(yy == 0, 1, 2) * jnp.where(zz == 0, 1, 2)).astype(F32)

    def inv_x(p):
        i = gx * n + (p - PAD)
        full = nx * n
        r = jnp.where(i == 0, 1 / 10.0, jnp.where(i == 1, 1 / 13.0, jnp.where(i == 2, 1 / 15.0, 1 / 16.0)))
        k = full - 1 - i
        return jnp.where(
            k == 0, 1 / 10.0, jnp.where(k == 1, 1 / 13.0, jnp.where(k == 2, 1 / 15.0, r))
        ).astype(F32)

    filter_y_own(des)
    arrived(moving)
    heat_fields_moving = send_fields(1, 3)

    def clear(edge, field, low, high):
        @pl.when(first_x)
        def _():
            if low:
                field[:, PAD - low : PAD] = jnp.zeros((2, low, 8, 128), F32)
            edge[:, :, 0:PAD] = jnp.zeros((8, 2, PAD, 128), F32)

        @pl.when(last_x)
        def _():
            field[:, end : end + high] = jnp.zeros((2, high, 8, 128), F32)
            edge[:, :, end : end + PAD] = jnp.zeros((8, 2, PAD, 128), F32)

        @pl.when(first_y)
        def _():
            edge[0:3] = jnp.zeros((3, 2, end + PAD, 128), F32)

        @pl.when(last_y)
        def _():
            edge[5:8] = jnp.zeros((3, 2, end + PAD, 128), F32)

    clear(cc, des, 4, 3)
    filter_y_rest(des, cc, 4)
    there_x = jnp.where(first_x, 0.0, 1.0).astype(F32)
    there_y = jnp.where(first_y, 0.0, 1.0).astype(F32)

    def density(smoothed, p, e, s):
        solid = smoothed * inv_yz * inv_x(p)
        return jnp.where(e == 1, 0.0, jnp.where(s == 1, 1.0, solid))

    before = density(filter_xz(PAD - 2, 2)[:, 1], PAD - 1, flx[0], flx[1])
    cub[:, PAD - 1] = there_x * (before * before * before)

    def density_body(i, acc):
        p = PAD + 8 * i
        smoothed = filter_xz(p, 8)
        for u in range(8):
            x = 8 * i + u
            rho = density(smoothed[:, u], p + u, flg[0, :, x], flg[1, :, x])
            squared = rho * rho
            held = (flg[0, :, x] + flg[1, :, x]) == 0
            coef[:, x] = jnp.where(held, (3.0 * squared) * inv_yz * inv_x(p + u), 0.0)
            cub[:, p + u] = squared * rho
            acc = acc + rho
        return acc

    occupied = lax.fori_loop(0, n // 8, density_body, jnp.zeros(shape, F32))

    for h in range(2):
        cubs[0, h] = row_pack(cub, h, 0, end, 7)
    cube_moving = [send(cubs, cube.at[:, :, 0:end], 0, 1)]

    def gather_body(i, last):
        for u in range(8):
            now = spread(cub[:, PAD + 8 * i + u])
            ca[:, 8 * i + u] = now + last
            last = now
        return last

    lax.fori_loop(0, n // 8, gather_body, spread(cub[:, PAD - 1]))

    def clear_fields(a, b):
        @pl.when(first_x)
        def _():
            fld[a:b, :, PAD - 1] = jnp.zeros((b - a, 2, 8, 128), F32)
            flo[a:b, :, 0:PAD] = jnp.zeros((b - a, 2, PAD, 128), F32)
            fhi[a:b, :, 0:PAD] = jnp.zeros((b - a, 2, PAD, 128), F32)

        @pl.when(last_x)
        def _():
            fld[a:b, :, end] = jnp.zeros((b - a, 2, 8, 128), F32)
            flo[a:b, :, end : end + PAD] = jnp.zeros((b - a, 2, PAD, 128), F32)
            fhi[a:b, :, end : end + PAD] = jnp.zeros((b - a, 2, PAD, 128), F32)

        @pl.when(first_y)
        def _():
            flo[a:b] = jnp.zeros((b - a, 2, end + PAD, 128), F32)

        @pl.when(last_y)
        def _():
            fhi[a:b] = jnp.zeros((b - a, 2, end + PAD, 128), F32)

    arrived(volt_field_moving)
    clear_fields(0, 1)

    def far_rows(k, edge):
        s, d = z_forward(edge)
        zrow[k, 0] = s
        zrow[k, 1] = d

    def forward_of(field, k):
        def forward(p):
            return yz_forward(
                field[:, p], zrow[k, 0, :, pl.ds(p, 1)], zrow[k, 1, :, pl.ds(p, 1)]
            )

        return forward

    far_rows(0, fhi[0])
    weights = ((0.001, 0.999), (0.05, 0.95), (0.05, 0.95))

    def apply_main(f):
        base, slope = weights[f]

        forward = forward_of(fld.at[f], f)

        def element(a, b, w):
            return x_backward(*weigh(*x_forward(a, b), w))

        a = forward(PAD - 1)
        b = forward(PAD)
        _, behind = element(a, b, there_x * base + slope * cub[:, PAD - 1])

        def body(i, carry):
            a, behind = carry
            for u in range(8):
                x = 8 * i + u
                b = forward(PAD + x + 1)
                front, new = element(a, b, base + slope * cub[:, PAD + x])
                kap[f, :, x] = yz_backward([front[c] + behind[c] for c in range(4)])
                a, behind = b, new
            return tuple(a), tuple(new)

        lax.fori_loop(0, n // 8, body, (tuple(b), tuple(behind)))

    def edge_weight(base, slope):
        where = lax.broadcasted_iota(jnp.int32, (2, end + PAD, 128), 1)
        real = jnp.where(where == PAD - 1, there_x, 1.0) * there_y
        return base * real + (slope * there_y) * cube[0]

    def whole_row(ref, j):
        return jnp.stack([row_pack(ref, h, 0, end + PAD, j) for h in range(2)])

    def rows_x_forward(a):
        return x_forward(a, [planes_after(c) for c in a])

    def apply_edge(f):
        a = rows_forward(flo[f], whole_row(fld.at[f], 0))
        front, behind = x_backward(*weigh(*rows_x_forward(a), edge_weight(*weights[f])))
        m = [front[c] + planes_before(behind[c]) for c in range(4)]
        ns, nd = m[0] + m[2], m[1] + m[3]
        out = (ns - nd) + z_prev(ns + nd)
        for h in range(2):
            row_add(kap.at[f], h, 0, n, 0, out[h, PAD:end])

    apply_main(0)

    arrived(cube_moving)

    @pl.when(first_y)
    def _():
        cube[0] = jnp.zeros((2, end + PAD, 128), F32)

    apply_edge(0)
    edge_cube = cube[0] * there_y
    edge_cube = edge_cube + planes_before(edge_cube)
    edge_cube = edge_cube + z_prev(edge_cube)
    for h in range(2):
        row_add(ca, h, 0, n, 0, edge_cube[h, PAD:end])

    def pivot(x, base, slope):
        cx = jnp.where(gx * n + x == 0, 1.0, 2.0).astype(F32)
        return base * (cx * touch_yz) + slope * ca[:, x]

    loaded(8, 9)

    def volt_body(i, carry):
        for u in range(8):
            x = 8 * i + u
            v = raw[0, :, x]
            moved = 1.8 * (raw[3, :, x] - kap[0, :, x]) / pivot(x, 0.001, 0.999)
            v1[:, PAD + x] = v + jnp.where(flg[2, :, x] == 0, moved, -0.6 * v)
        return carry

    lax.fori_loop(0, n // 8, volt_body, 0)
    for h in range(2):
        v1up[0, h] = row_pack(v1, h, PAD, n, 7)
        v1dn[0, h] = row_pack(v1, h, PAD, n, 0)
    volt_moving = send_up(v1up, v1lo) + send_down(v1dn, v1hi)
    volt_moving += [
        send(v1.at[:, end - 1 : end], v1.at[:, PAD - 1 : PAD], 1, 0),
        send(v1.at[:, PAD : PAD + 1], v1.at[:, end : end + 1], -1, 0),
    ]
    stores = []

    def store(src, dst):
        for h in range(2):
            c = pltpu.make_async_copy(
                src(h), dst.at[:, :, pl.ds(128 * h, 128)], out_sem.at[len(stores)]
            )
            c.start()
            stores.append(c)

    store(lambda h: v1.at[h, PAD:end], v_out)

    arrived(heat_fields_moving)
    clear_fields(1, 3)
    far_rows(1, fhi[1])
    far_rows(2, fhi[2])
    apply_main(2)
    apply_edge(2)
    apply_main(1)
    apply_edge(1)

    def heat_body(i, carry):
        for u in range(8):
            x = 8 * i + u
            free = flg[3, :, x] == 0
            step = 1.8 / pivot(x, 0.05, 0.95)
            d = raw[2, :, x]
            d1[:, PAD + x] = d + jnp.where(free, step * (raw[4, :, x] - kap[2, :, x]), -0.6 * d)
            t = raw[1, :, x]
            t0[:, x] = t - jnp.where(free, step * kap[1, :, x], 0.6 * t)
            tr[:, x] = jnp.where(free, step, 0.0)
        return carry

    lax.fori_loop(0, n // 8, heat_body, 0)
    for h in range(2):
        d1dn[0, h] = row_pack(d1, h, PAD, n, 0)
    dual_moving = send_down(d1dn, d1hi, both=False)
    dual_moving.append(send(d1.at[:, PAD : PAD + 1], d1.at[:, end : end + 1], -1, 0))
    store(lambda h: d1.at[h, PAD:end], d_out)

    arrived(volt_moving)

    def clear_high(field, *edges):
        @pl.when(last_x)
        def _():
            field[:, end] = jnp.zeros((2, 8, 128), F32)
            for edge in edges:
                edge[0, :, end : end + PAD] = jnp.zeros((2, PAD, 128), F32)

        @pl.when(last_y)
        def _():
            edges[0][0] = jnp.zeros((2, end + PAD, 128), F32)

    clear_high(v1, v1hi, v1lo)

    @pl.when(first_x)
    def _():
        v1[:, PAD - 1] = jnp.zeros((2, 8, 128), F32)
        v1hi[0, :, 0:PAD] = jnp.zeros((2, PAD, 128), F32)
        v1lo[0, :, 0:PAD] = jnp.zeros((2, PAD, 128), F32)

    @pl.when(first_y)
    def _():
        v1lo[0] = jnp.zeros((2, end + PAD, 128), F32)


    far_rows(3, v1hi[0])
    volt_forward = forward_of(v1, 3)
    a = volt_forward(PAD - 1)
    b = volt_forward(PAD)
    s, d = x_forward(a, b)
    lead = energy(s, d, s, d) * ((there_x * 0.001 + 0.999 * cub[:, PAD - 1]) / 8.0)

    def joule_body(i, carry):
        a, last, acc = carry
        for u in range(8):
            x = 8 * i + u
            b = volt_forward(PAD + x + 1)
            s, d = x_forward(a, b)
            e = energy(s, d, s, d)
            joule[:, x] = e
            now = spread(e * (0.001 / 8.0 + (0.999 / 8.0) * cub[:, PAD + x]))
            t = t0[:, x] + tr[:, x] * (now + last)
            t1[:, PAD + x] = t
            acc = acc + raw[4, :, x] * t
            a, last = b, now
        return tuple(a), last, acc

    _, _, warm = lax.fori_loop(
        0, n // 8, joule_body, (tuple(b), spread(lead), jnp.zeros(shape, F32))
    )

    def edge_heat():
        s, d = rows_x_forward(rows_forward(v1lo[0], whole_row(v1, 0)))
        e = energy(s, d, s, d) * (edge_weight(0.001, 0.999) * 0.125)
        e = e + planes_before(e)
        return (e + z_prev(e))[:, PAD:end]

    extra = edge_heat()
    warm_rows = jnp.zeros((8, 128), F32)
    for h in range(2):
        more = extra[h] * row_pack(tr, h, 0, n, 0)
        row_add(t1, h, PAD, n, 0, more)
        warm_rows = warm_rows + jnp.sum(
            (more * row_pack(raw.at[4], h, 0, n, 0)).reshape(n // 8, 8, 128), axis=0
        )
        t1dn[0, h] = row_pack(t1, h, PAD, n, 0)
    temp_moving = send_down(t1dn, t1hi, both=False)
    temp_moving.append(send(t1.at[:, PAD : PAD + 1], t1.at[:, end : end + 1], -1, 0))
    store(lambda h: t1.at[h, PAD:end], t_out)

    arrived(dual_moving)
    clear_high(d1, d1hi)
    far_rows(4, d1hi[0])
    dual_forward = forward_of(d1, 4)
    none = jnp.zeros((2, 1, 128), F32)

    def pair_forward(p):
        return tuple(yz_forward(t1[:, p], none, none)), tuple(dual_forward(p))

    def sens_body(i, carry):
        ta, da = carry
        for u in range(8):
            x = 8 * i + u
            tb, db = pair_forward(PAD + x + 1)
            ts, td = x_forward(ta, tb)
            ds, dd = x_forward(da, db)
            mean = (0.999 / 8.0) * (da[0] + db[0])
            value = joule[:, x] * mean - 0.95 * energy(ts, td, ds, dd)
            sen[:, PAD + x] = coef[:, x] * value
            ta, da = tb, db
        return ta, da

    carry = lax.fori_loop(0, n // 8 - 1, sens_body, pair_forward(PAD))
    dual_s, dual_d = rows_x_forward(rows_forward(whole_row(d1, 7), d1hi[0]))
    arrived(temp_moving)
    clear_high(t1, t1hi)
    sens_body(n // 8 - 1, carry)
    behind_s, behind_d = z_forward(t1hi[0])
    temp_s, temp_d = rows_x_forward((behind_s, behind_d, behind_s, behind_d))
    work = 0.95 * energy(temp_s, temp_d, dual_s, dual_d)
    for h in range(2):
        row_add(sen, h, PAD, n, 7, -work[h, PAD:end] * row_pack(coef, h, 0, n, 7))
    tails(sen, sup, sdn)
    sens_moving = send_up(sup, scc.at[0:3]) + send_down(sdn, scc.at[5:8])
    sens_moving += [
        send(sen.at[:, end - 3 : end], sen.at[:, PAD - 3 : PAD], 1, 0),
        send(sen.at[:, PAD : PAD + 3], sen.at[:, end : end + 3], -1, 0),
    ]
    filter_y_own(sen)

    def whole(a):
        return jnp.sum(jnp.sum(a, axis=0, keepdims=True), axis=1, keepdims=True)

    occupied_sum = whole(occupied[0] + occupied[1])
    warm_sum = whole(warm[0] + warm[1] + warm_rows)
    arrived(sens_moving)
    clear(scc, sen, 3, 3)
    filter_y_rest(sen, scc, 3)

    def last_body(i, acc):
        out = filter_xz(PAD + 8 * i, 8)
        fil[:, pl.ds(8 * i, 8)] = out
        return acc + jnp.sum(out * out, axis=1)

    square = lax.fori_loop(0, n // 8, last_body, jnp.zeros(shape, F32))
    store(lambda h: fil.at[h], f_out)

    lane = lax.broadcasted_iota(jnp.int32, (1, 128), 1)
    message = jnp.where(
        lane == 0,
        whole(square[0] + square[1]),
        jnp.where(lane == 1, occupied_sum, warm_sum),
    )

    def exchange(value, slots, me, size, peer, sends, recvs):
        slots[me, 0:1] = value
        for k in farthest_first(size):
            pltpu.make_async_remote_copy(
                src_ref=slots.at[me, pl.ds(0, 1)], dst_ref=slots.at[me, pl.ds(0, 1)],
                send_sem=sends.at[0], recv_sem=recvs.at[0],
                device_id=peer(k), device_id_type=MESH,
            ).start()
        others = slots.at[pl.ds(0, size - 1), pl.ds(0, 1)]
        every = pltpu.make_async_remote_copy(
            src_ref=others, dst_ref=others, send_sem=sends.at[0], recv_sem=recvs.at[0],
            device_id=peer(1), device_id_type=MESH,
        )
        every.wait_recv()
        pending.append((every, 0, 0))
        parts = [slots[k, 0:1] for k in range(size)]
        while len(parts) > 1:
            parts = [a + b for a, b in zip(parts[::2], parts[1::2])]
        return parts[0]

    message = exchange(message, slots1, me1, size1, peer1, r1_send, r1_recv)
    message = exchange(message, slots2, me2, size2, peer2, r2_send, r2_recv)
    sums_out[...] = jnp.broadcast_to(message, (8, 128))
    for c, dx, dy in pending:

        @pl.when(exists(dx, dy))
        def _(c=c):
            c.wait_send()

    for c in stores:
        c.wait()


def finish(
    total, v, t, d, f, sums_ref, v_out, t_out, d_out, f_out, occ_out, mean_out, buf, sem
):
    copies = [
        pltpu.make_async_copy(src, dst, sem.at[i])
        for i, (src, dst) in enumerate(((f, buf), (v, v_out), (t, t_out), (d, d_out)))
    ]
    for c in copies:
        c.start()
    sums = sums_ref[0:1] * (1.0 / total)
    scale = jnp.broadcast_to(1.0 / jnp.sqrt(sums[:, 0:1] + 1e-6), (8, 256))
    occ_out[0] = sums[0, 1]
    mean_out[0] = sums[0, 2]
    copies[0].wait()
    parts = 4
    step = buf.shape[0] // parts
    for i in range(parts):
        part = pl.ds(step * i, step)
        buf[part] = buf[part] * scale
        c = pltpu.make_async_copy(buf.at[part], f_out.at[part], sem.at[4 + i])
        c.start()
        copies.append(c)
    for c in copies[1:]:
        c.wait()


def per_device(nx, ny, *args):
    n = args[0].shape[0]
    assert args[0].shape[1:] == (8, 256) and n % 8 == 0
    field = jax.ShapeDtypeStruct(args[0].shape, F32)
    tile = jax.ShapeDtypeStruct((8, 128), F32)
    wide = n + 2 * PAD

    def vm(*shape, dtype=F32):
        return pltpu.VMEM(shape, dtype)

    planes = vm(2, wide, 8, 128)
    own = vm(2, n, 8, 128)
    edge = vm(1, 2, wide, 128)
    edge_out = vm(1, 2, n, 128)
    scratch = [
        planes, vm(5, 2, n, 8, 128), vm(4, 2, n, 8, 128, dtype=jnp.int32),
        vm(3, 2, wide, 8, 128), vm(2, 2, 8, 128, dtype=jnp.int32),
        vm(5, 2, 2, wide, 128), own,
        vm(8, 2, wide, 128), vm(3, 2, n, 128), vm(3, 2, n, 128),
        vm(3, 2, wide, 128), vm(3, 2, wide, 128), vm(3, 2, n, 128), vm(3, 2, n, 128),
        vm(256, 256, dtype=BF16), planes, planes,
        edge, vm(1, 2, PAD + n, 128), own,
        vm(3, 2, n, 8, 128), planes, edge, edge, edge_out, edge_out,
        planes, edge, edge_out, own, own, planes, edge, edge_out, own,
        planes, vm(8, 2, wide, 128), vm(3, 2, n, 128), vm(3, 2, n, 128), own,
        vm(nx * 2, 8, 128), vm(ny // 2, 8, 128),
        pltpu.SemaphoreType.DMA((20,)), pltpu.SemaphoreType.DMA((8,)),
        pltpu.SemaphoreType.DMA((64,)), pltpu.SemaphoreType.DMA((64,)),
        pltpu.SemaphoreType.DMA((1,)), pltpu.SemaphoreType.DMA((1,)),
        pltpu.SemaphoreType.DMA((1,)), pltpu.SemaphoreType.DMA((1,)),
    ]
    anywhere = pl.BlockSpec(memory_space=pl.ANY)
    hbm = pl.BlockSpec(memory_space=pltpu.HBM)
    vmem = pl.BlockSpec(memory_space=pltpu.VMEM)
    smem = pl.BlockSpec(memory_space=pltpu.SMEM)
    *fields, sums = pl.pallas_call(
        functools.partial(kernel, nx, ny, n),
        out_shape=(field, field, field, field, tile),
        in_specs=[hbm] * 10,
        out_specs=(anywhere,) * 4 + (vmem,),
        scratch_shapes=scratch,
        compiler_params=pltpu.CompilerParams(
            collective_id=0, has_side_effects=True, vmem_limit_bytes=103 * 512 * 1024
        ),
    )(*args)
    one = jax.ShapeDtypeStruct((1,), F32)
    *outs, occupied, mean = pl.pallas_call(
        functools.partial(finish, float(nx * ny * n * 8 * 256)),
        out_shape=(field, field, field, field, one, one),
        in_specs=[anywhere] * 4 + [vmem],
        out_specs=(hbm,) * 4 + (smem, smem),
        scratch_shapes=[vm(n, 8, 256), pltpu.SemaphoreType.DMA((8,))],
        compiler_params=pltpu.CompilerParams(vmem_limit_bytes=8 * 1024 * 1024),
    )(*fields, sums)
    return (*outs, occupied.reshape(()), mean.reshape(()))


def solution(mesh):
    spec = P("gx", "gy", None)
    return jax.shard_map(
        functools.partial(per_device, mesh.shape["gx"], mesh.shape["gy"]),
        mesh=mesh,
        in_specs=(spec,) * 10,
        out_specs=(spec,) * 4 + (P(), P()),
        check_vma=False,
    )
```

```python
import functools

import jax
import jax.numpy as jnp
from jax import lax
from jax.experimental import pallas as pl
from jax.experimental.pallas import tpu as pltpu
from jax.sharding import PartitionSpec as P

MESH = pl.DeviceIdType.MESH
F32 = jnp.float32
BF16 = jnp.bfloat16
PAD = 8
OFFSETS = ((0, 1), (0, -1), (1, 1), (-1, 1), (1, -1), (-1, -1), (1, 0), (-1, 0))


def lanes(shape):
    return lax.broadcasted_iota(jnp.int32, shape, len(shape) - 1)


def z_next(p):
    r = pltpu.roll(p, 127, axis=p.ndim - 1)
    lane = lanes(p.shape[1:])
    low = jnp.where(lane < 127, r[0], r[1])
    high = jnp.where(lane < 127, r[1], 0.0)
    return jnp.stack([low, high])


def z_prev(p):
    r = pltpu.roll(p, 1, axis=p.ndim - 1)
    lane = lanes(p.shape[1:])
    low = jnp.where(lane > 0, r[0], 0.0)
    high = jnp.where(lane > 0, r[1], r[0])
    return jnp.stack([low, high])


def rows_of(shape):
    return lax.broadcasted_iota(jnp.int32, shape, len(shape) - 2)


def y_next(p, row):
    r = pltpu.roll(p, 7, axis=1)
    return jnp.where(rows_of(p.shape) < 7, r, jnp.broadcast_to(row, p.shape))


def y_prev(p):
    r = pltpu.roll(p, 1, axis=1)
    return jnp.where(rows_of(p.shape) > 0, r, 0.0)


def z_forward(p):
    q = z_next(p)
    return p + q, q - p


def yz_forward(p, row_s, row_d):
    s, d = z_forward(p)
    sy, dy = y_next(s, row_s), y_next(d, row_d)
    return s + sy, d + dy, sy - s, dy - d


def rows_forward(near, far):
    (s, d), (sy, dy) = z_forward(near), z_forward(far)
    return s + sy, d + dy, sy - s, dy - d


def planes_after(p):
    return pltpu.roll(p, p.shape[1] - 1, axis=1)


def planes_before(p):
    return pltpu.roll(p, 1, axis=1)


def x_forward(a, b):
    return [a[i] + b[i] for i in range(1, 4)], [b[i] - a[i] for i in range(4)]


def weigh(sums, diffs, w):
    w1, w2, w3 = w * (1.0 / 48.0), w * (1.0 / 24.0), w * (1.0 / 16.0)
    return (
        [w3 * sums[0], w3 * sums[1], w2 * sums[2]],
        [w3 * diffs[0], w2 * diffs[1], w2 * diffs[2], w1 * diffs[3]],
    )


def x_backward(sums, diffs):
    front = [-diffs[0]] + [sums[i] - diffs[i + 1] for i in range(3)]
    behind = [diffs[0]] + [sums[i] + diffs[i + 1] for i in range(3)]
    return front, behind


def yz_backward(n):
    ns = (n[0] - n[2]) + y_prev(n[0] + n[2])
    nd = (n[1] - n[3]) + y_prev(n[1] + n[3])
    return (ns - nd) + z_prev(ns + nd)


def energy(sa, da, sb, db):
    three = da[0] * db[0] + sa[0] * sb[0] + sa[1] * sb[1]
    two = da[1] * db[1] + da[2] * db[2] + sa[2] * sb[2]
    return (1.0 / 16.0) * three + (1.0 / 24.0) * two + (1.0 / 48.0) * (da[3] * db[3])


def spread(p):
    t = p + y_prev(p)
    return t + z_prev(t)


def row_pack(ref, h, first, planes, row):
    every = ref.shape[1]
    flat = ref.reshape(2 * every * 8, 128)
    return flat[pl.ds((h * every + first) * 8 + row, planes, stride=8), :]


def row_add(ref, h, first, planes, row, value):
    every = ref.shape[1]
    flat = ref.reshape(2 * every * 8, 128)
    where = pl.ds((h * every + first) * 8 + row, planes, stride=8)
    flat[where, :] = flat[where, :] + value


def edge_column(edge, h, p):
    every = edge.shape[2]
    flat = edge.reshape(8 * 2 * every, 128)
    return flat[pl.ds(h * every + p, 8, stride=2 * every), :]


def kernel(
    nx, ny, n,
    des_in, v_in, t_in, d_in, q_in, o_in, e_in, s_in, g_in, c_in,
    v_out, t_out, d_out, f_out, sums_out,
    des, raw, flg, fld, flx, zrow, coef,
    cc, cup, cdn, flo, fhi, fup, fdn,
    wz, yf, cub, cube, cubs, ca,
    kap, v1, v1lo, v1hi, v1up, v1dn,
    d1, d1hi, d1dn, t0, tr, t1, t1hi, t1dn, joule,
    sen, scc, sup, sdn, fil, slots1, slots2,
    in_sem, out_sem, send_sem, recv_sem, r1_send, r1_recv, r2_send, r2_recv,
):
    gx, gy = lax.axis_index("gx"), lax.axis_index("gy")
    total = float(nx * n * ny * 8 * 256)
    end = PAD + n
    big, half = min(32, n), min(16, n)
    first_x, last_x = gx == 0, gx == nx - 1
    first_y, last_y = gy == 0, gy == ny - 1

    barrier = pltpu.get_barrier_semaphore()

    def device(dx, dy):
        return (lax.rem(gx + (nx + dx), nx), lax.rem(gy + (ny + dy), ny))

    chip, core = lax.div(gy, 2), lax.rem(gy, 2)
    size1, size2 = nx * 2, ny // 2
    me1, me2 = gx * 2 + core, chip

    def peer1(k):
        other = lax.rem(me1 + k, size1)
        return (lax.div(other, 2), chip * 2 + lax.rem(other, 2))

    def peer2(k):
        return (gx, lax.rem(me2 + k, size2) * 2 + core)

    def farthest_first(size):
        return sorted(range(1, size), key=lambda k: abs(2 * k - size))

    for dx, dy in OFFSETS:
        pl.semaphore_signal(barrier, inc=1, device_id=device(dx, dy), device_id_type=MESH)
    loads = []
    plan = [
        (des_in, lambda h: des.at[h, PAD:end]),
        (v_in, lambda h: raw.at[0, h]),
        (g_in, lambda h: flg.at[2, h]),
        (t_in, lambda h: raw.at[1, h]),
        (d_in, lambda h: raw.at[2, h]),
        (c_in, lambda h: flg.at[3, h]),
        (e_in, lambda h: flg.at[0, h]),
        (s_in, lambda h: flg.at[1, h]),
        (q_in, lambda h: raw.at[3, h]),
        (o_in, lambda h: raw.at[4, h]),
    ]
    for i, (src, dst) in enumerate(plan):
        pair = []
        for h in range(2):
            c = pltpu.make_async_copy(
                src.at[:, :, pl.ds(128 * h, 128)], dst(h), in_sem.at[2 * i + h]
            )
            pair.append(c)
        loads.append(pair)

    def load(*which):
        for i in which:
            for c in loads[i]:
                c.start()

    load(0, 1, 2)

    def loaded(*which):
        for i in which:
            for c in loads[i]:
                c.wait()

    for k in farthest_first(size1):
        pl.semaphore_signal(barrier, inc=1, device_id=peer1(k), device_id_type=MESH)
    for k in farthest_first(size2):
        pl.semaphore_signal(barrier, inc=1, device_id=peer2(k), device_id_type=MESH)

    count = [0]

    def exists(dx, dy):
        x, y = gx + dx, gy + dy
        return (x >= 0) & (x < nx) & (y >= 0) & (y < ny)

    def send(src, dst, dx, dy):
        k = count[0]
        count[0] += 1
        c = pltpu.make_async_remote_copy(
            src_ref=src, dst_ref=dst, send_sem=send_sem.at[k], recv_sem=recv_sem.at[k],
            device_id=device(dx, dy), device_id_type=MESH,
        )

        @pl.when(exists(dx, dy))
        def _():
            c.start()

        return c, dx, dy

    def send_up(src, dst):
        return [
            send(src, dst.at[:, :, PAD:end], 0, 1),
            send(src.at[:, :, n - PAD : n], dst.at[:, :, 0:PAD], 1, 1),
            send(src.at[:, :, 0:PAD], dst.at[:, :, end : end + PAD], -1, 1),
        ]

    def send_down(src, dst, both=True):
        some = [
            send(src, dst.at[:, :, PAD:end], 0, -1),
            send(src.at[:, :, 0:PAD], dst.at[:, :, end : end + PAD], -1, -1),
        ]
        if both:
            some.append(send(src.at[:, :, n - PAD : n], dst.at[:, :, 0:PAD], 1, -1))
        return some

    pending = []

    def arrived(copies):
        for c, dx, dy in copies:

            @pl.when(exists(-dx, -dy))
            def _(c=c):
                c.wait_recv()

        pending.extend(copies)

    def tails_up(ref, up):
        for h in range(2):
            a, b, c = (row_pack(ref, h, PAD, n, j) for j in (5, 6, 7))
            up[0, h] = a + 2.0 * b + 3.0 * c
            up[1, h] = b + 2.0 * c
            up[2, h] = c

    def tails_down(ref, down):
        for h in range(2):
            a, b, c = (row_pack(ref, h, PAD, n, j) for j in (0, 1, 2))
            down[0, h] = a
            down[1, h] = 2.0 * a + b
            down[2, h] = 3.0 * a + 2.0 * b + c

    loaded(0)
    load(3, 4, 5, 6, 7, 8, 9)
    tails_down(des, cdn)
    tails_up(des, cup)
    pl.semaphore_wait(barrier, len(OFFSETS) + size1 - 1 + size2 - 1)
    moving = send_up(cup, cc.at[0:3]) + send_down(cdn, cc.at[5:8])
    moving += [
        send(des.at[:, end - 4 : end], des.at[:, PAD - 4 : PAD], 1, 0),
        send(des.at[:, PAD : PAD + 3], des.at[:, end : end + 3], -1, 0),
    ]

    def mask(f, flag):
        def body(i, carry):
            x = i * 16
            free = flg[flag, :, pl.ds(x, 16)] == 0
            fld[f, :, pl.ds(PAD + x, 16)] = jnp.where(free, raw[f, :, pl.ds(x, 16)], 0.0)
            return carry

        lax.fori_loop(0, n // 16, body, 0)
        for h in range(2):
            fup[f, h] = row_pack(fld.at[f], h, PAD, n, 7)
            fdn[f, h] = row_pack(fld.at[f], h, PAD, n, 0)

    def send_fields(a, b):
        return (
            send_up(fup.at[a:b], flo.at[a:b])
            + send_down(fdn.at[a:b], fhi.at[a:b])
            + [
                send(fld.at[a:b, :, end - 1 : end], fld.at[a:b, :, PAD - 1 : PAD], 1, 0),
                send(fld.at[a:b, :, PAD : PAD + 1], fld.at[a:b, :, end : end + 1], -1, 0),
            ]
        )

    loaded(1, 2)
    mask(0, 2)
    volt_field_moving = send_fields(0, 1)
    loaded(6, 7)
    moving.append(send(flg.at[0:2, :, n - 1], flx, 1, 0))
    zero_rows = jnp.zeros((2, 2, end + PAD, 128), F32)
    cc[3:5] = zero_rows
    scc[3:5] = zero_rows
    wi = lax.broadcasted_iota(jnp.int32, (256, 256), 0)
    wj = lax.broadcasted_iota(jnp.int32, (256, 256), 1)
    wz[...] = jnp.maximum(4 - jnp.abs(wi - wj), 0).astype(F32).astype(BF16)
    loaded(3, 4, 5)
    mask(1, 3)
    mask(2, 3)

    row = lax.broadcasted_iota(jnp.int32, (8, 128), 0)

    def filter_y(ref, p):
        for h in range(2):
            a = ref[h, p]
            out = 4.0 * a
            for k in (1, 2, 3):
                out += jnp.where(row < 8 - k, float(4 - k), 0.0) * pltpu.roll(a, 8 - k, axis=0)
                out += jnp.where(row >= k, float(4 - k), 0.0) * pltpu.roll(a, k, axis=0)
            yf[h, p] = out

    def filter_y_own(ref):
        def body(i, carry):
            for u in range(8):
                filter_y(ref, PAD + 8 * i + u)
            return carry

        lax.fori_loop(0, n // 8, body, 0)

    def filter_y_rest(ref, edge, low):
        outer = list(range(PAD - low, PAD)) + list(range(end, end + 3))
        for p in outer:
            filter_y(ref, p)

        def add(p):
            for h in range(2):
                yf[h, p] += edge_column(edge, h, p)

        def body(i, carry):
            for u in range(8):
                add(PAD + 8 * i + u)
            return carry

        lax.fori_loop(0, n // 8, body, 0)
        for p in outer:
            add(p)

    def filter_xz(p, planes):
        halves = []
        for h in range(2):
            a = yf[h, pl.ds(p - 3, planes + 6)]
            a = a[:-1] + a[1:]
            a = a[:-2] + a[2:]
            a = a[:-1] + a[1:]
            a = a[:-2] + a[2:]
            halves.append(a.reshape(planes * 8, 128))
        a = jnp.concatenate(halves, axis=1)
        high = a.astype(BF16)
        rest = a - high.astype(F32)
        mid = rest.astype(BF16)
        low = (rest - mid.astype(F32)).astype(BF16)
        w = wz[...]
        out = (
            jnp.dot(low, w, preferred_element_type=F32)
            + jnp.dot(mid, w, preferred_element_type=F32)
            + jnp.dot(high, w, preferred_element_type=F32)
        )
        return jnp.stack(
            [out[:, :128].reshape(planes, 8, 128), out[:, 128:].reshape(planes, 8, 128)]
        )

    def inverse_window(i, full):
        w = jnp.where(i == 0, 10, jnp.where(i == 1, 13, jnp.where(i == 2, 15, 16)))
        k = full - 1 - i
        return jnp.where(k == 0, w - 6, jnp.where(k == 1, w - 3, jnp.where(k == 2, w - 1, w)))

    shape = (2, 8, 128)
    yy = gy * 8 + lax.broadcasted_iota(jnp.int32, shape, 1)
    zz = lax.broadcasted_iota(jnp.int32, shape, 0) * 128 + lax.broadcasted_iota(jnp.int32, shape, 2)
    inv_yz = 1.0 / (inverse_window(yy, ny * 8) * inverse_window(zz, 256)).astype(F32)
    touch_yz = (jnp.where(yy == 0, 1, 2) * jnp.where(zz == 0, 1, 2)).astype(F32)

    def inv_x(p):
        i = gx * n + (p - PAD)
        full = nx * n
        r = jnp.where(i == 0, 1 / 10.0, jnp.where(i == 1, 1 / 13.0, jnp.where(i == 2, 1 / 15.0, 1 / 16.0)))
        k = full - 1 - i
        return jnp.where(
            k == 0, 1 / 10.0, jnp.where(k == 1, 1 / 13.0, jnp.where(k == 2, 1 / 15.0, r))
        ).astype(F32)

    filter_y_own(des)
    arrived(moving)
    heat_fields_moving = send_fields(1, 3)

    def clear(edge, field, low, high):
        @pl.when(first_x)
        def _():
            if low:
                field[:, PAD - low : PAD] = jnp.zeros((2, low, 8, 128), F32)
            edge[:, :, 0:PAD] = jnp.zeros((8, 2, PAD, 128), F32)

        @pl.when(last_x)
        def _():
            field[:, end : end + high] = jnp.zeros((2, high, 8, 128), F32)
            edge[:, :, end : end + PAD] = jnp.zeros((8, 2, PAD, 128), F32)

        @pl.when(first_y)
        def _():
            edge[0:3] = jnp.zeros((3, 2, end + PAD, 128), F32)

        @pl.when(last_y)
        def _():
            edge[5:8] = jnp.zeros((3, 2, end + PAD, 128), F32)

    clear(cc, des, 4, 3)
    filter_y_rest(des, cc, 4)
    there_x = jnp.where(first_x, 0.0, 1.0).astype(F32)
    there_y = jnp.where(first_y, 0.0, 1.0).astype(F32)

    def density(smoothed, p, e, s):
        solid = smoothed * inv_yz * inv_x(p)
        return jnp.where(e == 1, 0.0, jnp.where(s == 1, 1.0, solid))

    before = density(filter_xz(PAD - 2, 2)[:, 1], PAD - 1, flx[0], flx[1])
    cub[:, PAD - 1] = there_x * (before * before * before)

    def density_body(i, acc):
        p = PAD + big * i
        smoothed = filter_xz(p, big)
        for u in range(big):
            x = big * i + u
            rho = density(smoothed[:, u], p + u, flg[0, :, x], flg[1, :, x])
            squared = rho * rho
            held = (flg[0, :, x] + flg[1, :, x]) == 0
            coef[:, x] = jnp.where(held, (3.0 * squared) * inv_yz * inv_x(p + u), 0.0)
            cub[:, p + u] = squared * rho
            acc = acc + rho
        return acc

    occupied = lax.fori_loop(0, n // big, density_body, jnp.zeros(shape, F32))

    for h in range(2):
        cubs[0, h] = row_pack(cub, h, 0, end, 7)
    cube_moving = [send(cubs, cube.at[:, :, 0:end], 0, 1)]

    def gather_body(i, last):
        for u in range(8):
            now = spread(cub[:, PAD + 8 * i + u])
            ca[:, 8 * i + u] = now + last
            last = now
        return last

    lax.fori_loop(0, n // 8, gather_body, spread(cub[:, PAD - 1]))

    def clear_fields(a, b):
        @pl.when(first_x)
        def _():
            fld[a:b, :, PAD - 1] = jnp.zeros((b - a, 2, 8, 128), F32)
            flo[a:b, :, 0:PAD] = jnp.zeros((b - a, 2, PAD, 128), F32)
            fhi[a:b, :, 0:PAD] = jnp.zeros((b - a, 2, PAD, 128), F32)

        @pl.when(last_x)
        def _():
            fld[a:b, :, end] = jnp.zeros((b - a, 2, 8, 128), F32)
            flo[a:b, :, end : end + PAD] = jnp.zeros((b - a, 2, PAD, 128), F32)
            fhi[a:b, :, end : end + PAD] = jnp.zeros((b - a, 2, PAD, 128), F32)

        @pl.when(first_y)
        def _():
            flo[a:b] = jnp.zeros((b - a, 2, end + PAD, 128), F32)

        @pl.when(last_y)
        def _():
            fhi[a:b] = jnp.zeros((b - a, 2, end + PAD, 128), F32)

    arrived(volt_field_moving)
    clear_fields(0, 1)

    def far_rows(k, edge):
        s, d = z_forward(edge)
        zrow[k, 0] = s
        zrow[k, 1] = d

    def forward_of(field, k):
        def forward(p):
            return yz_forward(
                field[:, p], zrow[k, 0, :, pl.ds(p, 1)], zrow[k, 1, :, pl.ds(p, 1)]
            )

        return forward

    far_rows(0, fhi[0])
    weights = ((0.001, 0.999), (0.05, 0.95), (0.05, 0.95))

    def apply_main(which, base, slope, step):
        forwards = [forward_of(fld.at[f], f) for f in which]

        def element(a, b, w):
            return x_backward(*weigh(*x_forward(a, b), w))

        start = []
        w = there_x * base + slope * cub[:, PAD - 1]
        for forward in forwards:
            a, b = forward(PAD - 1), forward(PAD)
            start.append((tuple(b), tuple(element(a, b, w)[1])))

        def body(i, carry):
            carry = list(carry)
            for u in range(step):
                x = step * i + u
                w = base + slope * cub[:, PAD + x]
                for k, f in enumerate(which):
                    a, behind = carry[k]
                    b = forwards[k](PAD + x + 1)
                    front, new = element(a, b, w)
                    kap[f, :, x] = yz_backward([front[c] + behind[c] for c in range(4)])
                    carry[k] = tuple(b), tuple(new)
            return tuple(carry)

        lax.fori_loop(0, n // step, body, tuple(start))

    def edge_weight(base, slope):
        where = lax.broadcasted_iota(jnp.int32, (2, end + PAD, 128), 1)
        real = jnp.where(where == PAD - 1, there_x, 1.0) * there_y
        return base * real + (slope * there_y) * cube[0]

    def whole_row(ref, j):
        return jnp.stack([row_pack(ref, h, 0, end + PAD, j) for h in range(2)])

    def rows_x_forward(a):
        return x_forward(a, [planes_after(c) for c in a])

    def apply_edge(f):
        a = rows_forward(flo[f], whole_row(fld.at[f], 0))
        front, behind = x_backward(*weigh(*rows_x_forward(a), edge_weight(*weights[f])))
        m = [front[c] + planes_before(behind[c]) for c in range(4)]
        ns, nd = m[0] + m[2], m[1] + m[3]
        out = (ns - nd) + z_prev(ns + nd)
        for h in range(2):
            row_add(kap.at[f], h, 0, n, 0, out[h, PAD:end])

    apply_main((0,), *weights[0], big)

    arrived(cube_moving)

    @pl.when(first_y)
    def _():
        cube[0] = jnp.zeros((2, end + PAD, 128), F32)

    apply_edge(0)
    edge_cube = cube[0] * there_y
    edge_cube = edge_cube + planes_before(edge_cube)
    edge_cube = edge_cube + z_prev(edge_cube)
    for h in range(2):
        row_add(ca, h, 0, n, 0, edge_cube[h, PAD:end])

    def pivot(x, base, slope):
        cx = jnp.where(gx * n + x == 0, 1.0, 2.0).astype(F32)
        return base * (cx * touch_yz) + slope * ca[:, x]

    loaded(8, 9)

    def volt_body(i, carry):
        for u in range(8):
            x = 8 * i + u
            v = raw[0, :, x]
            moved = 1.8 * (raw[3, :, x] - kap[0, :, x]) / pivot(x, 0.001, 0.999)
            v1[:, PAD + x] = v + jnp.where(flg[2, :, x] == 0, moved, -0.6 * v)
        return carry

    lax.fori_loop(0, n // 8, volt_body, 0)
    for h in range(2):
        v1up[0, h] = row_pack(v1, h, PAD, n, 7)
        v1dn[0, h] = row_pack(v1, h, PAD, n, 0)
    volt_moving = send_up(v1up, v1lo) + send_down(v1dn, v1hi)
    volt_moving += [
        send(v1.at[:, end - 1 : end], v1.at[:, PAD - 1 : PAD], 1, 0),
        send(v1.at[:, PAD : PAD + 1], v1.at[:, end : end + 1], -1, 0),
    ]
    stores = []

    def store(src, dst):
        for h in range(2):
            c = pltpu.make_async_copy(
                src(h), dst.at[:, :, pl.ds(128 * h, 128)], out_sem.at[len(stores)]
            )
            c.start()
            stores.append(c)

    store(lambda h: v1.at[h, PAD:end], v_out)

    arrived(heat_fields_moving)
    clear_fields(1, 3)
    far_rows(1, fhi[1])
    far_rows(2, fhi[2])
    apply_main((1, 2), *weights[1], half)
    apply_edge(1)
    apply_edge(2)

    def heat_body(i, carry):
        for u in range(8):
            x = 8 * i + u
            free = flg[3, :, x] == 0
            step = 1.8 / pivot(x, 0.05, 0.95)
            d = raw[2, :, x]
            d1[:, PAD + x] = d + jnp.where(free, step * (raw[4, :, x] - kap[2, :, x]), -0.6 * d)
            t = raw[1, :, x]
            t0[:, x] = t - jnp.where(free, step * kap[1, :, x], 0.6 * t)
            tr[:, x] = jnp.where(free, step, 0.0)
        return carry

    lax.fori_loop(0, n // 8, heat_body, 0)
    for h in range(2):
        d1dn[0, h] = row_pack(d1, h, PAD, n, 0)
    dual_moving = send_down(d1dn, d1hi, both=False)
    dual_moving.append(send(d1.at[:, PAD : PAD + 1], d1.at[:, end : end + 1], -1, 0))
    store(lambda h: d1.at[h, PAD:end], d_out)

    arrived(volt_moving)

    def clear_high(field, *edges):
        @pl.when(last_x)
        def _():
            field[:, end] = jnp.zeros((2, 8, 128), F32)
            for edge in edges:
                edge[0, :, end : end + PAD] = jnp.zeros((2, PAD, 128), F32)

        @pl.when(last_y)
        def _():
            edges[0][0] = jnp.zeros((2, end + PAD, 128), F32)

    clear_high(v1, v1hi, v1lo)

    @pl.when(first_x)
    def _():
        v1[:, PAD - 1] = jnp.zeros((2, 8, 128), F32)
        v1hi[0, :, 0:PAD] = jnp.zeros((2, PAD, 128), F32)
        v1lo[0, :, 0:PAD] = jnp.zeros((2, PAD, 128), F32)

    @pl.when(first_y)
    def _():
        v1lo[0] = jnp.zeros((2, end + PAD, 128), F32)


    far_rows(3, v1hi[0])
    volt_forward = forward_of(v1, 3)
    def row_energy(near, far):
        s, d = rows_x_forward(rows_forward(near, far))
        return energy(s, d, s, d)

    def row_gather(e):
        e = e + planes_before(e)
        return (e + z_prev(e))[:, PAD:end]

    row0 = whole_row(v1, 0)
    extra = row_gather(row_energy(v1lo[0], row0) * (edge_weight(0.001, 0.999) * 0.125))
    where = lax.broadcasted_iota(jnp.int32, (2, end + PAD, 128), 1)
    own_weight = 0.001 * jnp.where(where == PAD - 1, there_x, 1.0) + 0.999 * whole_row(cub, 0)
    heat0 = extra + row_gather(row_energy(row0, whole_row(v1, 1)) * (own_weight * 0.125))
    for h in range(2):
        t1dn[0, h] = row_pack(t0, h, 0, n, 0) + row_pack(tr, h, 0, n, 0) * heat0[h]
    temp_moving = send_down(t1dn, t1hi, both=False)

    a = volt_forward(PAD - 1)
    b = volt_forward(PAD)
    s, d = x_forward(a, b)
    lead = energy(s, d, s, d) * ((there_x * 0.001 + 0.999 * cub[:, PAD - 1]) / 8.0)

    def joule_body(i, carry):
        a, last, acc = carry
        for u in range(half):
            x = half * i + u
            b = volt_forward(PAD + x + 1)
            s, d = x_forward(a, b)
            e = energy(s, d, s, d)
            joule[:, x] = e
            now = spread(e * (0.001 / 8.0 + (0.999 / 8.0) * cub[:, PAD + x]))
            t = t0[:, x] + tr[:, x] * (now + last)
            t1[:, PAD + x] = t
            acc = acc + raw[4, :, x] * t
            a, last = b, now
        return tuple(a), last, acc

    carry = joule_body(0, (tuple(b), spread(lead), jnp.zeros(shape, F32)))
    for h in range(2):
        t1[h, PAD, 0:1] += extra[h, 0:1] * tr[h, 0, 0:1]
    temp_moving.append(send(t1.at[:, PAD : PAD + 1], t1.at[:, end : end + 1], -1, 0))
    _, _, warm = lax.fori_loop(1, n // half, joule_body, carry)

    warm_rows = jnp.zeros((8, 128), F32)
    for h in range(2):
        more = extra[h] * row_pack(tr, h, 0, n, 0)
        row_add(t1, h, PAD + 1, n - 1, 0, more[1:])
        warm_rows = warm_rows + jnp.sum(
            (more * row_pack(raw.at[4], h, 0, n, 0)).reshape(n // 8, 8, 128), axis=0
        )
    store(lambda h: t1.at[h, PAD:end], t_out)

    arrived(dual_moving)
    clear_high(d1, d1hi)
    far_rows(4, d1hi[0])
    dual_forward = forward_of(d1, 4)
    none = jnp.zeros((2, 1, 128), F32)

    def pair_forward(p):
        return tuple(yz_forward(t1[:, p], none, none)), tuple(dual_forward(p))

    def sens_body(i, carry):
        ta, da = carry
        for u in range(half):
            x = half * i + u
            tb, db = pair_forward(PAD + x + 1)
            ts, td = x_forward(ta, tb)
            ds, dd = x_forward(da, db)
            mean = (0.999 / 8.0) * (da[0] + db[0])
            value = joule[:, x] * mean - 0.95 * energy(ts, td, ds, dd)
            sen[:, PAD + x] = coef[:, x] * value
            ta, da = tb, db
        return ta, da

    carry = lax.fori_loop(0, n // half - 1, sens_body, pair_forward(PAD))
    dual_s, dual_d = rows_x_forward(rows_forward(whole_row(d1, 7), d1hi[0]))
    arrived(temp_moving)
    clear_high(t1, t1hi)
    sens_body(n // half - 1, carry)
    tails_down(sen, sdn)
    sens_moving = send_down(sdn, scc.at[5:8])
    behind_s, behind_d = z_forward(t1hi[0])
    temp_s, temp_d = rows_x_forward((behind_s, behind_d, behind_s, behind_d))
    work = 0.95 * energy(temp_s, temp_d, dual_s, dual_d)
    for h in range(2):
        row_add(sen, h, PAD, n, 7, -work[h, PAD:end] * row_pack(coef, h, 0, n, 7))
    tails_up(sen, sup)
    sens_moving += send_up(sup, scc.at[0:3])
    sens_moving += [
        send(sen.at[:, end - 3 : end], sen.at[:, PAD - 3 : PAD], 1, 0),
        send(sen.at[:, PAD : PAD + 3], sen.at[:, end : end + 3], -1, 0),
    ]
    filter_y_own(sen)

    def whole(a):
        return jnp.sum(jnp.sum(a, axis=0, keepdims=True), axis=1, keepdims=True)

    occupied_sum = whole(occupied[0] + occupied[1])
    warm_sum = whole(warm[0] + warm[1] + warm_rows)
    arrived(sens_moving)
    clear(scc, sen, 3, 3)
    filter_y_rest(sen, scc, 3)

    def last_body(i, acc):
        out = filter_xz(PAD + big * i, big)
        fil[:, pl.ds(big * i, big)] = out
        return acc + jnp.sum(out * out, axis=1)

    square = lax.fori_loop(0, n // big, last_body, jnp.zeros(shape, F32))
    store(lambda h: fil.at[h], f_out)

    lane = lax.broadcasted_iota(jnp.int32, (1, 128), 1)
    message = jnp.where(
        lane == 0,
        whole(square[0] + square[1]),
        jnp.where(lane == 1, occupied_sum, warm_sum),
    )

    def exchange(value, slots, me, size, peer, sends, recvs):
        slots[me, 0:1] = value
        for k in farthest_first(size):
            pltpu.make_async_remote_copy(
                src_ref=slots.at[me, pl.ds(0, 1)], dst_ref=slots.at[me, pl.ds(0, 1)],
                send_sem=sends.at[0], recv_sem=recvs.at[0],
                device_id=peer(k), device_id_type=MESH,
            ).start()
        others = slots.at[pl.ds(0, size - 1), pl.ds(0, 1)]
        every = pltpu.make_async_remote_copy(
            src_ref=others, dst_ref=others, send_sem=sends.at[0], recv_sem=recvs.at[0],
            device_id=peer(1), device_id_type=MESH,
        )
        every.wait_recv()
        pending.append((every, 0, 0))
        parts = [slots[k, 0:1] for k in range(size)]
        while len(parts) > 1:
            parts = [a + b for a, b in zip(parts[::2], parts[1::2])]
        return parts[0]

    message = exchange(message, slots1, me1, size1, peer1, r1_send, r1_recv)
    message = exchange(message, slots2, me2, size2, peer2, r2_send, r2_recv)
    sums_out[...] = jnp.broadcast_to(message, (8, 128))
    for c, dx, dy in pending:

        @pl.when(exists(dx, dy))
        def _(c=c):
            c.wait_send()

    for c in stores:
        c.wait()


def finish(
    total, v, t, d, f, sums_ref, v_out, t_out, d_out, f_out, occ_out, mean_out, buf, sem
):
    copies = [
        pltpu.make_async_copy(src, dst, sem.at[i])
        for i, (src, dst) in enumerate(((f, buf), (v, v_out), (t, t_out), (d, d_out)))
    ]
    for c in copies:
        c.start()
    sums = sums_ref[0:1] * (1.0 / total)
    scale = jnp.broadcast_to(1.0 / jnp.sqrt(sums[:, 0:1] + 1e-6), (8, 256))
    occ_out[0] = sums[0, 1]
    mean_out[0] = sums[0, 2]
    copies[0].wait()
    parts = 4
    step = buf.shape[0] // parts
    for i in range(parts):
        part = pl.ds(step * i, step)
        buf[part] = buf[part] * scale
        c = pltpu.make_async_copy(buf.at[part], f_out.at[part], sem.at[4 + i])
        c.start()
        copies.append(c)
    for c in copies[1:]:
        c.wait()


def per_device(nx, ny, *args):
    n = args[0].shape[0]
    assert args[0].shape[1:] == (8, 256) and n % 8 == 0
    field = jax.ShapeDtypeStruct(args[0].shape, F32)
    tile = jax.ShapeDtypeStruct((8, 128), F32)
    wide = n + 2 * PAD

    def vm(*shape, dtype=F32):
        return pltpu.VMEM(shape, dtype)

    planes = vm(2, wide, 8, 128)
    own = vm(2, n, 8, 128)
    edge = vm(1, 2, wide, 128)
    edge_out = vm(1, 2, n, 128)
    scratch = [
        planes, vm(5, 2, n, 8, 128), vm(4, 2, n, 8, 128, dtype=jnp.int32),
        vm(3, 2, wide, 8, 128), vm(2, 2, 8, 128, dtype=jnp.int32),
        vm(5, 2, 2, wide, 128), own,
        vm(8, 2, wide, 128), vm(3, 2, n, 128), vm(3, 2, n, 128),
        vm(3, 2, wide, 128), vm(3, 2, wide, 128), vm(3, 2, n, 128), vm(3, 2, n, 128),
        vm(256, 256, dtype=BF16), planes, planes,
        edge, vm(1, 2, PAD + n, 128), own,
        vm(3, 2, n, 8, 128), planes, edge, edge, edge_out, edge_out,
        planes, edge, edge_out, own, own, planes, edge, edge_out, own,
        planes, vm(8, 2, wide, 128), vm(3, 2, n, 128), vm(3, 2, n, 128), own,
        vm(nx * 2, 8, 128), vm(ny // 2, 8, 128),
        pltpu.SemaphoreType.DMA((20,)), pltpu.SemaphoreType.DMA((8,)),
        pltpu.SemaphoreType.DMA((64,)), pltpu.SemaphoreType.DMA((64,)),
        pltpu.SemaphoreType.DMA((1,)), pltpu.SemaphoreType.DMA((1,)),
        pltpu.SemaphoreType.DMA((1,)), pltpu.SemaphoreType.DMA((1,)),
    ]
    anywhere = pl.BlockSpec(memory_space=pl.ANY)
    hbm = pl.BlockSpec(memory_space=pltpu.HBM)
    vmem = pl.BlockSpec(memory_space=pltpu.VMEM)
    smem = pl.BlockSpec(memory_space=pltpu.SMEM)
    *fields, sums = pl.pallas_call(
        functools.partial(kernel, nx, ny, n),
        out_shape=(field, field, field, field, tile),
        in_specs=[hbm] * 10,
        out_specs=(anywhere,) * 4 + (vmem,),
        scratch_shapes=scratch,
        compiler_params=pltpu.CompilerParams(
            collective_id=0, has_side_effects=True, vmem_limit_bytes=103 * 512 * 1024
        ),
    )(*args)
    one = jax.ShapeDtypeStruct((1,), F32)
    *outs, occupied, mean = pl.pallas_call(
        functools.partial(finish, float(nx * ny * n * 8 * 256)),
        out_shape=(field, field, field, field, one, one),
        in_specs=[anywhere] * 4 + [vmem],
        out_specs=(hbm,) * 4 + (smem, smem),
        scratch_shapes=[vm(n, 8, 256), pltpu.SemaphoreType.DMA((8,))],
        compiler_params=pltpu.CompilerParams(vmem_limit_bytes=8 * 1024 * 1024),
    )(*fields, sums)
    return (*outs, occupied.reshape(()), mean.reshape(()))


def solution(mesh):
    spec = P("gx", "gy", None)
    return jax.shard_map(
        functools.partial(per_device, mesh.shape["gx"], mesh.shape["gy"]),
        mesh=mesh,
        in_specs=(spec,) * 10,
        out_specs=(spec,) * 4 + (P(), P()),
        check_vma=False,
    )
```

```python
import functools

import jax
import jax.numpy as jnp
from jax import lax
from jax.experimental import pallas as pl
from jax.experimental.pallas import tpu as pltpu
from jax.sharding import PartitionSpec as P

MESH = pl.DeviceIdType.MESH
F32 = jnp.float32
BF16 = jnp.bfloat16
PAD = 8
OFFSETS = ((0, 1), (0, -1), (1, 1), (-1, 1), (1, -1), (-1, -1), (1, 0), (-1, 0))


def lanes(shape):
    return lax.broadcasted_iota(jnp.int32, shape, len(shape) - 1)


def z_next(p):
    r = pltpu.roll(p, 127, axis=p.ndim - 1)
    lane = lanes(p.shape[1:])
    low = jnp.where(lane < 127, r[0], r[1])
    high = jnp.where(lane < 127, r[1], 0.0)
    return jnp.stack([low, high])


def z_prev(p):
    r = pltpu.roll(p, 1, axis=p.ndim - 1)
    lane = lanes(p.shape[1:])
    low = jnp.where(lane > 0, r[0], 0.0)
    high = jnp.where(lane > 0, r[1], r[0])
    return jnp.stack([low, high])


def rows_of(shape):
    return lax.broadcasted_iota(jnp.int32, shape, len(shape) - 2)


def y_next(p, row):
    r = pltpu.roll(p, 7, axis=1)
    return jnp.where(rows_of(p.shape) < 7, r, jnp.broadcast_to(row, p.shape))


def y_prev(p):
    r = pltpu.roll(p, 1, axis=1)
    return jnp.where(rows_of(p.shape) > 0, r, 0.0)


def z_forward(p):
    q = z_next(p)
    return p + q, q - p


def yz_forward(p, row_s, row_d):
    s, d = z_forward(p)
    sy, dy = y_next(s, row_s), y_next(d, row_d)
    return s + sy, d + dy, sy - s, dy - d


def rows_forward(near, far):
    (s, d), (sy, dy) = z_forward(near), z_forward(far)
    return s + sy, d + dy, sy - s, dy - d


def planes_after(p):
    return pltpu.roll(p, p.shape[1] - 1, axis=1)


def planes_before(p):
    return pltpu.roll(p, 1, axis=1)


def x_forward(a, b):
    return [a[i] + b[i] for i in range(1, 4)], [b[i] - a[i] for i in range(4)]


def weigh(sums, diffs, w):
    w1, w2, w3 = w * (1.0 / 48.0), w * (1.0 / 24.0), w * (1.0 / 16.0)
    return (
        [w3 * sums[0], w3 * sums[1], w2 * sums[2]],
        [w3 * diffs[0], w2 * diffs[1], w2 * diffs[2], w1 * diffs[3]],
    )


def x_backward(sums, diffs):
    front = [-diffs[0]] + [sums[i] - diffs[i + 1] for i in range(3)]
    behind = [diffs[0]] + [sums[i] + diffs[i + 1] for i in range(3)]
    return front, behind


def yz_backward(n):
    ns = (n[0] - n[2]) + y_prev(n[0] + n[2])
    nd = (n[1] - n[3]) + y_prev(n[1] + n[3])
    return (ns - nd) + z_prev(ns + nd)


def energy(sa, da, sb, db):
    three = da[0] * db[0] + sa[0] * sb[0] + sa[1] * sb[1]
    two = da[1] * db[1] + da[2] * db[2] + sa[2] * sb[2]
    return (1.0 / 16.0) * three + (1.0 / 24.0) * two + (1.0 / 48.0) * (da[3] * db[3])


def spread(p):
    t = p + y_prev(p)
    return t + z_prev(t)


def row_pack(ref, h, first, planes, row):
    every = ref.shape[1]
    flat = ref.reshape(2 * every * 8, 128)
    return flat[pl.ds((h * every + first) * 8 + row, planes, stride=8), :]


def row_add(ref, h, first, planes, row, value):
    every = ref.shape[1]
    flat = ref.reshape(2 * every * 8, 128)
    where = pl.ds((h * every + first) * 8 + row, planes, stride=8)
    flat[where, :] = flat[where, :] + value


def edge_column(edge, h, p):
    every = edge.shape[2]
    flat = edge.reshape(8 * 2 * every, 128)
    return flat[pl.ds(h * every + p, 8, stride=2 * every), :]


def kernel(
    nx, ny, n,
    des_in, v_in, t_in, d_in, q_in, o_in, e_in, s_in, g_in, c_in,
    v_out, t_out, d_out, f_out, sums_out,
    des, raw, flg, fld, flx, zrow, coef,
    cc, cup, cdn, flo, fhi, fup, fdn,
    wz, yf, cub, cube, cubs, ca,
    kap, v1, v1lo, v1hi, v1up, v1dn,
    d1, d1hi, d1dn, t0, tr, t1, t1hi, t1dn, joule,
    sen, scc, sup, sdn, fil, slots1, slots2,
    in_sem, out_sem, send_sem, recv_sem, r1_send, r1_recv, r2_send, r2_recv,
):
    gx, gy = lax.axis_index("gx"), lax.axis_index("gy")
    total = float(nx * n * ny * 8 * 256)
    end = PAD + n
    big, half = min(32, n), min(16, n)
    first_x, last_x = gx == 0, gx == nx - 1
    first_y, last_y = gy == 0, gy == ny - 1

    barrier = pltpu.get_barrier_semaphore()

    def device(dx, dy):
        return (lax.rem(gx + (nx + dx), nx), lax.rem(gy + (ny + dy), ny))

    chip, core = lax.div(gy, 2), lax.rem(gy, 2)
    size1, size2 = nx * 2, ny // 2
    me1, me2 = gx * 2 + core, chip

    def peer1(k):
        other = lax.rem(me1 + k, size1)
        return (lax.div(other, 2), chip * 2 + lax.rem(other, 2))

    def peer2(k):
        return (gx, lax.rem(me2 + k, size2) * 2 + core)

    def farthest_first(size):
        return sorted(range(1, size), key=lambda k: abs(2 * k - size))

    loads = []
    plan = [
        (des_in, lambda h: des.at[h, PAD:end]),
        (v_in, lambda h: raw.at[0, h]),
        (g_in, lambda h: flg.at[2, h]),
        (t_in, lambda h: raw.at[1, h]),
        (d_in, lambda h: raw.at[2, h]),
        (c_in, lambda h: flg.at[3, h]),
        (e_in, lambda h: flg.at[0, h]),
        (s_in, lambda h: flg.at[1, h]),
        (q_in, lambda h: raw.at[3, h]),
        (o_in, lambda h: raw.at[4, h]),
    ]
    for i, (src, dst) in enumerate(plan):
        pair = []
        for h in range(2):
            c = pltpu.make_async_copy(
                src.at[:, :, pl.ds(128 * h, 128)], dst(h), in_sem.at[2 * i + h]
            )
            pair.append(c)
        loads.append(pair)

    def load(*which):
        for i in which:
            for c in loads[i]:
                c.start()

    load(0)

    def loaded(*which):
        for i in which:
            for c in loads[i]:
                c.wait()

    for k in range(max(size1, size2) - 1):
        for size, peer in ((size2, peer2), (size1, peer1)):
            if k < size - 1:
                pl.semaphore_signal(
                    barrier, inc=1, device_id=peer(farthest_first(size)[k]), device_id_type=MESH
                )
    for dx, dy in OFFSETS:
        pl.semaphore_signal(barrier, inc=1, device_id=device(dx, dy), device_id_type=MESH)
    load(1, 2)

    count = [0]

    def exists(dx, dy):
        x, y = gx + dx, gy + dy
        return (x >= 0) & (x < nx) & (y >= 0) & (y < ny)

    def send(src, dst, dx, dy):
        k = count[0]
        count[0] += 1
        c = pltpu.make_async_remote_copy(
            src_ref=src, dst_ref=dst, send_sem=send_sem.at[k], recv_sem=recv_sem.at[k],
            device_id=device(dx, dy), device_id_type=MESH,
        )

        @pl.when(exists(dx, dy))
        def _():
            c.start()

        return c, dx, dy

    def send_up(src, dst):
        return [
            send(src, dst.at[:, :, PAD:end], 0, 1),
            send(src.at[:, :, n - PAD : n], dst.at[:, :, 0:PAD], 1, 1),
            send(src.at[:, :, 0:PAD], dst.at[:, :, end : end + PAD], -1, 1),
        ]

    def send_down(src, dst, both=True):
        some = [
            send(src, dst.at[:, :, PAD:end], 0, -1),
            send(src.at[:, :, 0:PAD], dst.at[:, :, end : end + PAD], -1, -1),
        ]
        if both:
            some.append(send(src.at[:, :, n - PAD : n], dst.at[:, :, 0:PAD], 1, -1))
        return some

    pending = []

    def arrived(copies):
        for c, dx, dy in copies:

            @pl.when(exists(-dx, -dy))
            def _(c=c):
                c.wait_recv()

        pending.extend(copies)

    def tails_up(ref, up):
        for h in range(2):
            a, b, c = (row_pack(ref, h, PAD, n, j) for j in (5, 6, 7))
            up[0, h] = a + 2.0 * b + 3.0 * c
            up[1, h] = b + 2.0 * c
            up[2, h] = c

    def tails_down(ref, down):
        for h in range(2):
            a, b, c = (row_pack(ref, h, PAD, n, j) for j in (0, 1, 2))
            down[0, h] = a
            down[1, h] = 2.0 * a + b
            down[2, h] = 3.0 * a + 2.0 * b + c

    loaded(0)
    load(3, 4, 5, 6, 7, 8, 9)
    tails_down(des, cdn)
    tails_up(des, cup)
    pl.semaphore_wait(barrier, len(OFFSETS) + size1 - 1 + size2 - 1)
    moving = send_up(cup, cc.at[0:3]) + send_down(cdn, cc.at[5:8])
    moving += [
        send(des.at[:, end - 4 : end], des.at[:, PAD - 4 : PAD], 1, 0),
        send(des.at[:, PAD : PAD + 3], des.at[:, end : end + 3], -1, 0),
    ]

    def mask(f, flag):
        def body(i, carry):
            x = i * 16
            free = flg[flag, :, pl.ds(x, 16)] == 0
            fld[f, :, pl.ds(PAD + x, 16)] = jnp.where(free, raw[f, :, pl.ds(x, 16)], 0.0)
            return carry

        lax.fori_loop(0, n // 16, body, 0)
        for h in range(2):
            fup[f, h] = row_pack(fld.at[f], h, PAD, n, 7)
            fdn[f, h] = row_pack(fld.at[f], h, PAD, n, 0)

    def send_fields(a, b):
        return (
            send_up(fup.at[a:b], flo.at[a:b])
            + send_down(fdn.at[a:b], fhi.at[a:b])
            + [
                send(fld.at[a:b, :, end - 1 : end], fld.at[a:b, :, PAD - 1 : PAD], 1, 0),
                send(fld.at[a:b, :, PAD : PAD + 1], fld.at[a:b, :, end : end + 1], -1, 0),
            ]
        )

    loaded(1, 2)
    mask(0, 2)
    volt_field_moving = send_fields(0, 1)
    loaded(6, 7)
    moving.append(send(flg.at[0:2, :, n - 1], flx, 1, 0))
    zero_rows = jnp.zeros((2, 2, end + PAD, 128), F32)
    cc[3:5] = zero_rows
    scc[3:5] = zero_rows
    wi = lax.broadcasted_iota(jnp.int32, (256, 256), 0)
    wj = lax.broadcasted_iota(jnp.int32, (256, 256), 1)
    wz[...] = jnp.maximum(4 - jnp.abs(wi - wj), 0).astype(F32).astype(BF16)
    loaded(3, 4, 5)
    mask(1, 3)
    mask(2, 3)

    row = lax.broadcasted_iota(jnp.int32, (8, 128), 0)

    def filter_y(ref, p):
        for h in range(2):
            a = ref[h, p]
            out = 4.0 * a
            for k in (1, 2, 3):
                out += jnp.where(row < 8 - k, float(4 - k), 0.0) * pltpu.roll(a, 8 - k, axis=0)
                out += jnp.where(row >= k, float(4 - k), 0.0) * pltpu.roll(a, k, axis=0)
            yf[h, p] = out

    def filter_y_own(ref):
        def body(i, carry):
            for u in range(8):
                filter_y(ref, PAD + 8 * i + u)
            return carry

        lax.fori_loop(0, n // 8, body, 0)

    def filter_y_rest(ref, edge, low):
        outer = list(range(PAD - low, PAD)) + list(range(end, end + 3))
        for p in outer:
            filter_y(ref, p)

        def add(p):
            for h in range(2):
                yf[h, p] += edge_column(edge, h, p)

        def body(i, carry):
            for u in range(8):
                add(PAD + 8 * i + u)
            return carry

        lax.fori_loop(0, n // 8, body, 0)
        for p in outer:
            add(p)

    def filter_xz(p, planes):
        halves = []
        for h in range(2):
            a = yf[h, pl.ds(p - 3, planes + 6)]
            a = a[:-1] + a[1:]
            a = a[:-2] + a[2:]
            a = a[:-1] + a[1:]
            a = a[:-2] + a[2:]
            halves.append(a.reshape(planes * 8, 128))
        a = jnp.concatenate(halves, axis=1)
        high = a.astype(BF16)
        rest = a - high.astype(F32)
        mid = rest.astype(BF16)
        low = (rest - mid.astype(F32)).astype(BF16)
        w = wz[...]
        out = (
            jnp.dot(low, w, preferred_element_type=F32)
            + jnp.dot(mid, w, preferred_element_type=F32)
            + jnp.dot(high, w, preferred_element_type=F32)
        )
        return jnp.stack(
            [out[:, :128].reshape(planes, 8, 128), out[:, 128:].reshape(planes, 8, 128)]
        )

    def inverse_window(i, full):
        w = jnp.where(i == 0, 10, jnp.where(i == 1, 13, jnp.where(i == 2, 15, 16)))
        k = full - 1 - i
        return jnp.where(k == 0, w - 6, jnp.where(k == 1, w - 3, jnp.where(k == 2, w - 1, w)))

    shape = (2, 8, 128)
    yy = gy * 8 + lax.broadcasted_iota(jnp.int32, shape, 1)
    zz = lax.broadcasted_iota(jnp.int32, shape, 0) * 128 + lax.broadcasted_iota(jnp.int32, shape, 2)
    inv_yz = 1.0 / (inverse_window(yy, ny * 8) * inverse_window(zz, 256)).astype(F32)
    touch_yz = (jnp.where(yy == 0, 1, 2) * jnp.where(zz == 0, 1, 2)).astype(F32)

    def inv_x(p):
        i = gx * n + (p - PAD)
        full = nx * n
        r = jnp.where(i == 0, 1 / 10.0, jnp.where(i == 1, 1 / 13.0, jnp.where(i == 2, 1 / 15.0, 1 / 16.0)))
        k = full - 1 - i
        return jnp.where(
            k == 0, 1 / 10.0, jnp.where(k == 1, 1 / 13.0, jnp.where(k == 2, 1 / 15.0, r))
        ).astype(F32)

    filter_y_own(des)
    arrived(moving)
    heat_fields_moving = send_fields(1, 3)

    def clear(edge, field, low, high):
        @pl.when(first_x)
        def _():
            if low:
                field[:, PAD - low : PAD] = jnp.zeros((2, low, 8, 128), F32)
            edge[:, :, 0:PAD] = jnp.zeros((8, 2, PAD, 128), F32)

        @pl.when(last_x)
        def _():
            field[:, end : end + high] = jnp.zeros((2, high, 8, 128), F32)
            edge[:, :, end : end + PAD] = jnp.zeros((8, 2, PAD, 128), F32)

        @pl.when(first_y)
        def _():
            edge[0:3] = jnp.zeros((3, 2, end + PAD, 128), F32)

        @pl.when(last_y)
        def _():
            edge[5:8] = jnp.zeros((3, 2, end + PAD, 128), F32)

    clear(cc, des, 4, 3)
    filter_y_rest(des, cc, 4)
    there_x = jnp.where(first_x, 0.0, 1.0).astype(F32)
    there_y = jnp.where(first_y, 0.0, 1.0).astype(F32)

    def density(smoothed, p, e, s):
        solid = smoothed * inv_yz * inv_x(p)
        return jnp.where(e == 1, 0.0, jnp.where(s == 1, 1.0, solid))

    before = density(filter_xz(PAD - 2, 2)[:, 1], PAD - 1, flx[0], flx[1])
    cub[:, PAD - 1] = there_x * (before * before * before)

    def density_body(i, acc):
        p = PAD + big * i
        smoothed = filter_xz(p, big)
        for u in range(big):
            x = big * i + u
            rho = density(smoothed[:, u], p + u, flg[0, :, x], flg[1, :, x])
            squared = rho * rho
            held = (flg[0, :, x] + flg[1, :, x]) == 0
            coef[:, x] = jnp.where(held, (3.0 * squared) * inv_yz * inv_x(p + u), 0.0)
            cub[:, p + u] = squared * rho
            acc = acc + rho
        return acc

    occupied = lax.fori_loop(0, n // big, density_body, jnp.zeros(shape, F32))

    for h in range(2):
        cubs[0, h] = row_pack(cub, h, 0, end, 7)
    cube_moving = [send(cubs, cube.at[:, :, 0:end], 0, 1)]

    def gather_body(i, last):
        for u in range(8):
            now = spread(cub[:, PAD + 8 * i + u])
            ca[:, 8 * i + u] = now + last
            last = now
        return last

    lax.fori_loop(0, n // 8, gather_body, spread(cub[:, PAD - 1]))

    def clear_fields(a, b):
        @pl.when(first_x)
        def _():
            fld[a:b, :, PAD - 1] = jnp.zeros((b - a, 2, 8, 128), F32)
            flo[a:b, :, 0:PAD] = jnp.zeros((b - a, 2, PAD, 128), F32)
            fhi[a:b, :, 0:PAD] = jnp.zeros((b - a, 2, PAD, 128), F32)

        @pl.when(last_x)
        def _():
            fld[a:b, :, end] = jnp.zeros((b - a, 2, 8, 128), F32)
            flo[a:b, :, end : end + PAD] = jnp.zeros((b - a, 2, PAD, 128), F32)
            fhi[a:b, :, end : end + PAD] = jnp.zeros((b - a, 2, PAD, 128), F32)

        @pl.when(first_y)
        def _():
            flo[a:b] = jnp.zeros((b - a, 2, end + PAD, 128), F32)

        @pl.when(last_y)
        def _():
            fhi[a:b] = jnp.zeros((b - a, 2, end + PAD, 128), F32)

    arrived(volt_field_moving)
    clear_fields(0, 1)

    def far_rows(k, edge):
        s, d = z_forward(edge)
        zrow[k, 0] = s
        zrow[k, 1] = d

    def forward_of(field, k):
        def forward(p):
            return yz_forward(
                field[:, p], zrow[k, 0, :, pl.ds(p, 1)], zrow[k, 1, :, pl.ds(p, 1)]
            )

        return forward

    far_rows(0, fhi[0])
    weights = ((0.001, 0.999), (0.05, 0.95), (0.05, 0.95))

    def apply_main(which, base, slope, step):
        forwards = [forward_of(fld.at[f], f) for f in which]

        def element(a, b, w):
            return x_backward(*weigh(*x_forward(a, b), w))

        start = []
        w = there_x * base + slope * cub[:, PAD - 1]
        for forward in forwards:
            a, b = forward(PAD - 1), forward(PAD)
            start.append((tuple(b), tuple(element(a, b, w)[1])))

        def body(i, carry):
            carry = list(carry)
            for u in range(step):
                x = step * i + u
                w = base + slope * cub[:, PAD + x]
                for k, f in enumerate(which):
                    a, behind = carry[k]
                    b = forwards[k](PAD + x + 1)
                    front, new = element(a, b, w)
                    kap[f, :, x] = yz_backward([front[c] + behind[c] for c in range(4)])
                    carry[k] = tuple(b), tuple(new)
            return tuple(carry)

        lax.fori_loop(0, n // step, body, tuple(start))

    def edge_weight(base, slope):
        where = lax.broadcasted_iota(jnp.int32, (2, end + PAD, 128), 1)
        real = jnp.where(where == PAD - 1, there_x, 1.0) * there_y
        return base * real + (slope * there_y) * cube[0]

    def whole_row(ref, j):
        return jnp.stack([row_pack(ref, h, 0, end + PAD, j) for h in range(2)])

    def rows_x_forward(a):
        return x_forward(a, [planes_after(c) for c in a])

    def apply_edge(f):
        a = rows_forward(flo[f], whole_row(fld.at[f], 0))
        front, behind = x_backward(*weigh(*rows_x_forward(a), edge_weight(*weights[f])))
        m = [front[c] + planes_before(behind[c]) for c in range(4)]
        ns, nd = m[0] + m[2], m[1] + m[3]
        out = (ns - nd) + z_prev(ns + nd)
        for h in range(2):
            row_add(kap.at[f], h, 0, n, 0, out[h, PAD:end])

    apply_main((0,), *weights[0], big)

    arrived(cube_moving)

    @pl.when(first_y)
    def _():
        cube[0] = jnp.zeros((2, end + PAD, 128), F32)

    apply_edge(0)
    edge_cube = cube[0] * there_y
    edge_cube = edge_cube + planes_before(edge_cube)
    edge_cube = edge_cube + z_prev(edge_cube)
    for h in range(2):
        row_add(ca, h, 0, n, 0, edge_cube[h, PAD:end])

    def pivot(x, base, slope):
        cx = jnp.where(gx * n + x == 0, 1.0, 2.0).astype(F32)
        return base * (cx * touch_yz) + slope * ca[:, x]

    loaded(8, 9)

    def volt_body(i, carry):
        for u in range(8):
            x = 8 * i + u
            v = raw[0, :, x]
            moved = 1.8 * (raw[3, :, x] - kap[0, :, x]) / pivot(x, 0.001, 0.999)
            v1[:, PAD + x] = v + jnp.where(flg[2, :, x] == 0, moved, -0.6 * v)
        return carry

    lax.fori_loop(0, n // 8, volt_body, 0)
    for h in range(2):
        v1up[0, h] = row_pack(v1, h, PAD, n, 7)
        v1dn[0, h] = row_pack(v1, h, PAD, n, 0)
    volt_moving = send_up(v1up, v1lo) + send_down(v1dn, v1hi)
    volt_moving += [
        send(v1.at[:, end - 1 : end], v1.at[:, PAD - 1 : PAD], 1, 0),
        send(v1.at[:, PAD : PAD + 1], v1.at[:, end : end + 1], -1, 0),
    ]
    stores = []

    def store(src, dst):
        for h in range(2):
            c = pltpu.make_async_copy(
                src(h), dst.at[:, :, pl.ds(128 * h, 128)], out_sem.at[len(stores)]
            )
            c.start()
            stores.append(c)

    store(lambda h: v1.at[h, PAD:end], v_out)

    arrived(heat_fields_moving)
    clear_fields(1, 3)
    far_rows(1, fhi[1])
    far_rows(2, fhi[2])
    apply_main((1, 2), *weights[1], half)
    apply_edge(1)
    apply_edge(2)

    def heat_body(i, carry):
        for u in range(8):
            x = 8 * i + u
            free = flg[3, :, x] == 0
            step = 1.8 / pivot(x, 0.05, 0.95)
            d = raw[2, :, x]
            d1[:, PAD + x] = d + jnp.where(free, step * (raw[4, :, x] - kap[2, :, x]), -0.6 * d)
            t = raw[1, :, x]
            t0[:, x] = t - jnp.where(free, step * kap[1, :, x], 0.6 * t)
            tr[:, x] = jnp.where(free, step, 0.0)
        return carry

    lax.fori_loop(0, n // 8, heat_body, 0)
    for h in range(2):
        d1dn[0, h] = row_pack(d1, h, PAD, n, 0)
    dual_moving = send_down(d1dn, d1hi, both=False)
    dual_moving.append(send(d1.at[:, PAD : PAD + 1], d1.at[:, end : end + 1], -1, 0))
    store(lambda h: d1.at[h, PAD:end], d_out)

    arrived(volt_moving)

    def clear_high(field, *edges):
        @pl.when(last_x)
        def _():
            field[:, end] = jnp.zeros((2, 8, 128), F32)
            for edge in edges:
                edge[0, :, end : end + PAD] = jnp.zeros((2, PAD, 128), F32)

        @pl.when(last_y)
        def _():
            edges[0][0] = jnp.zeros((2, end + PAD, 128), F32)

    clear_high(v1, v1hi, v1lo)

    @pl.when(first_x)
    def _():
        v1[:, PAD - 1] = jnp.zeros((2, 8, 128), F32)
        v1hi[0, :, 0:PAD] = jnp.zeros((2, PAD, 128), F32)
        v1lo[0, :, 0:PAD] = jnp.zeros((2, PAD, 128), F32)

    @pl.when(first_y)
    def _():
        v1lo[0] = jnp.zeros((2, end + PAD, 128), F32)


    far_rows(3, v1hi[0])
    volt_forward = forward_of(v1, 3)
    def row_energy(near, far):
        s, d = rows_x_forward(rows_forward(near, far))
        return energy(s, d, s, d)

    def row_gather(e):
        e = e + planes_before(e)
        return (e + z_prev(e))[:, PAD:end]

    row0 = whole_row(v1, 0)
    extra = row_gather(row_energy(v1lo[0], row0) * (edge_weight(0.001, 0.999) * 0.125))
    where = lax.broadcasted_iota(jnp.int32, (2, end + PAD, 128), 1)
    own_weight = 0.001 * jnp.where(where == PAD - 1, there_x, 1.0) + 0.999 * whole_row(cub, 0)
    heat0 = extra + row_gather(row_energy(row0, whole_row(v1, 1)) * (own_weight * 0.125))
    for h in range(2):
        t1dn[0, h] = row_pack(t0, h, 0, n, 0) + row_pack(tr, h, 0, n, 0) * heat0[h]
    temp_moving = send_down(t1dn, t1hi, both=False)

    a = volt_forward(PAD - 1)
    b = volt_forward(PAD)
    s, d = x_forward(a, b)
    lead = energy(s, d, s, d) * ((there_x * 0.001 + 0.999 * cub[:, PAD - 1]) / 8.0)

    def joule_body(i, carry):
        a, last, acc = carry
        for u in range(half):
            x = half * i + u
            b = volt_forward(PAD + x + 1)
            s, d = x_forward(a, b)
            e = energy(s, d, s, d)
            joule[:, x] = e
            now = spread(e * (0.001 / 8.0 + (0.999 / 8.0) * cub[:, PAD + x]))
            t = t0[:, x] + tr[:, x] * (now + last)
            t1[:, PAD + x] = t
            acc = acc + raw[4, :, x] * t
            a, last = b, now
        return tuple(a), last, acc

    carry = joule_body(0, (tuple(b), spread(lead), jnp.zeros(shape, F32)))
    for h in range(2):
        t1[h, PAD, 0:1] += extra[h, 0:1] * tr[h, 0, 0:1]
    temp_moving.append(send(t1.at[:, PAD : PAD + 1], t1.at[:, end : end + 1], -1, 0))
    _, _, warm = lax.fori_loop(1, n // half, joule_body, carry)

    warm_rows = jnp.zeros((8, 128), F32)
    for h in range(2):
        more = extra[h] * row_pack(tr, h, 0, n, 0)
        row_add(t1, h, PAD + 1, n - 1, 0, more[1:])
        warm_rows = warm_rows + jnp.sum(
            (more * row_pack(raw.at[4], h, 0, n, 0)).reshape(n // 8, 8, 128), axis=0
        )
    store(lambda h: t1.at[h, PAD:end], t_out)

    arrived(dual_moving)
    clear_high(d1, d1hi)
    far_rows(4, d1hi[0])
    dual_forward = forward_of(d1, 4)
    none = jnp.zeros((2, 1, 128), F32)

    def pair_forward(p):
        return tuple(yz_forward(t1[:, p], none, none)), tuple(dual_forward(p))

    def sens_body(i, carry):
        ta, da = carry
        for u in range(half):
            x = half * i + u
            tb, db = pair_forward(PAD + x + 1)
            ts, td = x_forward(ta, tb)
            ds, dd = x_forward(da, db)
            mean = (0.999 / 8.0) * (da[0] + db[0])
            value = joule[:, x] * mean - 0.95 * energy(ts, td, ds, dd)
            sen[:, PAD + x] = coef[:, x] * value
            ta, da = tb, db
        return ta, da

    carry = lax.fori_loop(0, n // half - 1, sens_body, pair_forward(PAD))
    dual_s, dual_d = rows_x_forward(rows_forward(whole_row(d1, 7), d1hi[0]))
    arrived(temp_moving)
    clear_high(t1, t1hi)
    sens_body(n // half - 1, carry)
    tails_down(sen, sdn)
    sens_moving = send_down(sdn, scc.at[5:8])
    behind_s, behind_d = z_forward(t1hi[0])
    temp_s, temp_d = rows_x_forward((behind_s, behind_d, behind_s, behind_d))
    work = 0.95 * energy(temp_s, temp_d, dual_s, dual_d)
    for h in range(2):
        row_add(sen, h, PAD, n, 7, -work[h, PAD:end] * row_pack(coef, h, 0, n, 7))
    tails_up(sen, sup)
    sens_moving += send_up(sup, scc.at[0:3])
    sens_moving += [
        send(sen.at[:, end - 3 : end], sen.at[:, PAD - 3 : PAD], 1, 0),
        send(sen.at[:, PAD : PAD + 3], sen.at[:, end : end + 3], -1, 0),
    ]
    filter_y_own(sen)

    def whole(a):
        return jnp.sum(jnp.sum(a, axis=0, keepdims=True), axis=1, keepdims=True)

    occupied_sum = whole(occupied[0] + occupied[1])
    warm_sum = whole(warm[0] + warm[1] + warm_rows)
    arrived(sens_moving)
    clear(scc, sen, 3, 3)
    filter_y_rest(sen, scc, 3)

    def last_body(i, acc):
        out = filter_xz(PAD + big * i, big)
        fil[:, pl.ds(big * i, big)] = out
        return acc + jnp.sum(out * out, axis=1)

    square = lax.fori_loop(0, n // big, last_body, jnp.zeros(shape, F32))
    store(lambda h: fil.at[h], f_out)

    lane = lax.broadcasted_iota(jnp.int32, (1, 128), 1)
    message = jnp.where(
        lane == 0,
        whole(square[0] + square[1]),
        jnp.where(lane == 1, occupied_sum, warm_sum),
    )

    def exchange(value, slots, me, size, peer, sends, recvs):
        slots[me, 0:1] = value
        for k in farthest_first(size):
            pltpu.make_async_remote_copy(
                src_ref=slots.at[me, pl.ds(0, 1)], dst_ref=slots.at[me, pl.ds(0, 1)],
                send_sem=sends.at[0], recv_sem=recvs.at[0],
                device_id=peer(k), device_id_type=MESH,
            ).start()
        others = slots.at[pl.ds(0, size - 1), pl.ds(0, 1)]
        every = pltpu.make_async_remote_copy(
            src_ref=others, dst_ref=others, send_sem=sends.at[0], recv_sem=recvs.at[0],
            device_id=peer(1), device_id_type=MESH,
        )
        every.wait_recv()
        pending.append((every, 0, 0))
        parts = [slots[k, 0:1] for k in range(size)]
        while len(parts) > 1:
            parts = [a + b for a, b in zip(parts[::2], parts[1::2])]
        return parts[0]

    message = exchange(message, slots1, me1, size1, peer1, r1_send, r1_recv)
    message = exchange(message, slots2, me2, size2, peer2, r2_send, r2_recv)
    sums_out[...] = jnp.broadcast_to(message, (8, 128))
    for c, dx, dy in pending:

        @pl.when(exists(dx, dy))
        def _(c=c):
            c.wait_send()

    for c in stores:
        c.wait()


def finish(
    total, v, t, d, f, sums_ref, v_out, t_out, d_out, f_out, occ_out, mean_out, buf, sem
):
    copies = [
        pltpu.make_async_copy(src, dst, sem.at[i])
        for i, (src, dst) in enumerate(((v, v_out), (t, t_out), (d, d_out)))
    ]
    for c in copies:
        c.start()
    sums = sums_ref[0:1] * (1.0 / total)
    scale = jnp.broadcast_to(1.0 / jnp.sqrt(sums[:, 0:1] + 1e-6), (8, 256))
    parts = 4
    step = buf.shape[0] // parts
    for i in range(parts):
        part = pl.ds(step * i, step)
        buf[part] = f[part] * scale
        c = pltpu.make_async_copy(buf.at[part], f_out.at[part], sem.at[3 + i])
        c.start()
        copies.append(c)
    occ_out[0] = sums[0, 1]
    mean_out[0] = sums[0, 2]
    for c in copies:
        c.wait()


def per_device(nx, ny, *args):
    n = args[0].shape[0]
    assert args[0].shape[1:] == (8, 256) and n % 8 == 0
    field = jax.ShapeDtypeStruct(args[0].shape, F32)
    tile = jax.ShapeDtypeStruct((8, 128), F32)
    wide = n + 2 * PAD

    def vm(*shape, dtype=F32):
        return pltpu.VMEM(shape, dtype)

    planes = vm(2, wide, 8, 128)
    own = vm(2, n, 8, 128)
    edge = vm(1, 2, wide, 128)
    edge_out = vm(1, 2, n, 128)
    scratch = [
        planes, vm(5, 2, n, 8, 128), vm(4, 2, n, 8, 128, dtype=jnp.int32),
        vm(3, 2, wide, 8, 128), vm(2, 2, 8, 128, dtype=jnp.int32),
        vm(5, 2, 2, wide, 128), own,
        vm(8, 2, wide, 128), vm(3, 2, n, 128), vm(3, 2, n, 128),
        vm(3, 2, wide, 128), vm(3, 2, wide, 128), vm(3, 2, n, 128), vm(3, 2, n, 128),
        vm(256, 256, dtype=BF16), planes, planes,
        edge, vm(1, 2, PAD + n, 128), own,
        vm(3, 2, n, 8, 128), planes, edge, edge, edge_out, edge_out,
        planes, edge, edge_out, own, own, planes, edge, edge_out, own,
        planes, vm(8, 2, wide, 128), vm(3, 2, n, 128), vm(3, 2, n, 128), own,
        vm(nx * 2, 8, 128), vm(ny // 2, 8, 128),
        pltpu.SemaphoreType.DMA((20,)), pltpu.SemaphoreType.DMA((8,)),
        pltpu.SemaphoreType.DMA((64,)), pltpu.SemaphoreType.DMA((64,)),
        pltpu.SemaphoreType.DMA((1,)), pltpu.SemaphoreType.DMA((1,)),
        pltpu.SemaphoreType.DMA((1,)), pltpu.SemaphoreType.DMA((1,)),
    ]
    anywhere = pl.BlockSpec(memory_space=pl.ANY)
    hbm = pl.BlockSpec(memory_space=pltpu.HBM)
    vmem = pl.BlockSpec(memory_space=pltpu.VMEM)
    smem = pl.BlockSpec(memory_space=pltpu.SMEM)
    *fields, sums = pl.pallas_call(
        functools.partial(kernel, nx, ny, n),
        out_shape=(field, field, field, field, tile),
        in_specs=[hbm] * 10,
        out_specs=(anywhere,) * 4 + (vmem,),
        scratch_shapes=scratch,
        compiler_params=pltpu.CompilerParams(
            collective_id=0, has_side_effects=True, vmem_limit_bytes=103 * 512 * 1024
        ),
    )(*args)
    one = jax.ShapeDtypeStruct((1,), F32)
    *outs, occupied, mean = pl.pallas_call(
        functools.partial(finish, float(nx * ny * n * 8 * 256)),
        out_shape=(field, field, field, field, one, one),
        in_specs=[anywhere] * 3 + [vmem, vmem],
        out_specs=(hbm,) * 4 + (smem, smem),
        scratch_shapes=[vm(n, 8, 256), pltpu.SemaphoreType.DMA((8,))],
        compiler_params=pltpu.CompilerParams(vmem_limit_bytes=8 * 1024 * 1024),
    )(*fields, sums)
    return (*outs, occupied.reshape(()), mean.reshape(()))


def solution(mesh):
    spec = P("gx", "gy", None)
    return jax.shard_map(
        functools.partial(per_device, mesh.shape["gx"], mesh.shape["gy"]),
        mesh=mesh,
        in_specs=(spec,) * 10,
        out_specs=(spec,) * 4 + (P(), P()),
        check_vma=False,
    )
```

```python
import functools

import jax
import jax.numpy as jnp
from jax import lax
from jax.experimental import pallas as pl
from jax.experimental.pallas import tpu as pltpu
from jax.sharding import PartitionSpec as P

MESH = pl.DeviceIdType.MESH
F32 = jnp.float32
BF16 = jnp.bfloat16
PAD = 8
OFFSETS = ((0, 1), (0, -1), (1, 1), (-1, 1), (1, -1), (-1, -1), (1, 0), (-1, 0))


def lanes(shape):
    return lax.broadcasted_iota(jnp.int32, shape, len(shape) - 1)


def z_next(p):
    r = pltpu.roll(p, 127, axis=p.ndim - 1)
    lane = lanes(p.shape[1:])
    low = jnp.where(lane < 127, r[0], r[1])
    high = jnp.where(lane < 127, r[1], 0.0)
    return jnp.stack([low, high])


def z_prev(p):
    r = pltpu.roll(p, 1, axis=p.ndim - 1)
    lane = lanes(p.shape[1:])
    low = jnp.where(lane > 0, r[0], 0.0)
    high = jnp.where(lane > 0, r[1], r[0])
    return jnp.stack([low, high])


def rows_of(shape):
    return lax.broadcasted_iota(jnp.int32, shape, len(shape) - 2)


def y_next(p, row):
    r = pltpu.roll(p, 7, axis=1)
    return jnp.where(rows_of(p.shape) < 7, r, jnp.broadcast_to(row, p.shape))


def y_prev(p):
    r = pltpu.roll(p, 1, axis=1)
    return jnp.where(rows_of(p.shape) > 0, r, 0.0)


def z_forward(p):
    q = z_next(p)
    return p + q, q - p


def yz_forward(p, row_s, row_d):
    s, d = z_forward(p)
    sy, dy = y_next(s, row_s), y_next(d, row_d)
    return s + sy, d + dy, sy - s, dy - d


def rows_forward(near, far):
    (s, d), (sy, dy) = z_forward(near), z_forward(far)
    return s + sy, d + dy, sy - s, dy - d


def planes_after(p):
    return pltpu.roll(p, p.shape[1] - 1, axis=1)


def planes_before(p):
    return pltpu.roll(p, 1, axis=1)


def x_forward(a, b):
    return [a[i] + b[i] for i in range(1, 4)], [b[i] - a[i] for i in range(4)]


def weigh(sums, diffs, w):
    w1, w2, w3 = w * (1.0 / 48.0), w * (1.0 / 24.0), w * (1.0 / 16.0)
    return (
        [w3 * sums[0], w3 * sums[1], w2 * sums[2]],
        [w3 * diffs[0], w2 * diffs[1], w2 * diffs[2], w1 * diffs[3]],
    )


def x_backward(sums, diffs):
    front = [-diffs[0]] + [sums[i] - diffs[i + 1] for i in range(3)]
    behind = [diffs[0]] + [sums[i] + diffs[i + 1] for i in range(3)]
    return front, behind


def yz_backward(n):
    ns = (n[0] - n[2]) + y_prev(n[0] + n[2])
    nd = (n[1] - n[3]) + y_prev(n[1] + n[3])
    return (ns - nd) + z_prev(ns + nd)


def energy(sa, da, sb, db):
    three = da[0] * db[0] + sa[0] * sb[0] + sa[1] * sb[1]
    two = da[1] * db[1] + da[2] * db[2] + sa[2] * sb[2]
    return (1.0 / 16.0) * three + (1.0 / 24.0) * two + (1.0 / 48.0) * (da[3] * db[3])


def spread(p):
    t = p + y_prev(p)
    return t + z_prev(t)


def row_pack(ref, h, first, planes, row):
    every = ref.shape[1]
    flat = ref.reshape(2 * every * 8, 128)
    return flat[pl.ds((h * every + first) * 8 + row, planes, stride=8), :]


def row_add(ref, h, first, planes, row, value):
    every = ref.shape[1]
    flat = ref.reshape(2 * every * 8, 128)
    where = pl.ds((h * every + first) * 8 + row, planes, stride=8)
    flat[where, :] = flat[where, :] + value


def edge_column(edge, h, p):
    every = edge.shape[2]
    flat = edge.reshape(8 * 2 * every, 128)
    return flat[pl.ds(h * every + p, 8, stride=2 * every), :]


def kernel(
    nx, ny, n,
    des_in, v_in, t_in, d_in, q_in, o_in, e_in, s_in, g_in, c_in,
    v_out, t_out, d_out, f_out, sums_out,
    des, raw, flg, fld, flx, zrow, coef,
    cc, cup, cdn, flo, fhi, fup, fdn,
    wz, yf, cub, cube, cubs, ca,
    kap, v1, v1lo, v1hi, v1up, v1dn,
    d1, d1hi, d1dn, t0, tr, t1, t1hi, t1dn, joule,
    sen, scc, sup, sdn, fil, slots1, slots2,
    in_sem, out_sem, send_sem, recv_sem, r1_send, r1_recv, r2_send, r2_recv,
):
    gx, gy = lax.axis_index("gx"), lax.axis_index("gy")
    total = float(nx * n * ny * 8 * 256)
    end = PAD + n
    big, half = min(32, n // 2), min(16, n)
    split = big + 8
    first_x, last_x = gx == 0, gx == nx - 1
    first_y, last_y = gy == 0, gy == ny - 1

    barrier = pltpu.get_barrier_semaphore()

    def device(dx, dy):
        return (lax.rem(gx + (nx + dx), nx), lax.rem(gy + (ny + dy), ny))

    chip, core = lax.div(gy, 2), lax.rem(gy, 2)
    size1, size2 = nx * 2, ny // 2
    me1, me2 = gx * 2 + core, chip

    def peer1(k):
        other = lax.rem(me1 + k, size1)
        return (lax.div(other, 2), chip * 2 + lax.rem(other, 2))

    def peer2(k):
        return (gx, lax.rem(me2 + k, size2) * 2 + core)

    def farthest_first(size):
        return sorted(range(1, size), key=lambda k: abs(2 * k - size))

    loads = []
    plan = [
        (des_in, lambda h: des.at[h, PAD:end]),
        (v_in, lambda h: raw.at[0, h]),
        (g_in, lambda h: flg.at[2, h]),
        (t_in, lambda h: raw.at[1, h]),
        (d_in, lambda h: raw.at[2, h]),
        (c_in, lambda h: flg.at[3, h]),
        (e_in, lambda h: flg.at[0, h]),
        (s_in, lambda h: flg.at[1, h]),
        (q_in, lambda h: raw.at[3, h]),
        (o_in, lambda h: raw.at[4, h]),
    ]
    for i, (src, dst) in enumerate(plan):
        pair = []
        for h in range(2):
            c = pltpu.make_async_copy(
                src.at[:, :, pl.ds(128 * h, 128)], dst(h), in_sem.at[2 * i + h]
            )
            pair.append(c)
        loads.append(pair)

    def load(*which):
        for i in which:
            for c in loads[i]:
                c.start()

    load(0)

    def loaded(*which):
        for i in which:
            for c in loads[i]:
                c.wait()

    for k in range(max(size1, size2) - 1):
        for size, peer in ((size2, peer2), (size1, peer1)):
            if k < size - 1:
                pl.semaphore_signal(
                    barrier, inc=1, device_id=peer(farthest_first(size)[k]), device_id_type=MESH
                )
    for dx, dy in OFFSETS:
        pl.semaphore_signal(barrier, inc=1, device_id=device(dx, dy), device_id_type=MESH)
    load(1, 2)

    count = [0]

    def exists(dx, dy):
        x, y = gx + dx, gy + dy
        return (x >= 0) & (x < nx) & (y >= 0) & (y < ny)

    def send(src, dst, dx, dy):
        k = count[0]
        count[0] += 1
        c = pltpu.make_async_remote_copy(
            src_ref=src, dst_ref=dst, send_sem=send_sem.at[k], recv_sem=recv_sem.at[k],
            device_id=device(dx, dy), device_id_type=MESH,
        )

        @pl.when(exists(dx, dy))
        def _():
            c.start()

        return c, dx, dy

    def send_up(src, dst):
        return [
            send(src, dst.at[:, :, PAD:end], 0, 1),
            send(src.at[:, :, n - PAD : n], dst.at[:, :, 0:PAD], 1, 1),
            send(src.at[:, :, 0:PAD], dst.at[:, :, end : end + PAD], -1, 1),
        ]

    def send_down(src, dst, both=True):
        some = [
            send(src, dst.at[:, :, PAD:end], 0, -1),
            send(src.at[:, :, 0:PAD], dst.at[:, :, end : end + PAD], -1, -1),
        ]
        if both:
            some.append(send(src.at[:, :, n - PAD : n], dst.at[:, :, 0:PAD], 1, -1))
        return some

    def send_first(src, dst, dy):
        return [
            send(src.at[:, :, 0:split], dst.at[:, :, PAD : PAD + split], 0, dy),
            send(src.at[:, :, n - PAD : n], dst.at[:, :, 0:PAD], 1, dy),
        ]

    def send_second(src, dst, dy):
        return [
            send(src.at[:, :, split:n], dst.at[:, :, PAD + split : end], 0, dy),
            send(src.at[:, :, 0:PAD], dst.at[:, :, end : end + PAD], -1, dy),
        ]

    pending = []

    def arrived(copies):
        for c, dx, dy in copies:

            @pl.when(exists(-dx, -dy))
            def _(c=c):
                c.wait_recv()

        pending.extend(copies)

    def tails_up(ref, up):
        for h in range(2):
            a, b, c = (row_pack(ref, h, PAD, n, j) for j in (5, 6, 7))
            up[0, h] = a + 2.0 * b + 3.0 * c
            up[1, h] = b + 2.0 * c
            up[2, h] = c

    def tails_down(ref, down):
        for h in range(2):
            a, b, c = (row_pack(ref, h, PAD, n, j) for j in (0, 1, 2))
            down[0, h] = a
            down[1, h] = 2.0 * a + b
            down[2, h] = 3.0 * a + 2.0 * b + c

    loaded(0)
    load(3, 4, 5, 6, 7, 8, 9)
    tails_down(des, cdn)
    tails_up(des, cup)
    pl.semaphore_wait(barrier, len(OFFSETS) + size1 - 1 + size2 - 1)
    moving1 = send_first(cup, cc.at[0:3], 1) + send_first(cdn, cc.at[5:8], -1)
    moving1.append(send(des.at[:, end - 4 : end], des.at[:, PAD - 4 : PAD], 1, 0))
    moving2 = send_second(cup, cc.at[0:3], 1) + send_second(cdn, cc.at[5:8], -1)
    moving2.append(send(des.at[:, PAD : PAD + 3], des.at[:, end : end + 3], -1, 0))

    def mask(f, flag):
        def body(i, carry):
            x = i * 16
            free = flg[flag, :, pl.ds(x, 16)] == 0
            fld[f, :, pl.ds(PAD + x, 16)] = jnp.where(free, raw[f, :, pl.ds(x, 16)], 0.0)
            return carry

        lax.fori_loop(0, n // 16, body, 0)
        for h in range(2):
            fup[f, h] = row_pack(fld.at[f], h, PAD, n, 7)
            fdn[f, h] = row_pack(fld.at[f], h, PAD, n, 0)

    def send_fields(a, b):
        return (
            send_up(fup.at[a:b], flo.at[a:b])
            + send_down(fdn.at[a:b], fhi.at[a:b])
            + [
                send(fld.at[a:b, :, end - 1 : end], fld.at[a:b, :, PAD - 1 : PAD], 1, 0),
                send(fld.at[a:b, :, PAD : PAD + 1], fld.at[a:b, :, end : end + 1], -1, 0),
            ]
        )

    loaded(1, 2)
    mask(0, 2)
    volt_field_moving = send_fields(0, 1)
    loaded(6, 7)
    moving2.append(send(flg.at[0:2, :, n - 1], flx, 1, 0))
    zero_rows = jnp.zeros((2, 2, end + PAD, 128), F32)
    cc[3:5] = zero_rows
    scc[3:5] = zero_rows
    wi = lax.broadcasted_iota(jnp.int32, (256, 256), 0)
    wj = lax.broadcasted_iota(jnp.int32, (256, 256), 1)
    wz[...] = jnp.maximum(4 - jnp.abs(wi - wj), 0).astype(F32).astype(BF16)
    loaded(3, 4, 5)
    mask(1, 3)
    mask(2, 3)

    row = lax.broadcasted_iota(jnp.int32, (8, 128), 0)

    def filter_y(ref, p):
        for h in range(2):
            a = ref[h, p]
            out = 4.0 * a
            for k in (1, 2, 3):
                out += jnp.where(row < 8 - k, float(4 - k), 0.0) * pltpu.roll(a, 8 - k, axis=0)
                out += jnp.where(row >= k, float(4 - k), 0.0) * pltpu.roll(a, k, axis=0)
            yf[h, p] = out

    def filter_y_own(ref):
        def body(i, carry):
            for u in range(8):
                filter_y(ref, PAD + 8 * i + u)
            return carry

        lax.fori_loop(0, n // 8, body, 0)

    def filter_y_rest(ref, edge, outer, start, stop):
        for p in outer:
            filter_y(ref, p)

        def add(p):
            for h in range(2):
                yf[h, p] += edge_column(edge, h, p)

        def body(i, carry):
            for u in range(8):
                add(start + 8 * i + u)
            return carry

        lax.fori_loop(0, (stop - start) // 8, body, 0)
        for p in outer:
            add(p)

    def filter_y_first(ref, edge, low):
        filter_y_rest(ref, edge, range(PAD - low, PAD), PAD, PAD + split)

    def filter_y_second(ref, edge):
        filter_y_rest(ref, edge, range(end, end + 3), PAD + split, end)

    def filter_xz(p, planes):
        halves = []
        for h in range(2):
            a = yf[h, pl.ds(p - 3, planes + 6)]
            a = a[:-1] + a[1:]
            a = a[:-2] + a[2:]
            a = a[:-1] + a[1:]
            a = a[:-2] + a[2:]
            halves.append(a.reshape(planes * 8, 128))
        a = jnp.concatenate(halves, axis=1)
        high = a.astype(BF16)
        rest = a - high.astype(F32)
        mid = rest.astype(BF16)
        low = (rest - mid.astype(F32)).astype(BF16)
        w = wz[...]
        out = (
            jnp.dot(low, w, preferred_element_type=F32)
            + jnp.dot(mid, w, preferred_element_type=F32)
            + jnp.dot(high, w, preferred_element_type=F32)
        )
        return jnp.stack(
            [out[:, :128].reshape(planes, 8, 128), out[:, 128:].reshape(planes, 8, 128)]
        )

    def inverse_window(i, full):
        w = jnp.where(i == 0, 10, jnp.where(i == 1, 13, jnp.where(i == 2, 15, 16)))
        k = full - 1 - i
        return jnp.where(k == 0, w - 6, jnp.where(k == 1, w - 3, jnp.where(k == 2, w - 1, w)))

    shape = (2, 8, 128)
    yy = gy * 8 + lax.broadcasted_iota(jnp.int32, shape, 1)
    zz = lax.broadcasted_iota(jnp.int32, shape, 0) * 128 + lax.broadcasted_iota(jnp.int32, shape, 2)
    inv_yz = 1.0 / (inverse_window(yy, ny * 8) * inverse_window(zz, 256)).astype(F32)
    touch_yz = (jnp.where(yy == 0, 1, 2) * jnp.where(zz == 0, 1, 2)).astype(F32)

    def inv_x(p):
        i = gx * n + (p - PAD)
        full = nx * n
        r = jnp.where(i == 0, 1 / 10.0, jnp.where(i == 1, 1 / 13.0, jnp.where(i == 2, 1 / 15.0, 1 / 16.0)))
        k = full - 1 - i
        return jnp.where(
            k == 0, 1 / 10.0, jnp.where(k == 1, 1 / 13.0, jnp.where(k == 2, 1 / 15.0, r))
        ).astype(F32)

    filter_y_own(des)

    def clear(edge, field, low, high):
        @pl.when(first_x)
        def _():
            if low:
                field[:, PAD - low : PAD] = jnp.zeros((2, low, 8, 128), F32)
            edge[:, :, 0:PAD] = jnp.zeros((8, 2, PAD, 128), F32)

        @pl.when(last_x)
        def _():
            field[:, end : end + high] = jnp.zeros((2, high, 8, 128), F32)
            edge[:, :, end : end + PAD] = jnp.zeros((8, 2, PAD, 128), F32)

        @pl.when(first_y)
        def _():
            edge[0:3] = jnp.zeros((3, 2, end + PAD, 128), F32)

        @pl.when(last_y)
        def _():
            edge[5:8] = jnp.zeros((3, 2, end + PAD, 128), F32)

    clear(cc, des, 4, 3)
    clear(scc, sen, 3, 3)
    arrived(moving1)
    heat_fields_moving = send_fields(1, 3)
    filter_y_first(des, cc, 4)
    there_x = jnp.where(first_x, 0.0, 1.0).astype(F32)
    there_y = jnp.where(first_y, 0.0, 1.0).astype(F32)

    def density(smoothed, p, e, s):
        solid = smoothed * inv_yz * inv_x(p)
        return jnp.where(e == 1, 0.0, jnp.where(s == 1, 1.0, solid))

    def density_body(i, acc):
        p = PAD + big * i
        smoothed = filter_xz(p, big)
        for u in range(big):
            x = big * i + u
            rho = density(smoothed[:, u], p + u, flg[0, :, x], flg[1, :, x])
            squared = rho * rho
            held = (flg[0, :, x] + flg[1, :, x]) == 0
            coef[:, x] = jnp.where(held, (3.0 * squared) * inv_yz * inv_x(p + u), 0.0)
            cub[:, p + u] = squared * rho
            acc = acc + rho
        return acc

    occupied = density_body(0, jnp.zeros(shape, F32))
    arrived(moving2)
    filter_y_second(des, cc)
    occupied = lax.fori_loop(1, n // big, density_body, occupied)
    before = density(filter_xz(PAD - 2, 2)[:, 1], PAD - 1, flx[0], flx[1])
    cub[:, PAD - 1] = there_x * (before * before * before)

    for h in range(2):
        cubs[0, h] = row_pack(cub, h, 0, end, 7)
    cube_moving = [send(cubs, cube.at[:, :, 0:end], 0, 1)]

    def gather_body(i, last):
        for u in range(8):
            now = spread(cub[:, PAD + 8 * i + u])
            ca[:, 8 * i + u] = now + last
            last = now
        return last

    lax.fori_loop(0, n // 8, gather_body, spread(cub[:, PAD - 1]))

    def clear_fields(a, b):
        @pl.when(first_x)
        def _():
            fld[a:b, :, PAD - 1] = jnp.zeros((b - a, 2, 8, 128), F32)
            flo[a:b, :, 0:PAD] = jnp.zeros((b - a, 2, PAD, 128), F32)
            fhi[a:b, :, 0:PAD] = jnp.zeros((b - a, 2, PAD, 128), F32)

        @pl.when(last_x)
        def _():
            fld[a:b, :, end] = jnp.zeros((b - a, 2, 8, 128), F32)
            flo[a:b, :, end : end + PAD] = jnp.zeros((b - a, 2, PAD, 128), F32)
            fhi[a:b, :, end : end + PAD] = jnp.zeros((b - a, 2, PAD, 128), F32)

        @pl.when(first_y)
        def _():
            flo[a:b] = jnp.zeros((b - a, 2, end + PAD, 128), F32)

        @pl.when(last_y)
        def _():
            fhi[a:b] = jnp.zeros((b - a, 2, end + PAD, 128), F32)

    arrived(volt_field_moving)
    clear_fields(0, 1)

    def far_rows(k, edge):
        s, d = z_forward(edge)
        zrow[k, 0] = s
        zrow[k, 1] = d

    def forward_of(field, k):
        def forward(p):
            return yz_forward(
                field[:, p], zrow[k, 0, :, pl.ds(p, 1)], zrow[k, 1, :, pl.ds(p, 1)]
            )

        return forward

    far_rows(0, fhi[0])
    weights = ((0.001, 0.999), (0.05, 0.95), (0.05, 0.95))

    def apply_main(which, base, slope, step):
        forwards = [forward_of(fld.at[f], f) for f in which]

        def element(a, b, w):
            return x_backward(*weigh(*x_forward(a, b), w))

        start = []
        w = there_x * base + slope * cub[:, PAD - 1]
        for forward in forwards:
            a, b = forward(PAD - 1), forward(PAD)
            start.append((tuple(b), tuple(element(a, b, w)[1])))

        def body(i, carry):
            carry = list(carry)
            for u in range(step):
                x = step * i + u
                w = base + slope * cub[:, PAD + x]
                for k, f in enumerate(which):
                    a, behind = carry[k]
                    b = forwards[k](PAD + x + 1)
                    front, new = element(a, b, w)
                    kap[f, :, x] = yz_backward([front[c] + behind[c] for c in range(4)])
                    carry[k] = tuple(b), tuple(new)
            return tuple(carry)

        lax.fori_loop(0, n // step, body, tuple(start))

    def edge_weight(base, slope):
        where = lax.broadcasted_iota(jnp.int32, (2, end + PAD, 128), 1)
        real = jnp.where(where == PAD - 1, there_x, 1.0) * there_y
        return base * real + (slope * there_y) * cube[0]

    def whole_row(ref, j):
        return jnp.stack([row_pack(ref, h, 0, end + PAD, j) for h in range(2)])

    def rows_x_forward(a):
        return x_forward(a, [planes_after(c) for c in a])

    def apply_edge(f):
        a = rows_forward(flo[f], whole_row(fld.at[f], 0))
        front, behind = x_backward(*weigh(*rows_x_forward(a), edge_weight(*weights[f])))
        m = [front[c] + planes_before(behind[c]) for c in range(4)]
        ns, nd = m[0] + m[2], m[1] + m[3]
        out = (ns - nd) + z_prev(ns + nd)
        for h in range(2):
            row_add(kap.at[f], h, 0, n, 0, out[h, PAD:end])

    apply_main((0,), *weights[0], big)

    arrived(cube_moving)

    @pl.when(first_y)
    def _():
        cube[0] = jnp.zeros((2, end + PAD, 128), F32)

    apply_edge(0)
    edge_cube = cube[0] * there_y
    edge_cube = edge_cube + planes_before(edge_cube)
    edge_cube = edge_cube + z_prev(edge_cube)
    for h in range(2):
        row_add(ca, h, 0, n, 0, edge_cube[h, PAD:end])

    def pivot(x, base, slope):
        cx = jnp.where(gx * n + x == 0, 1.0, 2.0).astype(F32)
        return base * (cx * touch_yz) + slope * ca[:, x]

    loaded(8, 9)

    def volt_body(i, carry):
        for u in range(8):
            x = 8 * i + u
            v = raw[0, :, x]
            moved = 1.8 * (raw[3, :, x] - kap[0, :, x]) / pivot(x, 0.001, 0.999)
            v1[:, PAD + x] = v + jnp.where(flg[2, :, x] == 0, moved, -0.6 * v)
        return carry

    lax.fori_loop(0, n // 8, volt_body, 0)
    for h in range(2):
        v1up[0, h] = row_pack(v1, h, PAD, n, 7)
        v1dn[0, h] = row_pack(v1, h, PAD, n, 0)
    volt_moving = send_up(v1up, v1lo) + send_down(v1dn, v1hi)
    volt_moving += [
        send(v1.at[:, end - 1 : end], v1.at[:, PAD - 1 : PAD], 1, 0),
        send(v1.at[:, PAD : PAD + 1], v1.at[:, end : end + 1], -1, 0),
    ]
    stores = []

    def store(src, dst):
        for h in range(2):
            c = pltpu.make_async_copy(
                src(h), dst.at[:, :, pl.ds(128 * h, 128)], out_sem.at[len(stores)]
            )
            c.start()
            stores.append(c)

    store(lambda h: v1.at[h, PAD:end], v_out)

    arrived(heat_fields_moving)
    clear_fields(1, 3)
    far_rows(1, fhi[1])
    far_rows(2, fhi[2])
    apply_main((1, 2), *weights[1], half)
    apply_edge(1)
    apply_edge(2)

    def heat_body(i, carry):
        for u in range(8):
            x = 8 * i + u
            free = flg[3, :, x] == 0
            step = 1.8 / pivot(x, 0.05, 0.95)
            d = raw[2, :, x]
            d1[:, PAD + x] = d + jnp.where(free, step * (raw[4, :, x] - kap[2, :, x]), -0.6 * d)
            t = raw[1, :, x]
            t0[:, x] = t - jnp.where(free, step * kap[1, :, x], 0.6 * t)
            tr[:, x] = jnp.where(free, step, 0.0)
        return carry

    lax.fori_loop(0, n // 8, heat_body, 0)
    for h in range(2):
        d1dn[0, h] = row_pack(d1, h, PAD, n, 0)
    dual_moving = send_down(d1dn, d1hi, both=False)
    dual_moving.append(send(d1.at[:, PAD : PAD + 1], d1.at[:, end : end + 1], -1, 0))
    store(lambda h: d1.at[h, PAD:end], d_out)

    arrived(volt_moving)

    def clear_high(field, *edges):
        @pl.when(last_x)
        def _():
            field[:, end] = jnp.zeros((2, 8, 128), F32)
            for edge in edges:
                edge[0, :, end : end + PAD] = jnp.zeros((2, PAD, 128), F32)

        @pl.when(last_y)
        def _():
            edges[0][0] = jnp.zeros((2, end + PAD, 128), F32)

    clear_high(v1, v1hi, v1lo)

    @pl.when(first_x)
    def _():
        v1[:, PAD - 1] = jnp.zeros((2, 8, 128), F32)
        v1hi[0, :, 0:PAD] = jnp.zeros((2, PAD, 128), F32)
        v1lo[0, :, 0:PAD] = jnp.zeros((2, PAD, 128), F32)

    @pl.when(first_y)
    def _():
        v1lo[0] = jnp.zeros((2, end + PAD, 128), F32)


    far_rows(3, v1hi[0])
    volt_forward = forward_of(v1, 3)
    def row_energy(near, far):
        s, d = rows_x_forward(rows_forward(near, far))
        return energy(s, d, s, d)

    def row_gather(e):
        e = e + planes_before(e)
        return (e + z_prev(e))[:, PAD:end]

    row0 = whole_row(v1, 0)
    extra = row_gather(row_energy(v1lo[0], row0) * (edge_weight(0.001, 0.999) * 0.125))
    where = lax.broadcasted_iota(jnp.int32, (2, end + PAD, 128), 1)
    own_weight = 0.001 * jnp.where(where == PAD - 1, there_x, 1.0) + 0.999 * whole_row(cub, 0)
    heat0 = extra + row_gather(row_energy(row0, whole_row(v1, 1)) * (own_weight * 0.125))
    for h in range(2):
        t1dn[0, h] = row_pack(t0, h, 0, n, 0) + row_pack(tr, h, 0, n, 0) * heat0[h]
    temp_moving = send_down(t1dn, t1hi, both=False)

    a = volt_forward(PAD - 1)
    b = volt_forward(PAD)
    s, d = x_forward(a, b)
    lead = energy(s, d, s, d) * ((there_x * 0.001 + 0.999 * cub[:, PAD - 1]) / 8.0)

    def joule_body(i, carry):
        a, last, acc = carry
        for u in range(half):
            x = half * i + u
            b = volt_forward(PAD + x + 1)
            s, d = x_forward(a, b)
            e = energy(s, d, s, d)
            joule[:, x] = e
            now = spread(e * (0.001 / 8.0 + (0.999 / 8.0) * cub[:, PAD + x]))
            t = t0[:, x] + tr[:, x] * (now + last)
            t1[:, PAD + x] = t
            acc = acc + raw[4, :, x] * t
            a, last = b, now
        return tuple(a), last, acc

    carry = joule_body(0, (tuple(b), spread(lead), jnp.zeros(shape, F32)))
    for h in range(2):
        t1[h, PAD, 0:1] += extra[h, 0:1] * tr[h, 0, 0:1]
    temp_moving.append(send(t1.at[:, PAD : PAD + 1], t1.at[:, end : end + 1], -1, 0))
    _, _, warm = lax.fori_loop(1, n // half, joule_body, carry)

    warm_rows = jnp.zeros((8, 128), F32)
    for h in range(2):
        more = extra[h] * row_pack(tr, h, 0, n, 0)
        row_add(t1, h, PAD + 1, n - 1, 0, more[1:])
        warm_rows = warm_rows + jnp.sum(
            (more * row_pack(raw.at[4], h, 0, n, 0)).reshape(n // 8, 8, 128), axis=0
        )
    store(lambda h: t1.at[h, PAD:end], t_out)

    arrived(dual_moving)
    clear_high(d1, d1hi)
    far_rows(4, d1hi[0])
    dual_forward = forward_of(d1, 4)
    none = jnp.zeros((2, 1, 128), F32)

    def pair_forward(p):
        return tuple(yz_forward(t1[:, p], none, none)), tuple(dual_forward(p))

    def sens_body(i, carry):
        ta, da = carry
        for u in range(half):
            x = half * i + u
            tb, db = pair_forward(PAD + x + 1)
            ts, td = x_forward(ta, tb)
            ds, dd = x_forward(da, db)
            mean = (0.999 / 8.0) * (da[0] + db[0])
            value = joule[:, x] * mean - 0.95 * energy(ts, td, ds, dd)
            sen[:, PAD + x] = coef[:, x] * value
            ta, da = tb, db
        return ta, da

    carry = lax.fori_loop(0, n // half - 1, sens_body, pair_forward(PAD))
    dual_s, dual_d = rows_x_forward(rows_forward(whole_row(d1, 7), d1hi[0]))
    arrived(temp_moving)
    clear_high(t1, t1hi)
    sens_body(n // half - 1, carry)
    tails_down(sen, sdn)
    sens1 = send_first(sdn, scc.at[5:8], -1)
    sens2 = send_second(sdn, scc.at[5:8], -1)
    behind_s, behind_d = z_forward(t1hi[0])
    temp_s, temp_d = rows_x_forward((behind_s, behind_d, behind_s, behind_d))
    work = 0.95 * energy(temp_s, temp_d, dual_s, dual_d)
    for h in range(2):
        row_add(sen, h, PAD, n, 7, -work[h, PAD:end] * row_pack(coef, h, 0, n, 7))
    tails_up(sen, sup)
    sens1 += send_first(sup, scc.at[0:3], 1)
    sens1.append(send(sen.at[:, end - 3 : end], sen.at[:, PAD - 3 : PAD], 1, 0))
    sens2 += send_second(sup, scc.at[0:3], 1)
    sens2.append(send(sen.at[:, PAD : PAD + 3], sen.at[:, end : end + 3], -1, 0))
    filter_y_own(sen)

    def whole(a):
        return jnp.sum(jnp.sum(a, axis=0, keepdims=True), axis=1, keepdims=True)

    occupied_sum = whole(occupied[0] + occupied[1])
    warm_sum = whole(warm[0] + warm[1] + warm_rows)
    arrived(sens1)
    filter_y_first(sen, scc, 3)

    def last_body(i, acc):
        out = filter_xz(PAD + big * i, big)
        fil[:, pl.ds(big * i, big)] = out
        return acc + jnp.sum(out * out, axis=1)

    square = last_body(0, jnp.zeros(shape, F32))
    arrived(sens2)
    filter_y_second(sen, scc)
    square = lax.fori_loop(1, n // big, last_body, square)
    store(lambda h: fil.at[h], f_out)

    lane = lax.broadcasted_iota(jnp.int32, (1, 128), 1)
    message = jnp.where(
        lane == 0,
        whole(square[0] + square[1]),
        jnp.where(lane == 1, occupied_sum, warm_sum),
    )

    def exchange(value, slots, me, size, peer, sends, recvs):
        slots[me, 0:1] = value
        for k in farthest_first(size):
            pltpu.make_async_remote_copy(
                src_ref=slots.at[me, pl.ds(0, 1)], dst_ref=slots.at[me, pl.ds(0, 1)],
                send_sem=sends.at[0], recv_sem=recvs.at[0],
                device_id=peer(k), device_id_type=MESH,
            ).start()
        others = slots.at[pl.ds(0, size - 1), pl.ds(0, 1)]
        every = pltpu.make_async_remote_copy(
            src_ref=others, dst_ref=others, send_sem=sends.at[0], recv_sem=recvs.at[0],
            device_id=peer(1), device_id_type=MESH,
        )
        every.wait_recv()
        pending.append((every, 0, 0))
        parts = [slots[k, 0:1] for k in range(size)]
        while len(parts) > 1:
            parts = [a + b for a, b in zip(parts[::2], parts[1::2])]
        return parts[0]

    message = exchange(message, slots1, me1, size1, peer1, r1_send, r1_recv)
    message = exchange(message, slots2, me2, size2, peer2, r2_send, r2_recv)
    sums_out[...] = jnp.broadcast_to(message, (8, 128))
    for c, dx, dy in pending:

        @pl.when(exists(dx, dy))
        def _(c=c):
            c.wait_send()

    for c in stores:
        c.wait()


def finish(
    total, v, t, d, f, sums_ref, v_out, t_out, d_out, f_out, occ_out, mean_out, buf, sem
):
    copies = [
        pltpu.make_async_copy(src, dst, sem.at[i])
        for i, (src, dst) in enumerate(((v, v_out), (t, t_out), (d, d_out)))
    ]
    for c in copies:
        c.start()
    sums = sums_ref[0:1] * (1.0 / total)
    scale = jnp.broadcast_to(1.0 / jnp.sqrt(sums[:, 0:1] + 1e-6), (8, 256))
    parts = 4
    step = buf.shape[0] // parts
    for i in range(parts):
        part = pl.ds(step * i, step)
        buf[part] = f[part] * scale
        c = pltpu.make_async_copy(buf.at[part], f_out.at[part], sem.at[3 + i])
        c.start()
        copies.append(c)
    occ_out[0] = sums[0, 1]
    mean_out[0] = sums[0, 2]
    for c in copies:
        c.wait()


def per_device(nx, ny, *args):
    n = args[0].shape[0]
    assert args[0].shape[1:] == (8, 256) and n % 8 == 0
    field = jax.ShapeDtypeStruct(args[0].shape, F32)
    tile = jax.ShapeDtypeStruct((8, 128), F32)
    wide = n + 2 * PAD

    def vm(*shape, dtype=F32):
        return pltpu.VMEM(shape, dtype)

    planes = vm(2, wide, 8, 128)
    own = vm(2, n, 8, 128)
    edge = vm(1, 2, wide, 128)
    edge_out = vm(1, 2, n, 128)
    scratch = [
        planes, vm(5, 2, n, 8, 128), vm(4, 2, n, 8, 128, dtype=jnp.int32),
        vm(3, 2, wide, 8, 128), vm(2, 2, 8, 128, dtype=jnp.int32),
        vm(5, 2, 2, wide, 128), own,
        vm(8, 2, wide, 128), vm(3, 2, n, 128), vm(3, 2, n, 128),
        vm(3, 2, wide, 128), vm(3, 2, wide, 128), vm(3, 2, n, 128), vm(3, 2, n, 128),
        vm(256, 256, dtype=BF16), planes, planes,
        edge, vm(1, 2, PAD + n, 128), own,
        vm(3, 2, n, 8, 128), planes, edge, edge, edge_out, edge_out,
        planes, edge, edge_out, own, own, planes, edge, edge_out, own,
        planes, vm(8, 2, wide, 128), vm(3, 2, n, 128), vm(3, 2, n, 128), own,
        vm(nx * 2, 8, 128), vm(ny // 2, 8, 128),
        pltpu.SemaphoreType.DMA((20,)), pltpu.SemaphoreType.DMA((8,)),
        pltpu.SemaphoreType.DMA((64,)), pltpu.SemaphoreType.DMA((64,)),
        pltpu.SemaphoreType.DMA((1,)), pltpu.SemaphoreType.DMA((1,)),
        pltpu.SemaphoreType.DMA((1,)), pltpu.SemaphoreType.DMA((1,)),
    ]
    anywhere = pl.BlockSpec(memory_space=pl.ANY)
    hbm = pl.BlockSpec(memory_space=pltpu.HBM)
    vmem = pl.BlockSpec(memory_space=pltpu.VMEM)
    smem = pl.BlockSpec(memory_space=pltpu.SMEM)
    *fields, sums = pl.pallas_call(
        functools.partial(kernel, nx, ny, n),
        out_shape=(field, field, field, field, tile),
        in_specs=[hbm] * 10,
        out_specs=(anywhere,) * 4 + (vmem,),
        scratch_shapes=scratch,
        compiler_params=pltpu.CompilerParams(
            collective_id=0, has_side_effects=True, vmem_limit_bytes=103 * 512 * 1024
        ),
    )(*args)
    one = jax.ShapeDtypeStruct((1,), F32)
    *outs, occupied, mean = pl.pallas_call(
        functools.partial(finish, float(nx * ny * n * 8 * 256)),
        out_shape=(field, field, field, field, one, one),
        in_specs=[anywhere] * 3 + [vmem, vmem],
        out_specs=(hbm,) * 4 + (smem, smem),
        scratch_shapes=[vm(n, 8, 256), pltpu.SemaphoreType.DMA((8,))],
        compiler_params=pltpu.CompilerParams(vmem_limit_bytes=8 * 1024 * 1024),
    )(*fields, sums)
    return (*outs, occupied.reshape(()), mean.reshape(()))


def solution(mesh):
    spec = P("gx", "gy", None)
    return jax.shard_map(
        functools.partial(per_device, mesh.shape["gx"], mesh.shape["gy"]),
        mesh=mesh,
        in_specs=(spec,) * 10,
        out_specs=(spec,) * 4 + (P(), P()),
        check_vma=False,
    )
```

```python
import functools

import jax
import jax.numpy as jnp
from jax import lax
from jax.experimental import pallas as pl
from jax.experimental.pallas import tpu as pltpu
from jax.sharding import PartitionSpec as P

MESH = pl.DeviceIdType.MESH
F32 = jnp.float32
BF16 = jnp.bfloat16
PAD = 8
OFFSETS = ((0, 1), (0, -1), (1, 1), (-1, 1), (1, -1), (-1, -1), (1, 0), (-1, 0))


def lanes(shape):
    return lax.broadcasted_iota(jnp.int32, shape, len(shape) - 1)


def z_next(p):
    r = pltpu.roll(p, 127, axis=p.ndim - 1)
    lane = lanes(p.shape[1:])
    low = jnp.where(lane < 127, r[0], r[1])
    high = jnp.where(lane < 127, r[1], 0.0)
    return jnp.stack([low, high])


def z_prev(p):
    r = pltpu.roll(p, 1, axis=p.ndim - 1)
    lane = lanes(p.shape[1:])
    low = jnp.where(lane > 0, r[0], 0.0)
    high = jnp.where(lane > 0, r[1], r[0])
    return jnp.stack([low, high])


def rows_of(shape):
    return lax.broadcasted_iota(jnp.int32, shape, len(shape) - 2)


def y_next(p, row):
    r = pltpu.roll(p, 7, axis=1)
    return jnp.where(rows_of(p.shape) < 7, r, jnp.broadcast_to(row, p.shape))


def y_prev(p):
    r = pltpu.roll(p, 1, axis=1)
    return jnp.where(rows_of(p.shape) > 0, r, 0.0)


def z_forward(p):
    q = z_next(p)
    return p + q, q - p


def yz_forward(p, row_s, row_d):
    s, d = z_forward(p)
    sy, dy = y_next(s, row_s), y_next(d, row_d)
    return s + sy, d + dy, sy - s, dy - d


def rows_forward(near, far):
    (s, d), (sy, dy) = z_forward(near), z_forward(far)
    return s + sy, d + dy, sy - s, dy - d


def planes_after(p):
    return pltpu.roll(p, p.shape[1] - 1, axis=1)


def planes_before(p):
    return pltpu.roll(p, 1, axis=1)


def x_forward(a, b):
    return [a[i] + b[i] for i in range(1, 4)], [b[i] - a[i] for i in range(4)]


def weigh(sums, diffs, w):
    w1, w2, w3 = w * (1.0 / 48.0), w * (1.0 / 24.0), w * (1.0 / 16.0)
    return (
        [w3 * sums[0], w3 * sums[1], w2 * sums[2]],
        [w3 * diffs[0], w2 * diffs[1], w2 * diffs[2], w1 * diffs[3]],
    )


def x_backward(sums, diffs):
    front = [-diffs[0]] + [sums[i] - diffs[i + 1] for i in range(3)]
    behind = [diffs[0]] + [sums[i] + diffs[i + 1] for i in range(3)]
    return front, behind


def yz_backward(n):
    ns = (n[0] - n[2]) + y_prev(n[0] + n[2])
    nd = (n[1] - n[3]) + y_prev(n[1] + n[3])
    return (ns - nd) + z_prev(ns + nd)


def energy(sa, da, sb, db):
    three = da[0] * db[0] + sa[0] * sb[0] + sa[1] * sb[1]
    two = da[1] * db[1] + da[2] * db[2] + sa[2] * sb[2]
    return (1.0 / 16.0) * three + (1.0 / 24.0) * two + (1.0 / 48.0) * (da[3] * db[3])


def spread(p):
    t = p + y_prev(p)
    return t + z_prev(t)


def row_pack(ref, h, first, planes, row):
    every = ref.shape[1]
    flat = ref.reshape(2 * every * 8, 128)
    return flat[pl.ds((h * every + first) * 8 + row, planes, stride=8), :]


def row_add(ref, h, first, planes, row, value):
    every = ref.shape[1]
    flat = ref.reshape(2 * every * 8, 128)
    where = pl.ds((h * every + first) * 8 + row, planes, stride=8)
    flat[where, :] = flat[where, :] + value


def edge_column(edge, h, p):
    every = edge.shape[2]
    flat = edge.reshape(8 * 2 * every, 128)
    return flat[pl.ds(h * every + p, 8, stride=2 * every), :]


def kernel(
    nx, ny, n,
    des_in, v_in, t_in, d_in, q_in, o_in, e_in, s_in, g_in, c_in,
    v_out, t_out, d_out, f_out, sums_out,
    des, raw, flg, fld, flx, zrow, coef,
    cc, cup, cdn, flo, fhi, fup, fdn,
    wz, yf, cub, cube, cubs, ca,
    kap, v1, v1lo, v1hi, v1up, v1dn,
    d1, d1hi, d1dn, t0, tr, t1, t1hi, t1dn, joule,
    sen, scc, sup, sdn, fil, slots1, slots2,
    in_sem, out_sem, send_sem, recv_sem, r1_send, r1_recv, r2_send, r2_recv,
):
    gx, gy = lax.axis_index("gx"), lax.axis_index("gy")
    total = float(nx * n * ny * 8 * 256)
    end = PAD + n
    big, half = min(32, n // 2), min(16, n)
    split = big + 8
    first_x, last_x = gx == 0, gx == nx - 1
    first_y, last_y = gy == 0, gy == ny - 1

    barrier = pltpu.get_barrier_semaphore()

    def device(dx, dy):
        return (lax.rem(gx + (nx + dx), nx), lax.rem(gy + (ny + dy), ny))

    chip, core = lax.div(gy, 2), lax.rem(gy, 2)
    size1, size2 = nx * 2, ny // 2
    me1, me2 = gx * 2 + core, chip

    def peer1(k):
        other = lax.rem(me1 + k, size1)
        return (lax.div(other, 2), chip * 2 + lax.rem(other, 2))

    def peer2(k):
        return (gx, lax.rem(me2 + k, size2) * 2 + core)

    def farthest_first(size):
        return sorted(range(1, size), key=lambda k: abs(2 * k - size))

    loads = []
    plan = [
        (des_in, lambda h: des.at[h, PAD:end]),
        (v_in, lambda h: raw.at[0, h]),
        (g_in, lambda h: flg.at[2, h]),
        (t_in, lambda h: raw.at[1, h]),
        (d_in, lambda h: raw.at[2, h]),
        (c_in, lambda h: flg.at[3, h]),
        (e_in, lambda h: flg.at[0, h]),
        (s_in, lambda h: flg.at[1, h]),
        (q_in, lambda h: raw.at[3, h]),
        (o_in, lambda h: raw.at[4, h]),
    ]
    for i, (src, dst) in enumerate(plan):
        pair = []
        for h in range(2):
            c = pltpu.make_async_copy(
                src.at[:, :, pl.ds(128 * h, 128)], dst(h), in_sem.at[2 * i + h]
            )
            pair.append(c)
        loads.append(pair)

    def load(*which):
        for i in which:
            for c in loads[i]:
                c.start()

    load(0)

    def loaded(*which):
        for i in which:
            for c in loads[i]:
                c.wait()

    for k in range(max(size1, size2) - 1):
        for size, peer in ((size2, peer2), (size1, peer1)):
            if k < size - 1:
                pl.semaphore_signal(
                    barrier, inc=1, device_id=peer(farthest_first(size)[k]), device_id_type=MESH
                )
    for dx, dy in OFFSETS:
        pl.semaphore_signal(barrier, inc=1, device_id=device(dx, dy), device_id_type=MESH)
    load(1, 2)

    count = [0]

    def exists(dx, dy):
        x, y = gx + dx, gy + dy
        return (x >= 0) & (x < nx) & (y >= 0) & (y < ny)

    def send(src, dst, dx, dy):
        k = count[0]
        count[0] += 1
        c = pltpu.make_async_remote_copy(
            src_ref=src, dst_ref=dst, send_sem=send_sem.at[k], recv_sem=recv_sem.at[k],
            device_id=device(dx, dy), device_id_type=MESH,
        )

        @pl.when(exists(dx, dy))
        def _():
            c.start()

        return c, dx, dy

    def send_up(src, dst):
        return [
            send(src, dst.at[:, :, PAD:end], 0, 1),
            send(src.at[:, :, n - PAD : n], dst.at[:, :, 0:PAD], 1, 1),
            send(src.at[:, :, 0:PAD], dst.at[:, :, end : end + PAD], -1, 1),
        ]

    def send_down(src, dst, both=True):
        some = [
            send(src, dst.at[:, :, PAD:end], 0, -1),
            send(src.at[:, :, 0:PAD], dst.at[:, :, end : end + PAD], -1, -1),
        ]
        if both:
            some.append(send(src.at[:, :, n - PAD : n], dst.at[:, :, 0:PAD], 1, -1))
        return some

    def send_first(src, dst, dy):
        return [
            send(src.at[:, :, 0:split], dst.at[:, :, PAD : PAD + split], 0, dy),
            send(src.at[:, :, n - PAD : n], dst.at[:, :, 0:PAD], 1, dy),
        ]

    def send_second(src, dst, dy):
        return [
            send(src.at[:, :, split:n], dst.at[:, :, PAD + split : end], 0, dy),
            send(src.at[:, :, 0:PAD], dst.at[:, :, end : end + PAD], -1, dy),
        ]

    pending = []

    def arrived(copies):
        for c, dx, dy in copies:

            @pl.when(exists(-dx, -dy))
            def _(c=c):
                c.wait_recv()

        pending.extend(copies)

    def tails_up(ref, up):
        for h in range(2):
            a, b, c = (row_pack(ref, h, PAD, n, j) for j in (5, 6, 7))
            up[0, h] = a + 2.0 * b + 3.0 * c
            up[1, h] = b + 2.0 * c
            up[2, h] = c

    def tails_down(ref, down):
        for h in range(2):
            a, b, c = (row_pack(ref, h, PAD, n, j) for j in (0, 1, 2))
            down[0, h] = a
            down[1, h] = 2.0 * a + b
            down[2, h] = 3.0 * a + 2.0 * b + c

    loaded(0)
    load(3, 4, 5, 6, 7, 8, 9)
    tails_down(des, cdn)
    tails_up(des, cup)
    pl.semaphore_wait(barrier, len(OFFSETS) + size1 - 1 + size2 - 1)
    moving1 = send_first(cup, cc.at[0:3], 1) + send_first(cdn, cc.at[5:8], -1)
    moving1.append(send(des.at[:, end - 4 : end], des.at[:, PAD - 4 : PAD], 1, 0))
    moving2 = send_second(cup, cc.at[0:3], 1) + send_second(cdn, cc.at[5:8], -1)
    moving2.append(send(des.at[:, PAD : PAD + 3], des.at[:, end : end + 3], -1, 0))

    def mask(f, flag):
        def body(i, carry):
            x = i * 16
            free = flg[flag, :, pl.ds(x, 16)] == 0
            fld[f, :, pl.ds(PAD + x, 16)] = jnp.where(free, raw[f, :, pl.ds(x, 16)], 0.0)
            return carry

        lax.fori_loop(0, n // 16, body, 0)
        for h in range(2):
            fup[f, h] = row_pack(fld.at[f], h, PAD, n, 7)
            fdn[f, h] = row_pack(fld.at[f], h, PAD, n, 0)

    def send_fields(a, b):
        return (
            send_up(fup.at[a:b], flo.at[a:b])
            + send_down(fdn.at[a:b], fhi.at[a:b])
            + [
                send(fld.at[a:b, :, end - 1 : end], fld.at[a:b, :, PAD - 1 : PAD], 1, 0),
                send(fld.at[a:b, :, PAD : PAD + 1], fld.at[a:b, :, end : end + 1], -1, 0),
            ]
        )

    loaded(1, 2)
    mask(0, 2)
    volt_field_moving = send_fields(0, 1)
    loaded(6, 7)
    flags_moving = [send(flg.at[0:2, :, n - 1], flx, 1, 0)]
    zero_rows = jnp.zeros((2, 2, end + PAD, 128), F32)
    cc[3:5] = zero_rows
    scc[3:5] = zero_rows
    wi = lax.broadcasted_iota(jnp.int32, (256, 256), 0)
    wj = lax.broadcasted_iota(jnp.int32, (256, 256), 1)
    wz[...] = jnp.maximum(4 - jnp.abs(wi - wj), 0).astype(F32).astype(BF16)
    loaded(3, 4, 5)
    mask(1, 3)
    mask(2, 3)

    row = lax.broadcasted_iota(jnp.int32, (8, 128), 0)

    def filter_y(ref, p):
        for h in range(2):
            a = ref[h, p]
            out = 4.0 * a
            for k in (1, 2, 3):
                out += jnp.where(row < 8 - k, float(4 - k), 0.0) * pltpu.roll(a, 8 - k, axis=0)
                out += jnp.where(row >= k, float(4 - k), 0.0) * pltpu.roll(a, k, axis=0)
            yf[h, p] = out

    def filter_y_own(ref):
        def body(i, carry):
            for u in range(8):
                filter_y(ref, PAD + 8 * i + u)
            return carry

        lax.fori_loop(0, n // 8, body, 0)

    def filter_y_rest(ref, edge, outer, start, stop):
        for p in outer:
            filter_y(ref, p)

        def add(p):
            for h in range(2):
                yf[h, p] += edge_column(edge, h, p)

        for p in [*outer, *range(start, stop)]:
            add(p)

    def filter_y_first(ref, edge, low):
        filter_y_rest(ref, edge, range(PAD - low, PAD), PAD, PAD + split)

    def filter_y_second(ref, edge):
        filter_y_rest(ref, edge, range(end, end + 3), PAD + split, end)

    def filter_xz(p, planes):
        halves = []
        for h in range(2):
            a = yf[h, pl.ds(p - 3, planes + 6)]
            a = a[:-1] + a[1:]
            a = a[:-2] + a[2:]
            a = a[:-1] + a[1:]
            a = a[:-2] + a[2:]
            halves.append(a.reshape(planes * 8, 128))
        a = jnp.concatenate(halves, axis=1)
        high = a.astype(BF16)
        rest = a - high.astype(F32)
        mid = rest.astype(BF16)
        low = (rest - mid.astype(F32)).astype(BF16)
        w = wz[...]
        out = (
            jnp.dot(low, w, preferred_element_type=F32)
            + jnp.dot(mid, w, preferred_element_type=F32)
            + jnp.dot(high, w, preferred_element_type=F32)
        )
        return jnp.stack(
            [out[:, :128].reshape(planes, 8, 128), out[:, 128:].reshape(planes, 8, 128)]
        )

    def inverse_window(i, full):
        w = jnp.where(i == 0, 10, jnp.where(i == 1, 13, jnp.where(i == 2, 15, 16)))
        k = full - 1 - i
        return jnp.where(k == 0, w - 6, jnp.where(k == 1, w - 3, jnp.where(k == 2, w - 1, w)))

    shape = (2, 8, 128)
    yy = gy * 8 + lax.broadcasted_iota(jnp.int32, shape, 1)
    zz = lax.broadcasted_iota(jnp.int32, shape, 0) * 128 + lax.broadcasted_iota(jnp.int32, shape, 2)
    inv_yz = 1.0 / (inverse_window(yy, ny * 8) * inverse_window(zz, 256)).astype(F32)
    touch_yz = (jnp.where(yy == 0, 1, 2) * jnp.where(zz == 0, 1, 2)).astype(F32)

    def inv_x(p):
        i = gx * n + (p - PAD)
        full = nx * n
        r = jnp.where(i == 0, 1 / 10.0, jnp.where(i == 1, 1 / 13.0, jnp.where(i == 2, 1 / 15.0, 1 / 16.0)))
        k = full - 1 - i
        return jnp.where(
            k == 0, 1 / 10.0, jnp.where(k == 1, 1 / 13.0, jnp.where(k == 2, 1 / 15.0, r))
        ).astype(F32)

    filter_y_own(des)

    def clear(edge, field, low, high):
        @pl.when(first_x)
        def _():
            if low:
                field[:, PAD - low : PAD] = jnp.zeros((2, low, 8, 128), F32)
            edge[:, :, 0:PAD] = jnp.zeros((8, 2, PAD, 128), F32)

        @pl.when(last_x)
        def _():
            field[:, end : end + high] = jnp.zeros((2, high, 8, 128), F32)
            edge[:, :, end : end + PAD] = jnp.zeros((8, 2, PAD, 128), F32)

        @pl.when(first_y)
        def _():
            edge[0:3] = jnp.zeros((3, 2, end + PAD, 128), F32)

        @pl.when(last_y)
        def _():
            edge[5:8] = jnp.zeros((3, 2, end + PAD, 128), F32)

    clear(cc, des, 4, 3)
    clear(scc, sen, 3, 3)
    arrived(moving1)
    heat_fields_moving = send_fields(1, 3)
    filter_y_first(des, cc, 4)
    there_x = jnp.where(first_x, 0.0, 1.0).astype(F32)
    there_y = jnp.where(first_y, 0.0, 1.0).astype(F32)

    def density(smoothed, p, e, s):
        solid = smoothed * inv_yz * inv_x(p)
        return jnp.where(e == 1, 0.0, jnp.where(s == 1, 1.0, solid))

    def density_body(i, acc):
        p = PAD + big * i
        smoothed = filter_xz(p, big)
        for u in range(big):
            x = big * i + u
            rho = density(smoothed[:, u], p + u, flg[0, :, x], flg[1, :, x])
            squared = rho * rho
            held = (flg[0, :, x] + flg[1, :, x]) == 0
            coef[:, x] = jnp.where(held, (3.0 * squared) * inv_yz * inv_x(p + u), 0.0)
            cub[:, p + u] = squared * rho
            acc = acc + rho
        return acc

    occupied = density_body(0, jnp.zeros(shape, F32))
    arrived(flags_moving)
    before = density(filter_xz(PAD - 2, 2)[:, 1], PAD - 1, flx[0], flx[1])
    cub[:, PAD - 1] = there_x * (before * before * before)
    arrived(moving2)
    filter_y_second(des, cc)
    occupied = lax.fori_loop(1, n // big, density_body, occupied)

    for h in range(2):
        cubs[0, h] = row_pack(cub, h, 0, end, 7)
    cube_moving = [send(cubs, cube.at[:, :, 0:end], 0, 1)]

    def gather_body(i, last):
        for u in range(8):
            now = spread(cub[:, PAD + 8 * i + u])
            ca[:, 8 * i + u] = now + last
            last = now
        return last

    lax.fori_loop(0, n // 8, gather_body, spread(cub[:, PAD - 1]))

    def clear_fields(a, b):
        @pl.when(first_x)
        def _():
            fld[a:b, :, PAD - 1] = jnp.zeros((b - a, 2, 8, 128), F32)
            flo[a:b, :, 0:PAD] = jnp.zeros((b - a, 2, PAD, 128), F32)
            fhi[a:b, :, 0:PAD] = jnp.zeros((b - a, 2, PAD, 128), F32)

        @pl.when(last_x)
        def _():
            fld[a:b, :, end] = jnp.zeros((b - a, 2, 8, 128), F32)
            flo[a:b, :, end : end + PAD] = jnp.zeros((b - a, 2, PAD, 128), F32)
            fhi[a:b, :, end : end + PAD] = jnp.zeros((b - a, 2, PAD, 128), F32)

        @pl.when(first_y)
        def _():
            flo[a:b] = jnp.zeros((b - a, 2, end + PAD, 128), F32)

        @pl.when(last_y)
        def _():
            fhi[a:b] = jnp.zeros((b - a, 2, end + PAD, 128), F32)

    arrived(volt_field_moving)
    clear_fields(0, 1)

    def far_rows(k, edge):
        s, d = z_forward(edge)
        zrow[k, 0] = s
        zrow[k, 1] = d

    def forward_of(field, k):
        def forward(p):
            return yz_forward(
                field[:, p], zrow[k, 0, :, pl.ds(p, 1)], zrow[k, 1, :, pl.ds(p, 1)]
            )

        return forward

    far_rows(0, fhi[0])
    weights = ((0.001, 0.999), (0.05, 0.95), (0.05, 0.95))

    def apply_main(which, base, slope, step):
        forwards = [forward_of(fld.at[f], f) for f in which]

        def element(a, b, w):
            return x_backward(*weigh(*x_forward(a, b), w))

        start = []
        w = there_x * base + slope * cub[:, PAD - 1]
        for forward in forwards:
            a, b = forward(PAD - 1), forward(PAD)
            start.append((tuple(b), tuple(element(a, b, w)[1])))

        def body(i, carry):
            carry = list(carry)
            for u in range(step):
                x = step * i + u
                w = base + slope * cub[:, PAD + x]
                for k, f in enumerate(which):
                    a, behind = carry[k]
                    b = forwards[k](PAD + x + 1)
                    front, new = element(a, b, w)
                    kap[f, :, x] = yz_backward([front[c] + behind[c] for c in range(4)])
                    carry[k] = tuple(b), tuple(new)
            return tuple(carry)

        lax.fori_loop(0, n // step, body, tuple(start))

    def edge_weight(base, slope):
        where = lax.broadcasted_iota(jnp.int32, (2, end + PAD, 128), 1)
        real = jnp.where(where == PAD - 1, there_x, 1.0) * there_y
        return base * real + (slope * there_y) * cube[0]

    def whole_row(ref, j):
        return jnp.stack([row_pack(ref, h, 0, end + PAD, j) for h in range(2)])

    def rows_x_forward(a):
        return x_forward(a, [planes_after(c) for c in a])

    def edge_forward(f):
        return rows_x_forward(rows_forward(flo[f], whole_row(fld.at[f], 0)))

    def apply_edge(f, parts):
        front, behind = x_backward(*weigh(*parts, edge_weight(*weights[f])))
        m = [front[c] + planes_before(behind[c]) for c in range(4)]
        ns, nd = m[0] + m[2], m[1] + m[3]
        out = (ns - nd) + z_prev(ns + nd)
        for h in range(2):
            row_add(kap.at[f], h, 0, n, 0, out[h, PAD:end])

    apply_main((0,), *weights[0], big)

    volt_parts = edge_forward(0)
    arrived(cube_moving)

    @pl.when(first_y)
    def _():
        cube[0] = jnp.zeros((2, end + PAD, 128), F32)

    apply_edge(0, volt_parts)
    edge_cube = cube[0] * there_y
    edge_cube = edge_cube + planes_before(edge_cube)
    edge_cube = edge_cube + z_prev(edge_cube)
    for h in range(2):
        row_add(ca, h, 0, n, 0, edge_cube[h, PAD:end])

    def pivot(x, base, slope):
        cx = jnp.where(gx * n + x == 0, 1.0, 2.0).astype(F32)
        return base * (cx * touch_yz) + slope * ca[:, x]

    loaded(8, 9)

    def volt_body(i, carry):
        for u in range(8):
            x = 8 * i + u
            v = raw[0, :, x]
            moved = 1.8 * (raw[3, :, x] - kap[0, :, x]) / pivot(x, 0.001, 0.999)
            v1[:, PAD + x] = v + jnp.where(flg[2, :, x] == 0, moved, -0.6 * v)
        return carry

    lax.fori_loop(0, n // 8, volt_body, 0)
    for h in range(2):
        v1up[0, h] = row_pack(v1, h, PAD, n, 7)
        v1dn[0, h] = row_pack(v1, h, PAD, n, 0)
    volt_moving = send_up(v1up, v1lo) + send_down(v1dn, v1hi)
    volt_moving += [
        send(v1.at[:, end - 1 : end], v1.at[:, PAD - 1 : PAD], 1, 0),
        send(v1.at[:, PAD : PAD + 1], v1.at[:, end : end + 1], -1, 0),
    ]
    stores = []

    def store(src, dst):
        for h in range(2):
            c = pltpu.make_async_copy(
                src(h), dst.at[:, :, pl.ds(128 * h, 128)], out_sem.at[len(stores)]
            )
            c.start()
            stores.append(c)

    store(lambda h: v1.at[h, PAD:end], v_out)

    arrived(heat_fields_moving)
    clear_fields(1, 3)
    far_rows(1, fhi[1])
    far_rows(2, fhi[2])
    apply_main((1, 2), *weights[1], half)
    apply_edge(1, edge_forward(1))
    apply_edge(2, edge_forward(2))

    def heat_body(i, carry):
        for u in range(8):
            x = 8 * i + u
            free = flg[3, :, x] == 0
            step = 1.8 / pivot(x, 0.05, 0.95)
            d = raw[2, :, x]
            d1[:, PAD + x] = d + jnp.where(free, step * (raw[4, :, x] - kap[2, :, x]), -0.6 * d)
            t = raw[1, :, x]
            t0[:, x] = t - jnp.where(free, step * kap[1, :, x], 0.6 * t)
            tr[:, x] = jnp.where(free, step, 0.0)
        return carry

    lax.fori_loop(0, n // 8, heat_body, 0)
    for h in range(2):
        d1dn[0, h] = row_pack(d1, h, PAD, n, 0)
    dual_moving = send_down(d1dn, d1hi, both=False)
    dual_moving.append(send(d1.at[:, PAD : PAD + 1], d1.at[:, end : end + 1], -1, 0))
    store(lambda h: d1.at[h, PAD:end], d_out)

    arrived(volt_moving)

    def clear_high(field, *edges):
        @pl.when(last_x)
        def _():
            field[:, end] = jnp.zeros((2, 8, 128), F32)
            for edge in edges:
                edge[0, :, end : end + PAD] = jnp.zeros((2, PAD, 128), F32)

        @pl.when(last_y)
        def _():
            edges[0][0] = jnp.zeros((2, end + PAD, 128), F32)

    clear_high(v1, v1hi, v1lo)

    @pl.when(first_x)
    def _():
        v1[:, PAD - 1] = jnp.zeros((2, 8, 128), F32)
        v1hi[0, :, 0:PAD] = jnp.zeros((2, PAD, 128), F32)
        v1lo[0, :, 0:PAD] = jnp.zeros((2, PAD, 128), F32)

    @pl.when(first_y)
    def _():
        v1lo[0] = jnp.zeros((2, end + PAD, 128), F32)


    far_rows(3, v1hi[0])
    volt_forward = forward_of(v1, 3)
    def row_energy(near, far):
        s, d = rows_x_forward(rows_forward(near, far))
        return energy(s, d, s, d)

    def row_gather(e):
        e = e + planes_before(e)
        return (e + z_prev(e))[:, PAD:end]

    row0 = whole_row(v1, 0)
    extra = row_gather(row_energy(v1lo[0], row0) * (edge_weight(0.001, 0.999) * 0.125))
    where = lax.broadcasted_iota(jnp.int32, (2, end + PAD, 128), 1)
    own_weight = 0.001 * jnp.where(where == PAD - 1, there_x, 1.0) + 0.999 * whole_row(cub, 0)
    heat0 = extra + row_gather(row_energy(row0, whole_row(v1, 1)) * (own_weight * 0.125))
    for h in range(2):
        t1dn[0, h] = row_pack(t0, h, 0, n, 0) + row_pack(tr, h, 0, n, 0) * heat0[h]
    temp_moving = send_down(t1dn, t1hi, both=False)

    a = volt_forward(PAD - 1)
    b = volt_forward(PAD)
    s, d = x_forward(a, b)
    lead = energy(s, d, s, d) * ((there_x * 0.001 + 0.999 * cub[:, PAD - 1]) / 8.0)

    def joule_body(i, carry):
        a, last, acc = carry
        for u in range(big):
            x = big * i + u
            b = volt_forward(PAD + x + 1)
            s, d = x_forward(a, b)
            e = energy(s, d, s, d)
            joule[:, x] = e
            now = spread(e * (0.001 / 8.0 + (0.999 / 8.0) * cub[:, PAD + x]))
            t = t0[:, x] + tr[:, x] * (now + last)
            t1[:, PAD + x] = t
            acc = acc + raw[4, :, x] * t
            a, last = b, now
        return tuple(a), last, acc

    carry = joule_body(0, (tuple(b), spread(lead), jnp.zeros(shape, F32)))
    for h in range(2):
        t1[h, PAD, 0:1] += extra[h, 0:1] * tr[h, 0, 0:1]
    temp_moving.append(send(t1.at[:, PAD : PAD + 1], t1.at[:, end : end + 1], -1, 0))
    _, _, warm = lax.fori_loop(1, n // big, joule_body, carry)

    warm_rows = jnp.zeros((8, 128), F32)
    for h in range(2):
        more = extra[h] * row_pack(tr, h, 0, n, 0)
        row_add(t1, h, PAD + 1, n - 1, 0, more[1:])
        warm_rows = warm_rows + jnp.sum(
            (more * row_pack(raw.at[4], h, 0, n, 0)).reshape(n // 8, 8, 128), axis=0
        )
    store(lambda h: t1.at[h, PAD:end], t_out)

    arrived(dual_moving)
    clear_high(d1, d1hi)
    far_rows(4, d1hi[0])
    dual_forward = forward_of(d1, 4)
    none = jnp.zeros((2, 1, 128), F32)

    def pair_forward(p):
        return tuple(yz_forward(t1[:, p], none, none)), tuple(dual_forward(p))

    def sens_body(i, carry):
        ta, da = carry
        for u in range(half):
            x = half * i + u
            tb, db = pair_forward(PAD + x + 1)
            ts, td = x_forward(ta, tb)
            ds, dd = x_forward(da, db)
            mean = (0.999 / 8.0) * (da[0] + db[0])
            value = joule[:, x] * mean - 0.95 * energy(ts, td, ds, dd)
            sen[:, PAD + x] = coef[:, x] * value
            ta, da = tb, db
        return ta, da

    carry = lax.fori_loop(0, n // half - 1, sens_body, pair_forward(PAD))
    dual_s, dual_d = rows_x_forward(rows_forward(whole_row(d1, 7), d1hi[0]))
    arrived(temp_moving)
    clear_high(t1, t1hi)
    sens_body(n // half - 1, carry)
    tails_down(sen, sdn)
    sens1 = send_first(sdn, scc.at[5:8], -1)
    sens2 = send_second(sdn, scc.at[5:8], -1)
    behind_s, behind_d = z_forward(t1hi[0])
    temp_s, temp_d = rows_x_forward((behind_s, behind_d, behind_s, behind_d))
    work = 0.95 * energy(temp_s, temp_d, dual_s, dual_d)
    for h in range(2):
        row_add(sen, h, PAD, n, 7, -work[h, PAD:end] * row_pack(coef, h, 0, n, 7))
    tails_up(sen, sup)
    sens1 += send_first(sup, scc.at[0:3], 1)
    sens1.append(send(sen.at[:, end - 3 : end], sen.at[:, PAD - 3 : PAD], 1, 0))
    sens2 += send_second(sup, scc.at[0:3], 1)
    sens2.append(send(sen.at[:, PAD : PAD + 3], sen.at[:, end : end + 3], -1, 0))
    filter_y_own(sen)

    def whole(a):
        return jnp.sum(jnp.sum(a, axis=0, keepdims=True), axis=1, keepdims=True)

    occupied_sum = whole(occupied[0] + occupied[1])
    warm_sum = whole(warm[0] + warm[1] + warm_rows)
    arrived(sens1)
    filter_y_first(sen, scc, 3)

    def last_body(i, acc):
        out = filter_xz(PAD + big * i, big)
        fil[:, pl.ds(big * i, big)] = out
        return acc + jnp.sum(out * out, axis=1)

    square = last_body(0, jnp.zeros(shape, F32))
    arrived(sens2)
    filter_y_second(sen, scc)
    square = lax.fori_loop(1, n // big, last_body, square)
    store(lambda h: fil.at[h], f_out)

    lane = lax.broadcasted_iota(jnp.int32, (1, 128), 1)
    message = jnp.where(
        lane == 0,
        whole(square[0] + square[1]),
        jnp.where(lane == 1, occupied_sum, warm_sum),
    )

    def exchange(value, slots, me, size, peer, sends, recvs):
        slots[me, 0:1] = value
        for k in farthest_first(size):
            pltpu.make_async_remote_copy(
                src_ref=slots.at[me, pl.ds(0, 1)], dst_ref=slots.at[me, pl.ds(0, 1)],
                send_sem=sends.at[0], recv_sem=recvs.at[0],
                device_id=peer(k), device_id_type=MESH,
            ).start()
        others = slots.at[pl.ds(0, size - 1), pl.ds(0, 1)]
        every = pltpu.make_async_remote_copy(
            src_ref=others, dst_ref=others, send_sem=sends.at[0], recv_sem=recvs.at[0],
            device_id=peer(1), device_id_type=MESH,
        )
        every.wait_recv()
        pending.append((every, 0, 0))
        parts = [slots[k, 0:1] for k in range(size)]
        while len(parts) > 1:
            parts = [a + b for a, b in zip(parts[::2], parts[1::2])]
        return parts[0]

    message = exchange(message, slots1, me1, size1, peer1, r1_send, r1_recv)
    message = exchange(message, slots2, me2, size2, peer2, r2_send, r2_recv)
    sums_out[...] = jnp.broadcast_to(message, (8, 128))
    for c, dx, dy in pending:

        @pl.when(exists(dx, dy))
        def _(c=c):
            c.wait_send()

    for c in stores:
        c.wait()


def finish(
    total, v, t, d, f, sums_ref, v_out, t_out, d_out, f_out, occ_out, mean_out, buf, sem
):
    copies = [
        pltpu.make_async_copy(src, dst, sem.at[i])
        for i, (src, dst) in enumerate(((v, v_out), (t, t_out), (d, d_out)))
    ]
    for c in copies:
        c.start()
    sums = sums_ref[0:1] * (1.0 / total)
    scale = jnp.broadcast_to(1.0 / jnp.sqrt(sums[:, 0:1] + 1e-6), (8, 256))
    parts = 4
    step = buf.shape[0] // parts
    for i in range(parts):
        part = pl.ds(step * i, step)
        buf[part] = f[part] * scale
        c = pltpu.make_async_copy(buf.at[part], f_out.at[part], sem.at[3 + i])
        c.start()
        copies.append(c)
    occ_out[0] = sums[0, 1]
    mean_out[0] = sums[0, 2]
    for c in copies:
        c.wait()


def per_device(nx, ny, *args):
    n = args[0].shape[0]
    assert args[0].shape[1:] == (8, 256) and n % 8 == 0
    field = jax.ShapeDtypeStruct(args[0].shape, F32)
    tile = jax.ShapeDtypeStruct((8, 128), F32)
    wide = n + 2 * PAD

    def vm(*shape, dtype=F32):
        return pltpu.VMEM(shape, dtype)

    planes = vm(2, wide, 8, 128)
    own = vm(2, n, 8, 128)
    edge = vm(1, 2, wide, 128)
    edge_out = vm(1, 2, n, 128)
    scratch = [
        planes, vm(5, 2, n, 8, 128), vm(4, 2, n, 8, 128, dtype=jnp.int32),
        vm(3, 2, wide, 8, 128), vm(2, 2, 8, 128, dtype=jnp.int32),
        vm(5, 2, 2, wide, 128), own,
        vm(8, 2, wide, 128), vm(3, 2, n, 128), vm(3, 2, n, 128),
        vm(3, 2, wide, 128), vm(3, 2, wide, 128), vm(3, 2, n, 128), vm(3, 2, n, 128),
        vm(256, 256, dtype=BF16), planes, planes,
        edge, vm(1, 2, PAD + n, 128), own,
        vm(3, 2, n, 8, 128), planes, edge, edge, edge_out, edge_out,
        planes, edge, edge_out, own, own, planes, edge, edge_out, own,
        planes, vm(8, 2, wide, 128), vm(3, 2, n, 128), vm(3, 2, n, 128), own,
        vm(nx * 2, 8, 128), vm(ny // 2, 8, 128),
        pltpu.SemaphoreType.DMA((20,)), pltpu.SemaphoreType.DMA((8,)),
        pltpu.SemaphoreType.DMA((64,)), pltpu.SemaphoreType.DMA((64,)),
        pltpu.SemaphoreType.DMA((1,)), pltpu.SemaphoreType.DMA((1,)),
        pltpu.SemaphoreType.DMA((1,)), pltpu.SemaphoreType.DMA((1,)),
    ]
    anywhere = pl.BlockSpec(memory_space=pl.ANY)
    hbm = pl.BlockSpec(memory_space=pltpu.HBM)
    vmem = pl.BlockSpec(memory_space=pltpu.VMEM)
    smem = pl.BlockSpec(memory_space=pltpu.SMEM)
    *fields, sums = pl.pallas_call(
        functools.partial(kernel, nx, ny, n),
        out_shape=(field, field, field, field, tile),
        in_specs=[hbm] * 10,
        out_specs=(anywhere,) * 4 + (vmem,),
        scratch_shapes=scratch,
        compiler_params=pltpu.CompilerParams(
            collective_id=0, has_side_effects=True, vmem_limit_bytes=103 * 512 * 1024
        ),
    )(*args)
    one = jax.ShapeDtypeStruct((1,), F32)
    *outs, occupied, mean = pl.pallas_call(
        functools.partial(finish, float(nx * ny * n * 8 * 256)),
        out_shape=(field, field, field, field, one, one),
        in_specs=[anywhere] * 3 + [vmem, vmem],
        out_specs=(hbm,) * 4 + (smem, smem),
        scratch_shapes=[vm(n, 8, 256), pltpu.SemaphoreType.DMA((8,))],
        compiler_params=pltpu.CompilerParams(vmem_limit_bytes=8 * 1024 * 1024),
    )(*fields, sums)
    return (*outs, occupied.reshape(()), mean.reshape(()))


def solution(mesh):
    spec = P("gx", "gy", None)
    return jax.shard_map(
        functools.partial(per_device, mesh.shape["gx"], mesh.shape["gy"]),
        mesh=mesh,
        in_specs=(spec,) * 10,
        out_specs=(spec,) * 4 + (P(), P()),
        check_vma=False,
    )
```

```python
import functools

import jax
import jax.numpy as jnp
from jax import lax
from jax.experimental import pallas as pl
from jax.experimental.pallas import tpu as pltpu
from jax.sharding import PartitionSpec as P

MESH = pl.DeviceIdType.MESH
F32 = jnp.float32
BF16 = jnp.bfloat16
PAD = 8
OFFSETS = ((0, 1), (0, -1), (1, 1), (-1, 1), (1, -1), (-1, -1), (1, 0), (-1, 0))


def lanes(shape):
    return lax.broadcasted_iota(jnp.int32, shape, len(shape) - 1)


def z_next(p):
    r = pltpu.roll(p, 127, axis=p.ndim - 1)
    lane = lanes(p.shape[1:])
    low = jnp.where(lane < 127, r[0], r[1])
    high = jnp.where(lane < 127, r[1], 0.0)
    return jnp.stack([low, high])


def z_prev(p):
    r = pltpu.roll(p, 1, axis=p.ndim - 1)
    lane = lanes(p.shape[1:])
    low = jnp.where(lane > 0, r[0], 0.0)
    high = jnp.where(lane > 0, r[1], r[0])
    return jnp.stack([low, high])


def rows_of(shape):
    return lax.broadcasted_iota(jnp.int32, shape, len(shape) - 2)


def y_next(p, row):
    r = pltpu.roll(p, 7, axis=1)
    return jnp.where(rows_of(p.shape) < 7, r, jnp.broadcast_to(row, p.shape))


def y_prev(p):
    r = pltpu.roll(p, 1, axis=1)
    return jnp.where(rows_of(p.shape) > 0, r, 0.0)


def z_forward(p):
    q = z_next(p)
    return p + q, q - p


def yz_forward(p, row_s, row_d):
    s, d = z_forward(p)
    sy, dy = y_next(s, row_s), y_next(d, row_d)
    return s + sy, d + dy, sy - s, dy - d


def rows_forward(near, far):
    (s, d), (sy, dy) = z_forward(near), z_forward(far)
    return s + sy, d + dy, sy - s, dy - d


def planes_after(p):
    return pltpu.roll(p, p.shape[1] - 1, axis=1)


def planes_before(p):
    return pltpu.roll(p, 1, axis=1)


def x_forward(a, b):
    return [a[i] + b[i] for i in range(1, 4)], [b[i] - a[i] for i in range(4)]


def weigh(sums, diffs, w):
    w1, w2, w3 = w * (1.0 / 48.0), w * (1.0 / 24.0), w * (1.0 / 16.0)
    return (
        [w3 * sums[0], w3 * sums[1], w2 * sums[2]],
        [w3 * diffs[0], w2 * diffs[1], w2 * diffs[2], w1 * diffs[3]],
    )


def x_backward(sums, diffs):
    front = [-diffs[0]] + [sums[i] - diffs[i + 1] for i in range(3)]
    behind = [diffs[0]] + [sums[i] + diffs[i + 1] for i in range(3)]
    return front, behind


def yz_backward(n):
    ns = (n[0] - n[2]) + y_prev(n[0] + n[2])
    nd = (n[1] - n[3]) + y_prev(n[1] + n[3])
    return (ns - nd) + z_prev(ns + nd)


def energy(sa, da, sb, db):
    three = da[0] * db[0] + sa[0] * sb[0] + sa[1] * sb[1]
    two = da[1] * db[1] + da[2] * db[2] + sa[2] * sb[2]
    return (1.0 / 16.0) * three + (1.0 / 24.0) * two + (1.0 / 48.0) * (da[3] * db[3])


def spread(p):
    t = p + y_prev(p)
    return t + z_prev(t)


def row_pack(ref, h, first, planes, row):
    every = ref.shape[1]
    flat = ref.reshape(2 * every * 8, 128)
    return flat[pl.ds((h * every + first) * 8 + row, planes, stride=8), :]


def row_add(ref, h, first, planes, row, value):
    every = ref.shape[1]
    flat = ref.reshape(2 * every * 8, 128)
    where = pl.ds((h * every + first) * 8 + row, planes, stride=8)
    flat[where, :] = flat[where, :] + value


def edge_column(edge, h, p):
    every = edge.shape[2]
    flat = edge.reshape(8 * 2 * every, 128)
    return flat[pl.ds(h * every + p, 8, stride=2 * every), :]


def kernel(
    nx, ny, n,
    des_in, v_in, t_in, d_in, q_in, o_in, e_in, s_in, g_in, c_in,
    v_out, t_out, d_out, f_out, sums_out,
    des, raw, flg, fld, flx, zrow, coef,
    cc, cup, cdn, flo, fhi, fup, fdn,
    wz, yf, cub, cube, cubs, ca,
    kap, v1, v1lo, v1hi, v1up, v1dn,
    d1, d1hi, d1dn, t0, tr, t1, t1hi, t1dn, joule,
    sen, scc, sup, sdn, fil, slots1, slots2,
    in_sem, out_sem, send_sem, recv_sem, r1_send, r1_recv, r2_send, r2_recv,
):
    gx, gy = lax.axis_index("gx"), lax.axis_index("gy")
    total = float(nx * n * ny * 8 * 256)
    end = PAD + n
    big, half = min(32, n // 2), min(16, n)
    split = big + 8
    first_x, last_x = gx == 0, gx == nx - 1
    first_y, last_y = gy == 0, gy == ny - 1

    barrier = pltpu.get_barrier_semaphore()

    def device(dx, dy):
        return (lax.rem(gx + (nx + dx), nx), lax.rem(gy + (ny + dy), ny))

    chip, core = lax.div(gy, 2), lax.rem(gy, 2)
    size1, size2 = nx * 2, ny // 2
    me1, me2 = gx * 2 + core, chip

    def peer1(k):
        other = lax.rem(me1 + k, size1)
        return (lax.div(other, 2), chip * 2 + lax.rem(other, 2))

    def peer2(k):
        return (gx, lax.rem(me2 + k, size2) * 2 + core)

    def farthest_first(size):
        return sorted(range(1, size), key=lambda k: abs(2 * k - size))

    loads = []
    plan = [
        (des_in, lambda h: des.at[h, PAD:end]),
        (v_in, lambda h: raw.at[0, h]),
        (g_in, lambda h: flg.at[2, h]),
        (t_in, lambda h: raw.at[1, h]),
        (d_in, lambda h: raw.at[2, h]),
        (c_in, lambda h: flg.at[3, h]),
        (e_in, lambda h: flg.at[0, h]),
        (s_in, lambda h: flg.at[1, h]),
        (q_in, lambda h: raw.at[3, h]),
        (o_in, lambda h: raw.at[4, h]),
    ]
    for i, (src, dst) in enumerate(plan):
        pair = []
        for h in range(2):
            c = pltpu.make_async_copy(
                src.at[:, :, pl.ds(128 * h, 128)], dst(h), in_sem.at[2 * i + h]
            )
            pair.append(c)
        loads.append(pair)

    def load(*which):
        for i in which:
            for c in loads[i]:
                c.start()

    load(0)

    def loaded(*which):
        for i in which:
            for c in loads[i]:
                c.wait()

    for k in range(max(size1, size2) - 1):
        for size, peer in ((size2, peer2), (size1, peer1)):
            if k < size - 1:
                pl.semaphore_signal(
                    barrier, inc=1, device_id=peer(farthest_first(size)[k]), device_id_type=MESH
                )
    for dx, dy in OFFSETS:
        pl.semaphore_signal(barrier, inc=1, device_id=device(dx, dy), device_id_type=MESH)
    load(1, 2)

    count = [0]

    def exists(dx, dy):
        x, y = gx + dx, gy + dy
        return (x >= 0) & (x < nx) & (y >= 0) & (y < ny)

    def send(src, dst, dx, dy):
        k = count[0]
        count[0] += 1
        c = pltpu.make_async_remote_copy(
            src_ref=src, dst_ref=dst, send_sem=send_sem.at[k], recv_sem=recv_sem.at[k],
            device_id=device(dx, dy), device_id_type=MESH,
        )

        @pl.when(exists(dx, dy))
        def _():
            c.start()

        return c, dx, dy

    def send_up(src, dst):
        return [
            send(src, dst.at[:, :, PAD:end], 0, 1),
            send(src.at[:, :, n - PAD : n], dst.at[:, :, 0:PAD], 1, 1),
            send(src.at[:, :, 0:PAD], dst.at[:, :, end : end + PAD], -1, 1),
        ]

    def send_down(src, dst, both=True):
        some = [
            send(src, dst.at[:, :, PAD:end], 0, -1),
            send(src.at[:, :, 0:PAD], dst.at[:, :, end : end + PAD], -1, -1),
        ]
        if both:
            some.append(send(src.at[:, :, n - PAD : n], dst.at[:, :, 0:PAD], 1, -1))
        return some

    def send_first(src, dst, dy):
        return [
            send(src.at[:, :, 0:split], dst.at[:, :, PAD : PAD + split], 0, dy),
            send(src.at[:, :, n - PAD : n], dst.at[:, :, 0:PAD], 1, dy),
        ]

    def send_second(src, dst, dy):
        return [
            send(src.at[:, :, split:n], dst.at[:, :, PAD + split : end], 0, dy),
            send(src.at[:, :, 0:PAD], dst.at[:, :, end : end + PAD], -1, dy),
        ]

    pending = []

    def arrived(copies):
        for c, dx, dy in copies:

            @pl.when(exists(-dx, -dy))
            def _(c=c):
                c.wait_recv()

        pending.extend(copies)

    def tails_up(ref, up):
        for h in range(2):
            a, b, c = (row_pack(ref, h, PAD, n, j) for j in (5, 6, 7))
            up[0, h] = a + 2.0 * b + 3.0 * c
            up[1, h] = b + 2.0 * c
            up[2, h] = c

    def tails_down(ref, down):
        for h in range(2):
            a, b, c = (row_pack(ref, h, PAD, n, j) for j in (0, 1, 2))
            down[0, h] = a
            down[1, h] = 2.0 * a + b
            down[2, h] = 3.0 * a + 2.0 * b + c

    loaded(0)
    load(3, 4, 5, 6, 7, 8, 9)
    tails_down(des, cdn)
    tails_up(des, cup)
    pl.semaphore_wait(barrier, len(OFFSETS) + size1 - 1 + size2 - 1)
    moving1 = send_first(cup, cc.at[0:3], 1) + send_first(cdn, cc.at[5:8], -1)
    moving1.append(send(des.at[:, end - 4 : end], des.at[:, PAD - 4 : PAD], 1, 0))
    moving2 = send_second(cup, cc.at[0:3], 1) + send_second(cdn, cc.at[5:8], -1)
    moving2.append(send(des.at[:, PAD : PAD + 3], des.at[:, end : end + 3], -1, 0))

    def mask(f, flag):
        def body(i, carry):
            x = i * 16
            free = flg[flag, :, pl.ds(x, 16)] == 0
            fld[f, :, pl.ds(PAD + x, 16)] = jnp.where(free, raw[f, :, pl.ds(x, 16)], 0.0)
            return carry

        lax.fori_loop(0, n // 16, body, 0)
        for h in range(2):
            fup[f, h] = row_pack(fld.at[f], h, PAD, n, 7)
            fdn[f, h] = row_pack(fld.at[f], h, PAD, n, 0)

    def send_fields(a, b):
        return (
            send_up(fup.at[a:b], flo.at[a:b])
            + send_down(fdn.at[a:b], fhi.at[a:b])
            + [
                send(fld.at[a:b, :, end - 1 : end], fld.at[a:b, :, PAD - 1 : PAD], 1, 0),
                send(fld.at[a:b, :, PAD : PAD + 1], fld.at[a:b, :, end : end + 1], -1, 0),
            ]
        )

    loaded(1, 2)
    mask(0, 2)
    volt_field_moving = send_fields(0, 1)
    loaded(6, 7)
    flags_moving = [send(flg.at[0:2, :, n - 1], flx, 1, 0)]
    zero_rows = jnp.zeros((2, 2, end + PAD, 128), F32)
    cc[3:5] = zero_rows
    scc[3:5] = zero_rows
    wi = lax.broadcasted_iota(jnp.int32, (256, 256), 0)
    wj = lax.broadcasted_iota(jnp.int32, (256, 256), 1)
    wz[...] = jnp.maximum(4 - jnp.abs(wi - wj), 0).astype(F32).astype(BF16)
    loaded(3, 4, 5)
    mask(1, 3)
    mask(2, 3)

    row = lax.broadcasted_iota(jnp.int32, (8, 128), 0)

    def filter_y(ref, p):
        for h in range(2):
            a = ref[h, p]
            out = 4.0 * a
            for k in (1, 2, 3):
                out += jnp.where(row < 8 - k, float(4 - k), 0.0) * pltpu.roll(a, 8 - k, axis=0)
                out += jnp.where(row >= k, float(4 - k), 0.0) * pltpu.roll(a, k, axis=0)
            yf[h, p] = out

    def filter_y_own(ref):
        def body(i, carry):
            for u in range(8):
                filter_y(ref, PAD + 8 * i + u)
            return carry

        lax.fori_loop(0, n // 8, body, 0)

    def filter_y_rest(ref, edge, outer, start, stop):
        for p in outer:
            filter_y(ref, p)

        def add(p):
            for h in range(2):
                yf[h, p] += edge_column(edge, h, p)

        for p in [*outer, *range(start, stop)]:
            add(p)

    def filter_y_first(ref, edge, low):
        filter_y_rest(ref, edge, range(PAD - low, PAD), PAD, PAD + split)

    def filter_y_second(ref, edge):
        filter_y_rest(ref, edge, range(end, end + 3), PAD + split, end)

    def filter_xz(p, planes):
        halves = []
        for h in range(2):
            a = yf[h, pl.ds(p - 3, planes + 6)]
            a = a[:-1] + a[1:]
            a = a[:-2] + a[2:]
            a = a[:-1] + a[1:]
            a = a[:-2] + a[2:]
            halves.append(a.reshape(planes * 8, 128))
        a = jnp.concatenate(halves, axis=1)
        high = a.astype(BF16)
        rest = a - high.astype(F32)
        mid = rest.astype(BF16)
        low = (rest - mid.astype(F32)).astype(BF16)
        w = wz[...]
        out = (
            jnp.dot(low, w, preferred_element_type=F32)
            + jnp.dot(mid, w, preferred_element_type=F32)
            + jnp.dot(high, w, preferred_element_type=F32)
        )
        return jnp.stack(
            [out[:, :128].reshape(planes, 8, 128), out[:, 128:].reshape(planes, 8, 128)]
        )

    def inverse_window(i, full):
        w = jnp.where(i == 0, 10, jnp.where(i == 1, 13, jnp.where(i == 2, 15, 16)))
        k = full - 1 - i
        return jnp.where(k == 0, w - 6, jnp.where(k == 1, w - 3, jnp.where(k == 2, w - 1, w)))

    shape = (2, 8, 128)
    yy = gy * 8 + lax.broadcasted_iota(jnp.int32, shape, 1)
    zz = lax.broadcasted_iota(jnp.int32, shape, 0) * 128 + lax.broadcasted_iota(jnp.int32, shape, 2)
    inv_yz = 1.0 / (inverse_window(yy, ny * 8) * inverse_window(zz, 256)).astype(F32)
    touch_yz = (jnp.where(yy == 0, 1, 2) * jnp.where(zz == 0, 1, 2)).astype(F32)

    def inv_x(p):
        i = gx * n + (p - PAD)
        full = nx * n
        r = jnp.where(i == 0, 1 / 10.0, jnp.where(i == 1, 1 / 13.0, jnp.where(i == 2, 1 / 15.0, 1 / 16.0)))
        k = full - 1 - i
        return jnp.where(
            k == 0, 1 / 10.0, jnp.where(k == 1, 1 / 13.0, jnp.where(k == 2, 1 / 15.0, r))
        ).astype(F32)

    filter_y_own(des)

    def clear(edge, field, low, high):
        @pl.when(first_x)
        def _():
            if low:
                field[:, PAD - low : PAD] = jnp.zeros((2, low, 8, 128), F32)
            edge[:, :, 0:PAD] = jnp.zeros((8, 2, PAD, 128), F32)

        @pl.when(last_x)
        def _():
            field[:, end : end + high] = jnp.zeros((2, high, 8, 128), F32)
            edge[:, :, end : end + PAD] = jnp.zeros((8, 2, PAD, 128), F32)

        @pl.when(first_y)
        def _():
            edge[0:3] = jnp.zeros((3, 2, end + PAD, 128), F32)

        @pl.when(last_y)
        def _():
            edge[5:8] = jnp.zeros((3, 2, end + PAD, 128), F32)

    clear(cc, des, 4, 3)
    clear(scc, sen, 3, 3)
    arrived(moving1)
    heat_fields_moving = send_fields(1, 3)
    filter_y_first(des, cc, 4)
    there_x = jnp.where(first_x, 0.0, 1.0).astype(F32)
    there_y = jnp.where(first_y, 0.0, 1.0).astype(F32)

    def density(smoothed, p, e, s):
        solid = smoothed * inv_yz * inv_x(p)
        return jnp.where(e == 1, 0.0, jnp.where(s == 1, 1.0, solid))

    def density_body(i, acc):
        p = PAD + big * i
        smoothed = filter_xz(p, big)
        for u in range(big):
            x = big * i + u
            rho = density(smoothed[:, u], p + u, flg[0, :, x], flg[1, :, x])
            squared = rho * rho
            held = (flg[0, :, x] + flg[1, :, x]) == 0
            coef[:, x] = jnp.where(held, (3.0 * squared) * inv_yz * inv_x(p + u), 0.0)
            cub[:, p + u] = squared * rho
            acc = acc + rho
        return acc

    occupied = density_body(0, jnp.zeros(shape, F32))
    arrived(flags_moving)
    before = density(filter_xz(PAD - 2, 2)[:, 1], PAD - 1, flx[0], flx[1])
    cub[:, PAD - 1] = there_x * (before * before * before)

    def send_cube(start, stop):
        for h in range(2):
            cubs[0, h, start:stop] = row_pack(cub, h, start, stop - start, 7)
        part = (slice(None), slice(None), slice(start, stop))
        return send(cubs.at[part], cube.at[part], 0, 1)

    cube_moving = [send_cube(0, PAD + big)]
    arrived(moving2)
    filter_y_second(des, cc)
    occupied = lax.fori_loop(1, n // big, density_body, occupied)

    cube_moving.append(send_cube(PAD + big, end))

    def gather_body(i, last):
        for u in range(8):
            now = spread(cub[:, PAD + 8 * i + u])
            ca[:, 8 * i + u] = now + last
            last = now
        return last

    lax.fori_loop(0, n // 8, gather_body, spread(cub[:, PAD - 1]))

    def clear_fields(a, b):
        @pl.when(first_x)
        def _():
            fld[a:b, :, PAD - 1] = jnp.zeros((b - a, 2, 8, 128), F32)
            flo[a:b, :, 0:PAD] = jnp.zeros((b - a, 2, PAD, 128), F32)
            fhi[a:b, :, 0:PAD] = jnp.zeros((b - a, 2, PAD, 128), F32)

        @pl.when(last_x)
        def _():
            fld[a:b, :, end] = jnp.zeros((b - a, 2, 8, 128), F32)
            flo[a:b, :, end : end + PAD] = jnp.zeros((b - a, 2, PAD, 128), F32)
            fhi[a:b, :, end : end + PAD] = jnp.zeros((b - a, 2, PAD, 128), F32)

        @pl.when(first_y)
        def _():
            flo[a:b] = jnp.zeros((b - a, 2, end + PAD, 128), F32)

        @pl.when(last_y)
        def _():
            fhi[a:b] = jnp.zeros((b - a, 2, end + PAD, 128), F32)

    arrived(volt_field_moving)
    clear_fields(0, 1)

    def far_rows(k, edge):
        s, d = z_forward(edge)
        zrow[k, 0] = s
        zrow[k, 1] = d

    def forward_of(field, k):
        def forward(p):
            return yz_forward(
                field[:, p], zrow[k, 0, :, pl.ds(p, 1)], zrow[k, 1, :, pl.ds(p, 1)]
            )

        return forward

    far_rows(0, fhi[0])
    weights = ((0.001, 0.999), (0.05, 0.95), (0.05, 0.95))

    def apply_main(which, base, slope, step):
        forwards = [forward_of(fld.at[f], f) for f in which]

        def element(a, b, w):
            return x_backward(*weigh(*x_forward(a, b), w))

        start = []
        w = there_x * base + slope * cub[:, PAD - 1]
        for forward in forwards:
            a, b = forward(PAD - 1), forward(PAD)
            start.append((tuple(b), tuple(element(a, b, w)[1])))

        def body(i, carry):
            carry = list(carry)
            for u in range(step):
                x = step * i + u
                w = base + slope * cub[:, PAD + x]
                for k, f in enumerate(which):
                    a, behind = carry[k]
                    b = forwards[k](PAD + x + 1)
                    front, new = element(a, b, w)
                    kap[f, :, x] = yz_backward([front[c] + behind[c] for c in range(4)])
                    carry[k] = tuple(b), tuple(new)
            return tuple(carry)

        lax.fori_loop(0, n // step, body, tuple(start))

    def edge_weight(base, slope):
        where = lax.broadcasted_iota(jnp.int32, (2, end + PAD, 128), 1)
        real = jnp.where(where == PAD - 1, there_x, 1.0) * there_y
        return base * real + (slope * there_y) * cube[0]

    def whole_row(ref, j):
        return jnp.stack([row_pack(ref, h, 0, end + PAD, j) for h in range(2)])

    def rows_x_forward(a):
        return x_forward(a, [planes_after(c) for c in a])

    def edge_forward(f):
        return rows_x_forward(rows_forward(flo[f], whole_row(fld.at[f], 0)))

    def apply_edge(f, parts):
        front, behind = x_backward(*weigh(*parts, edge_weight(*weights[f])))
        m = [front[c] + planes_before(behind[c]) for c in range(4)]
        ns, nd = m[0] + m[2], m[1] + m[3]
        out = (ns - nd) + z_prev(ns + nd)
        for h in range(2):
            row_add(kap.at[f], h, 0, n, 0, out[h, PAD:end])

    apply_main((0,), *weights[0], big)

    volt_parts = edge_forward(0)
    arrived(cube_moving)

    @pl.when(first_y)
    def _():
        cube[0] = jnp.zeros((2, end + PAD, 128), F32)

    apply_edge(0, volt_parts)
    edge_cube = cube[0] * there_y
    edge_cube = edge_cube + planes_before(edge_cube)
    edge_cube = edge_cube + z_prev(edge_cube)
    for h in range(2):
        row_add(ca, h, 0, n, 0, edge_cube[h, PAD:end])

    def pivot(x, base, slope):
        cx = jnp.where(gx * n + x == 0, 1.0, 2.0).astype(F32)
        return base * (cx * touch_yz) + slope * ca[:, x]

    loaded(8, 9)

    def volt_body(i, carry):
        for u in range(8):
            x = 8 * i + u
            v = raw[0, :, x]
            moved = 1.8 * (raw[3, :, x] - kap[0, :, x]) / pivot(x, 0.001, 0.999)
            v1[:, PAD + x] = v + jnp.where(flg[2, :, x] == 0, moved, -0.6 * v)
        return carry

    lax.fori_loop(0, n // 8, volt_body, 0)
    for h in range(2):
        v1up[0, h] = row_pack(v1, h, PAD, n, 7)
        v1dn[0, h] = row_pack(v1, h, PAD, n, 0)
    volt_moving = send_up(v1up, v1lo) + send_down(v1dn, v1hi)
    volt_moving += [
        send(v1.at[:, end - 1 : end], v1.at[:, PAD - 1 : PAD], 1, 0),
        send(v1.at[:, PAD : PAD + 1], v1.at[:, end : end + 1], -1, 0),
    ]
    stores = []

    def store(src, dst):
        for h in range(2):
            c = pltpu.make_async_copy(
                src(h), dst.at[:, :, pl.ds(128 * h, 128)], out_sem.at[len(stores)]
            )
            c.start()
            stores.append(c)

    store(lambda h: v1.at[h, PAD:end], v_out)

    arrived(heat_fields_moving)
    clear_fields(1, 3)
    far_rows(1, fhi[1])
    far_rows(2, fhi[2])
    apply_main((1, 2), *weights[1], half)
    apply_edge(1, edge_forward(1))
    apply_edge(2, edge_forward(2))

    def heat_body(i, carry):
        for u in range(8):
            x = 8 * i + u
            free = flg[3, :, x] == 0
            step = 1.8 / pivot(x, 0.05, 0.95)
            d = raw[2, :, x]
            d1[:, PAD + x] = d + jnp.where(free, step * (raw[4, :, x] - kap[2, :, x]), -0.6 * d)
            t = raw[1, :, x]
            t0[:, x] = t - jnp.where(free, step * kap[1, :, x], 0.6 * t)
            tr[:, x] = jnp.where(free, step, 0.0)
        return carry

    lax.fori_loop(0, n // 8, heat_body, 0)
    for h in range(2):
        d1dn[0, h] = row_pack(d1, h, PAD, n, 0)
    dual_moving = send_down(d1dn, d1hi, both=False)
    dual_moving.append(send(d1.at[:, PAD : PAD + 1], d1.at[:, end : end + 1], -1, 0))
    store(lambda h: d1.at[h, PAD:end], d_out)

    arrived(volt_moving)

    def clear_high(field, *edges):
        @pl.when(last_x)
        def _():
            field[:, end] = jnp.zeros((2, 8, 128), F32)
            for edge in edges:
                edge[0, :, end : end + PAD] = jnp.zeros((2, PAD, 128), F32)

        @pl.when(last_y)
        def _():
            edges[0][0] = jnp.zeros((2, end + PAD, 128), F32)

    clear_high(v1, v1hi, v1lo)

    @pl.when(first_x)
    def _():
        v1[:, PAD - 1] = jnp.zeros((2, 8, 128), F32)
        v1hi[0, :, 0:PAD] = jnp.zeros((2, PAD, 128), F32)
        v1lo[0, :, 0:PAD] = jnp.zeros((2, PAD, 128), F32)

    @pl.when(first_y)
    def _():
        v1lo[0] = jnp.zeros((2, end + PAD, 128), F32)


    far_rows(3, v1hi[0])
    volt_forward = forward_of(v1, 3)
    def row_energy(near, far):
        s, d = rows_x_forward(rows_forward(near, far))
        return energy(s, d, s, d)

    def row_gather(e):
        e = e + planes_before(e)
        return (e + z_prev(e))[:, PAD:end]

    row0 = whole_row(v1, 0)
    extra = row_gather(row_energy(v1lo[0], row0) * (edge_weight(0.001, 0.999) * 0.125))
    where = lax.broadcasted_iota(jnp.int32, (2, end + PAD, 128), 1)
    own_weight = 0.001 * jnp.where(where == PAD - 1, there_x, 1.0) + 0.999 * whole_row(cub, 0)
    heat0 = extra + row_gather(row_energy(row0, whole_row(v1, 1)) * (own_weight * 0.125))
    for h in range(2):
        t1dn[0, h] = row_pack(t0, h, 0, n, 0) + row_pack(tr, h, 0, n, 0) * heat0[h]
    temp_moving = send_down(t1dn, t1hi, both=False)

    a = volt_forward(PAD - 1)
    b = volt_forward(PAD)
    s, d = x_forward(a, b)
    lead = energy(s, d, s, d) * ((there_x * 0.001 + 0.999 * cub[:, PAD - 1]) / 8.0)

    def joule_body(i, carry):
        a, last, acc = carry
        for u in range(big):
            x = big * i + u
            b = volt_forward(PAD + x + 1)
            s, d = x_forward(a, b)
            e = energy(s, d, s, d)
            joule[:, x] = e
            now = spread(e * (0.001 / 8.0 + (0.999 / 8.0) * cub[:, PAD + x]))
            t = t0[:, x] + tr[:, x] * (now + last)
            t1[:, PAD + x] = t
            acc = acc + raw[4, :, x] * t
            a, last = b, now
        return tuple(a), last, acc

    carry = joule_body(0, (tuple(b), spread(lead), jnp.zeros(shape, F32)))
    for h in range(2):
        t1[h, PAD, 0:1] += extra[h, 0:1] * tr[h, 0, 0:1]
    temp_moving.append(send(t1.at[:, PAD : PAD + 1], t1.at[:, end : end + 1], -1, 0))
    _, _, warm = lax.fori_loop(1, n // big, joule_body, carry)

    warm_rows = jnp.zeros((8, 128), F32)
    for h in range(2):
        more = extra[h] * row_pack(tr, h, 0, n, 0)
        row_add(t1, h, PAD + 1, n - 1, 0, more[1:])
        warm_rows = warm_rows + jnp.sum(
            (more * row_pack(raw.at[4], h, 0, n, 0)).reshape(n // 8, 8, 128), axis=0
        )
    store(lambda h: t1.at[h, PAD:end], t_out)

    arrived(dual_moving)
    clear_high(d1, d1hi)
    far_rows(4, d1hi[0])
    dual_forward = forward_of(d1, 4)
    none = jnp.zeros((2, 1, 128), F32)

    def pair_forward(p):
        return tuple(yz_forward(t1[:, p], none, none)), tuple(dual_forward(p))

    def sens_body(i, carry):
        ta, da = carry
        for u in range(half):
            x = half * i + u
            tb, db = pair_forward(PAD + x + 1)
            ts, td = x_forward(ta, tb)
            ds, dd = x_forward(da, db)
            mean = (0.999 / 8.0) * (da[0] + db[0])
            value = joule[:, x] * mean - 0.95 * energy(ts, td, ds, dd)
            sen[:, PAD + x] = coef[:, x] * value
            ta, da = tb, db
        return ta, da

    carry = lax.fori_loop(0, n // half - 1, sens_body, pair_forward(PAD))
    dual_s, dual_d = rows_x_forward(rows_forward(whole_row(d1, 7), d1hi[0]))
    arrived(temp_moving)
    clear_high(t1, t1hi)
    sens_body(n // half - 1, carry)
    tails_down(sen, sdn)
    sens1 = send_first(sdn, scc.at[5:8], -1)
    sens2 = send_second(sdn, scc.at[5:8], -1)
    behind_s, behind_d = z_forward(t1hi[0])
    temp_s, temp_d = rows_x_forward((behind_s, behind_d, behind_s, behind_d))
    work = 0.95 * energy(temp_s, temp_d, dual_s, dual_d)
    for h in range(2):
        row_add(sen, h, PAD, n, 7, -work[h, PAD:end] * row_pack(coef, h, 0, n, 7))
    tails_up(sen, sup)
    sens1 += send_first(sup, scc.at[0:3], 1)
    sens1.append(send(sen.at[:, end - 3 : end], sen.at[:, PAD - 3 : PAD], 1, 0))
    sens2 += send_second(sup, scc.at[0:3], 1)
    sens2.append(send(sen.at[:, PAD : PAD + 3], sen.at[:, end : end + 3], -1, 0))
    filter_y_own(sen)

    def whole(a):
        return jnp.sum(jnp.sum(a, axis=0, keepdims=True), axis=1, keepdims=True)

    occupied_sum = whole(occupied[0] + occupied[1])
    warm_sum = whole(warm[0] + warm[1] + warm_rows)
    arrived(sens1)
    filter_y_first(sen, scc, 3)

    def last_body(i, acc):
        out = filter_xz(PAD + big * i, big)
        fil[:, pl.ds(big * i, big)] = out
        return acc + jnp.sum(out * out, axis=1)

    square = last_body(0, jnp.zeros(shape, F32))
    arrived(sens2)
    filter_y_second(sen, scc)
    square = lax.fori_loop(1, n // big, last_body, square)
    store(lambda h: fil.at[h], f_out)

    lane = lax.broadcasted_iota(jnp.int32, (1, 128), 1)
    message = jnp.where(
        lane == 0,
        whole(square[0] + square[1]),
        jnp.where(lane == 1, occupied_sum, warm_sum),
    )

    def exchange(value, slots, me, size, peer, sends, recvs):
        slots[me, 0:1] = value
        for k in farthest_first(size):
            pltpu.make_async_remote_copy(
                src_ref=slots.at[me, pl.ds(0, 1)], dst_ref=slots.at[me, pl.ds(0, 1)],
                send_sem=sends.at[0], recv_sem=recvs.at[0],
                device_id=peer(k), device_id_type=MESH,
            ).start()
        others = slots.at[pl.ds(0, size - 1), pl.ds(0, 1)]
        every = pltpu.make_async_remote_copy(
            src_ref=others, dst_ref=others, send_sem=sends.at[0], recv_sem=recvs.at[0],
            device_id=peer(1), device_id_type=MESH,
        )
        every.wait_recv()
        pending.append((every, 0, 0))
        parts = [slots[k, 0:1] for k in range(size)]
        while len(parts) > 1:
            parts = [a + b for a, b in zip(parts[::2], parts[1::2])]
        return parts[0]

    message = exchange(message, slots1, me1, size1, peer1, r1_send, r1_recv)
    message = exchange(message, slots2, me2, size2, peer2, r2_send, r2_recv)
    sums_out[...] = jnp.broadcast_to(message, (8, 128))
    for c, dx, dy in pending:

        @pl.when(exists(dx, dy))
        def _(c=c):
            c.wait_send()

    for c in stores:
        c.wait()


def finish(
    total, v, t, d, f, sums_ref, v_out, t_out, d_out, f_out, occ_out, mean_out, buf, sem
):
    copies = [
        pltpu.make_async_copy(src, dst, sem.at[i])
        for i, (src, dst) in enumerate(((v, v_out), (t, t_out), (d, d_out)))
    ]
    for c in copies:
        c.start()
    sums = sums_ref[0:1] * (1.0 / total)
    scale = jnp.broadcast_to(1.0 / jnp.sqrt(sums[:, 0:1] + 1e-6), (8, 256))
    parts = 4
    step = buf.shape[0] // parts
    for i in range(parts):
        part = pl.ds(step * i, step)
        buf[part] = f[part] * scale
        c = pltpu.make_async_copy(buf.at[part], f_out.at[part], sem.at[3 + i])
        c.start()
        copies.append(c)
    occ_out[0] = sums[0, 1]
    mean_out[0] = sums[0, 2]
    for c in copies:
        c.wait()


def per_device(nx, ny, *args):
    n = args[0].shape[0]
    assert args[0].shape[1:] == (8, 256) and n % 8 == 0
    field = jax.ShapeDtypeStruct(args[0].shape, F32)
    tile = jax.ShapeDtypeStruct((8, 128), F32)
    wide = n + 2 * PAD

    def vm(*shape, dtype=F32):
        return pltpu.VMEM(shape, dtype)

    planes = vm(2, wide, 8, 128)
    own = vm(2, n, 8, 128)
    edge = vm(1, 2, wide, 128)
    edge_out = vm(1, 2, n, 128)
    scratch = [
        planes, vm(5, 2, n, 8, 128), vm(4, 2, n, 8, 128, dtype=jnp.int32),
        vm(3, 2, wide, 8, 128), vm(2, 2, 8, 128, dtype=jnp.int32),
        vm(5, 2, 2, wide, 128), own,
        vm(8, 2, wide, 128), vm(3, 2, n, 128), vm(3, 2, n, 128),
        vm(3, 2, wide, 128), vm(3, 2, wide, 128), vm(3, 2, n, 128), vm(3, 2, n, 128),
        vm(256, 256, dtype=BF16), planes, planes,
        edge, vm(1, 2, PAD + n, 128), own,
        vm(3, 2, n, 8, 128), planes, edge, edge, edge_out, edge_out,
        planes, edge, edge_out, own, own, planes, edge, edge_out, own,
        planes, vm(8, 2, wide, 128), vm(3, 2, n, 128), vm(3, 2, n, 128), own,
        vm(nx * 2, 8, 128), vm(ny // 2, 8, 128),
        pltpu.SemaphoreType.DMA((20,)), pltpu.SemaphoreType.DMA((8,)),
        pltpu.SemaphoreType.DMA((64,)), pltpu.SemaphoreType.DMA((64,)),
        pltpu.SemaphoreType.DMA((1,)), pltpu.SemaphoreType.DMA((1,)),
        pltpu.SemaphoreType.DMA((1,)), pltpu.SemaphoreType.DMA((1,)),
    ]
    anywhere = pl.BlockSpec(memory_space=pl.ANY)
    hbm = pl.BlockSpec(memory_space=pltpu.HBM)
    vmem = pl.BlockSpec(memory_space=pltpu.VMEM)
    smem = pl.BlockSpec(memory_space=pltpu.SMEM)
    *fields, sums = pl.pallas_call(
        functools.partial(kernel, nx, ny, n),
        out_shape=(field, field, field, field, tile),
        in_specs=[hbm] * 10,
        out_specs=(anywhere,) * 4 + (vmem,),
        scratch_shapes=scratch,
        compiler_params=pltpu.CompilerParams(
            collective_id=0, has_side_effects=True, vmem_limit_bytes=103 * 512 * 1024
        ),
    )(*args)
    one = jax.ShapeDtypeStruct((1,), F32)
    *outs, occupied, mean = pl.pallas_call(
        functools.partial(finish, float(nx * ny * n * 8 * 256)),
        out_shape=(field, field, field, field, one, one),
        in_specs=[anywhere] * 3 + [vmem, vmem],
        out_specs=(hbm,) * 4 + (smem, smem),
        scratch_shapes=[vm(n, 8, 256), pltpu.SemaphoreType.DMA((8,))],
        compiler_params=pltpu.CompilerParams(vmem_limit_bytes=8 * 1024 * 1024),
    )(*fields, sums)
    return (*outs, occupied.reshape(()), mean.reshape(()))


def solution(mesh):
    spec = P("gx", "gy", None)
    return jax.shard_map(
        functools.partial(per_device, mesh.shape["gx"], mesh.shape["gy"]),
        mesh=mesh,
        in_specs=(spec,) * 10,
        out_specs=(spec,) * 4 + (P(), P()),
        check_vma=False,
    )
```
